32 devices in a mesh: ctx: 8 (over z, x), shard: 4 (over y, core).
Axes of the slice: x: 2, y: 2, z: 4, core: 2. Of those that a mesh axis runs over, the one named last changes fastest.
Arguments:
- tokens: bfloat16 [8, 512, 2048], P('shard', 'ctx'), may hold values from -6 to 6
- cotangent: bfloat16 [8, 512, 2048], P('shard', 'ctx'), may hold values from -6 to 6
- adapter_index: int32 [8, 1], P('shard'), may hold values from 0 to 7
- w_attn: bfloat16 [4, 2048, 2048], P(None, 'shard'), may hold values from -0.125 to 0.125
- w_gate_up: bfloat16 [2, 2048, 8192], P(None, 'shard'), may hold values from -0.125 to 0.125
- w_down: bfloat16 [8192, 2048], P('shard'), may hold values from -0.0625 to 0.0625
- gains: bfloat16 [4, 2048], P(None, 'shard'), may hold values from 0.5 to 1.5
- a_wide: bfloat16 [6, 8, 16, 2048], P(None, None, None, 'shard'), may hold values from -0.125 to 0.125
- a_down: bfloat16 [8, 16, 8192], P(None, None, 'shard'), may hold values from -0.0625 to 0.0625
- b_model: bfloat16 [5, 8, 16, 2048], P(None, None, None, 'shard'), may hold values from -1.5 to 1.5
- b_hidden: bfloat16 [2, 8, 16, 8192], P(None, None, None, 'shard'), may hold values from -1.5 to 1.5
Outputs:
- output: bfloat16 [8, 512, 2048], P('shard', 'ctx')
- input_grad: float32 [8, 512, 2048], P('shard', 'ctx')
- grad_a_wide: float32 [6, 8, 16, 2048], P(None, None, None, 'shard')
- grad_a_down: float32 [8, 16, 8192], P(None, None, 'shard')
- grad_b_model: float32 [5, 8, 16, 2048], P(None, None, None, 'shard')
- grad_b_hidden: float32 [2, 8, 16, 8192], P(None, None, None, 'shard')
The draws below stay inside these ranges and needn't reach their ends.
Inputs may be any that keep to these rules, and one draw needn't show every extreme that they name: `adapter_index`: every one of the 8 adapters is the adapter of at least one sequence.
All inputs are finite; a program needn't handle non-finite values.
Results may differ from the reference program's by a relative error of at most 0.025.
Values may be sent and summed in bfloat16 or wider, within the bound.
No kernel may reach another device: no remote copies, remote signals or barrier semaphores. Data moves between devices by JAX's collectives and lax.ppermute only.
A program may use at most 512 MiB of HBM per device.

```python
import math
import jax
import jax.numpy as jnp
from jax import lax

D = 2048
HEADS = 16
HD = 128
FF = 8192
RANK = 16
NADAPT = 8
BLOCK = 256
BATCH = 8
LEN = 512


def shard_levels(own_key, shape, pieces, smallest, largest):
    def one(position, shards_of):
        heights = jax.random.uniform(jax.random.fold_in(jax.random.fold_in(own_key, 6), position), (shards_of,), jnp.float32, smallest / len(pieces), largest / len(pieces))
        return jnp.repeat(jnp.exp(heights), shape[position] // shards_of).reshape((-1,) + (1,) * (len(shape) - position - 1))

    factor_of = one(*pieces[0])
    for cut in pieces[1:]:
        factor_of = factor_of * one(*cut)
    return factor_of


def distinct(stream_key, rows, number_of, top, lift):
    ranking = jax.random.permutation(jax.random.fold_in(stream_key, 1), number_of)
    pull = ranking
    for power in range(3):
        pull = pull * pull // number_of
    pull = pull * lift // number_of
    tickets = jax.random.randint(jax.random.fold_in(stream_key, 2), (rows, number_of), 0, 4096) + pull
    fixed_rows = jax.random.permutation(jax.random.fold_in(stream_key, 3), rows)[jnp.arange(number_of) % rows]
    tickets = jnp.where(jnp.arange(rows)[:, None] == fixed_rows[None, :], 1 << 14, tickets)
    score = tickets * number_of + jnp.arange(number_of)
    return lax.top_k(score.astype(jnp.int32), top)[1].astype(jnp.int32)


def normal_values(rng, shape, spread, reach, split=(), kind=jnp.bfloat16):
    factor_of = shard_levels(rng, shape, split, -0.22, 0.18) if split else 1.0
    array = jax.random.normal(rng, shape, jnp.float32) * spread * factor_of
    return jnp.minimum(jnp.maximum(array, -reach), reach).astype(kind)


def setup_inputs(seed: int = 0) -> dict:
    splits = jax.random.split(jax.random.key(seed), 12)
    return {
        "tokens": normal_values(splits[0], (BATCH, LEN, D), 1.0, 6.0, ((0, 4), (1, 8))),
        "cotangent": normal_values(splits[1], (BATCH, LEN, D), 1.0, 6.0, ((0, 4), (1, 8))),
        "adapter_index": distinct(splits[2], BATCH, NADAPT, 1, 0),
        "w_attn": normal_values(splits[3], (4, D, D), D ** -0.5, 0.125, ((1, 4),)),
        "w_gate_up": normal_values(splits[4], (2, D, FF), D ** -0.5, 0.125, ((1, 4),)),
        "w_down": normal_values(splits[5], (FF, D), FF ** -0.5, 0.0625, ((0, 4),)),
        "gains": jnp.clip(1.0 + 0.1 * jax.random.normal(splits[6], (4, D), jnp.float32), 0.5, 1.5).astype(jnp.bfloat16),
        "a_wide": normal_values(splits[7], (6, NADAPT, RANK, D), D ** -0.5, 0.125, ((3, 4),)),
        "a_down": normal_values(splits[8], (NADAPT, RANK, FF), FF ** -0.5, 0.0625, ((2, 4),)),
        "b_model": normal_values(splits[9], (5, NADAPT, RANK, D), RANK ** -0.5, 1.5, ((3, 4),)),
        "b_hidden": normal_values(splits[10], (2, NADAPT, RANK, FF), RANK ** -0.5, 1.5, ((3, 4),)),
    }


epsilon = 1e-06
rope_base = 500000.0
far_below = -1e+30

@jax.custom_vjp
def low(v):
    return lax.optimization_barrier(v.astype(jnp.bfloat16)).astype(jnp.float32)

@jax.custom_vjp
def low_back(v):
    return v

def low_keep(v):
    return (low(v), None)

def low_pass(kept, grad):
    return (grad,)

def back_keep(v):
    return (v, None)

def back_low(kept, grad):
    return (low(grad),)
low.defvjp(low_keep, low_pass)
low_back.defvjp(back_keep, back_low)

def matmul(left_arg, right_arg):
    return jnp.dot(left_arg, right_arg, precision=lax.Precision.HIGHEST, preferred_element_type=jnp.float32)

def rms_norm(value_in, gain_row):
    return value_in * lax.rsqrt(lax.optimization_barrier(jnp.mean(value_in * value_in, axis=-1, keepdims=True)) + epsilon) * gain_row

def rope_tables(length_rows):
    positions = jnp.arange(length_rows, dtype=jnp.float32)
    freqs_rows = jnp.exp(jnp.arange(0, HD, 2, dtype=jnp.float32) * (-math.log(rope_base) / HD))
    angles = positions[:, None] * freqs_rows[None, :]
    return (jnp.cos(angles)[:, None, :], jnp.sin(angles)[:, None, :])

def rotate(value_in, cosine_table, sine_table):
    half_width = value_in.shape[-1] // 2
    first_half = value_in[..., :half_width]
    second_half = value_in[..., half_width:]
    return jnp.concatenate([first_half * cosine_table - second_half * sine_table, second_half * cosine_table + first_half * sine_table], axis=-1)

def adapt_proj(inputs, weight, down_map, up_map):
    lowrank = low_back(low(matmul(inputs, down_map.T)))
    return matmul(inputs, weight) + matmul(lowrank, up_map)

def attend(queries, key_rows, values):
    length_rows = queries.shape[0]
    block_rows = min(512, length_rows)
    factor = 1.0 / math.sqrt(HD)
    key_block = jnp.arange(length_rows, dtype=jnp.int32) // BLOCK

    def one_block(block_index):
        first_row = block_index * block_rows
        row_slice = lax.dynamic_slice_in_dim(queries, first_row, block_rows, 0)
        row_block = (first_row + jnp.arange(block_rows, dtype=jnp.int32)) // BLOCK
        scores = low_back(jnp.einsum('qhd,khd->hqk', row_slice, key_rows, precision=lax.Precision.HIGHEST) * factor)
        visible = key_block[None, :] <= row_block[:, None]
        scores = jnp.where(visible[None], scores, far_below)
        top_score = lax.optimization_barrier(jnp.max(scores, axis=-1, keepdims=True))
        weights = jnp.exp(scores - top_score)
        prob_rows = low(weights / lax.optimization_barrier(jnp.sum(weights, axis=-1, keepdims=True)))
        return jnp.einsum('hqk,khd->qhd', prob_rows, values, precision=lax.Precision.HIGHEST)
    blocks = lax.map(jax.checkpoint(one_block), jnp.arange(length_rows // block_rows, dtype=jnp.int32))
    return blocks.reshape(length_rows, HEADS, HD)

def layer_forward(token_rows, wide_sel, down_sel, model_sel, hidden_sel, frozen):
    attention_weights, gate_upper, down_weights, norm_gains, cosine_table, sine_table = frozen
    length_rows = token_rows.shape[0]
    query_pre = low_back(adapt_proj(token_rows, attention_weights[0], wide_sel[0], model_sel[0]))
    key_pre = low_back(adapt_proj(token_rows, attention_weights[1], wide_sel[1], model_sel[1]))
    value_pre = low_back(adapt_proj(token_rows, attention_weights[2], wide_sel[2], model_sel[2]))
    queries = low(rotate(rms_norm(query_pre, norm_gains[0]).reshape(length_rows, HEADS, HD), cosine_table, sine_table))
    key_rows = low(rotate(rms_norm(key_pre, norm_gains[1]).reshape(length_rows, HEADS, HD), cosine_table, sine_table))
    values = low(value_pre).reshape(length_rows, HEADS, HD)
    mixed_low = low(low_back(attend(queries, key_rows, values).reshape(length_rows, D)))
    attention_pre = low_back(adapt_proj(mixed_low, attention_weights[3], wide_sel[3], model_sel[3]))
    resid_sum = token_rows + rms_norm(attention_pre, norm_gains[2])
    resid_low = low(resid_sum)
    gate_pre = low_back(adapt_proj(resid_low, gate_upper[0], wide_sel[4], hidden_sel[0]))
    upper_pre = low_back(adapt_proj(resid_low, gate_upper[1], wide_sel[5], hidden_sel[1]))
    activation = low(jax.nn.silu(gate_pre) * upper_pre)
    feed_pre = low_back(adapt_proj(activation, down_weights, down_sel, model_sel[4]))
    return resid_sum + rms_norm(feed_pre, norm_gains[3])

def reference(tokens, cotangent, adapter_index, w_attn, w_gate_up, w_down, gains, a_wide, a_down, b_model, b_hidden):
    wide_downs = a_wide.astype(jnp.float32)
    down_maps = a_down.astype(jnp.float32)
    model_ups = b_model.astype(jnp.float32)
    hidden_ups = b_hidden.astype(jnp.float32)
    cosine_table, sine_table = rope_tables(LEN)
    frozen = (w_attn.astype(jnp.float32), w_gate_up.astype(jnp.float32), w_down.astype(jnp.float32), gains.astype(jnp.float32), cosine_table, sine_table)

    def scan_step(totals, seq_item):
        seq_tokens, seq_cotangent, adapter_pick = seq_item

        def forward_one(token_rows, wide_sel, down_sel, model_sel, hidden_sel):
            return layer_forward(token_rows, wide_sel, down_sel, model_sel, hidden_sel, frozen)
        output_rows, pull_back = jax.vjp(forward_one, seq_tokens, wide_downs[:, adapter_pick], down_maps[adapter_pick], model_ups[:, adapter_pick], hidden_ups[:, adapter_pick])
        grad_list = pull_back(seq_cotangent)
        totals = (totals[0].at[:, adapter_pick].add(grad_list[1]), totals[1].at[adapter_pick].add(grad_list[2]), totals[2].at[:, adapter_pick].add(grad_list[3]), totals[3].at[:, adapter_pick].add(grad_list[4]))
        return (totals, (output_rows.astype(jnp.bfloat16), grad_list[0]))
    init_state = (jnp.zeros(a_wide.shape, jnp.float32), jnp.zeros(a_down.shape, jnp.float32), jnp.zeros(b_model.shape, jnp.float32), jnp.zeros(b_hidden.shape, jnp.float32))
    totals, (output, input_grad) = lax.scan(scan_step, init_state, (tokens.astype(jnp.float32), cotangent.astype(jnp.float32), adapter_index[:, 0]))
    return (output, input_grad, totals[0], totals[1], totals[2], totals[3])
```

```python
import math

import jax
import jax.numpy as jnp
from jax import lax
from jax.sharding import PartitionSpec as P

D = 2048
HEADS = 16
HD = 128
BLOCK = 256
CHUNKS = 1

epsilon = 1e-06
rope_base = 500000.0
far_below = -1e30
BF = jnp.bfloat16
F32 = jnp.float32


def dot(left, right):
    return lax.dot_general(left, right, (((1,), (0,)), ((), ())), preferred_element_type=F32)


def dot_nt(left, right):
    return lax.dot_general(left, right, (((1,), (1,)), ((), ())), preferred_element_type=F32)


def dot_tn(left, right):
    return lax.dot_general(left, right, (((0,), (0,)), ((), ())), preferred_element_type=F32)


def over_shard(value, flip):
    size = lax.axis_size("shard")
    return lax.ppermute(value, "shard", [(i, i ^ flip) for i in range(size)])


def over_ctx(value, flip):
    size = lax.axis_size("ctx")
    return lax.ppermute(value, "ctx", [(i, i ^ flip) for i in range(size)])


FLIPS = (0, 2, 1, 3)


def gather_rows(own):
    pair = jnp.concatenate([own, over_shard(own, 2)], axis=0)
    return jnp.concatenate([pair, over_shard(pair, 1)], axis=0)


def scatter_rows(partial):
    rows = partial.shape[0] // 4
    got = over_shard(partial[2 * rows :].astype(BF), 1)
    half = partial[: 2 * rows] + got.astype(F32)
    got = over_shard(half[rows:].astype(BF), 2)
    return half[:rows] + got.astype(F32)


def column_block(value, index, width):
    return lax.dynamic_slice_in_dim(value, index * width, width, value.ndim - 1)


def scatter_columns(partial, shard):
    width = partial.shape[-1] // 4
    blocks = [column_block(partial, shard ^ flip, width) for flip in FLIPS]
    got = over_shard(jnp.stack(blocks[2:]).astype(BF), 1).astype(F32)
    far = (blocks[1] + got[1]).astype(BF)
    return blocks[0] + got[0] + over_shard(far, 2).astype(F32)


def natural(parts, shard):
    out = []
    for index in range(4):
        value = parts[0]
        for flip, part in zip(FLIPS[1:], parts[1:]):
            value = jnp.where((shard ^ flip) == index, part, value)
        out.append(value)
    return out


def relayout(weight, shard, quarter):
    count, depth, full = weight.shape
    width = full // 4
    slim = depth // 4
    mine = lax.dynamic_slice_in_dim(weight, quarter * slim, slim, 1)
    to_far = jnp.stack([column_block(mine, shard ^ 2, width), column_block(mine, shard ^ 3, width)])
    arrived = over_shard(to_far, 2)
    crossed = over_shard(arrived[1], 1)
    held = jnp.stack([arrived[0], crossed])
    from_x = over_ctx(held, 1)
    from_z = over_ctx(held, 2)
    diag_a = over_ctx(from_z[0], 1)
    diag_b = over_ctx(from_x[1], 2)
    near = over_shard(column_block(weight, shard ^ 1, width), 1)
    own = column_block(weight, shard, width)
    whole = jnp.zeros((count, 4 * depth, width), weight.dtype)

    def put(whole, piece, block, part):
        return lax.dynamic_update_slice(
            whole, piece, (jnp.int32(0), block * depth + part * slim, jnp.int32(0))
        )

    zero = jnp.int32(0)
    whole = put(whole, own, shard, zero)
    whole = put(whole, near, shard ^ 1, zero)
    for place, flip in enumerate((2, 3)):
        whole = put(whole, held[place], shard ^ flip, quarter)
        whole = put(whole, from_x[place], shard ^ flip, quarter ^ 1)
        whole = put(whole, from_z[place], shard ^ flip, quarter ^ 2)
    whole = put(whole, diag_a, shard ^ 2, quarter ^ 3)
    whole = put(whole, diag_b, shard ^ 3, quarter ^ 3)
    return whole


def rms_scale(value):
    return lax.rsqrt(jnp.mean(value * value, axis=-1, keepdims=True) + epsilon)


def rms_back(value, scale, gain, grad):
    weighted = grad * gain
    return scale * weighted - value * (
        scale * scale * scale * jnp.mean(value * weighted, axis=-1, keepdims=True)
    )


def rotate(value, cosine, sine):
    half = value.shape[-1] // 2
    first, second = value[..., :half], value[..., half:]
    return jnp.concatenate([first * cosine - second * sine, second * cosine + first * sine], axis=-1)


def group_of(sequence, part, per_sequence, ctx_size):
    if per_sequence > 1:
        return sequence * per_sequence + part
    depth = sequence % (ctx_size // 2)
    return 2 * depth + (depth + sequence // (ctx_size // 2)) % 2


def on_device(
    tokens,
    cotangent,
    adapter_index,
    w_attn,
    w_gate_up,
    w_down,
    gains,
    a_wide,
    a_down,
    b_model,
    b_hidden,
):
    seqs, rows = tokens.shape[0], tokens.shape[1]
    shards, ctxs = lax.axis_size("shard"), lax.axis_size("ctx")
    shard, ctx = lax.axis_index("shard"), lax.axis_index("ctx")
    batch = seqs * shards
    per_sequence = ctxs // batch
    group_rows = batch * rows
    heads = HEADS // shards
    wide = heads * HD
    adapters = a_down.shape[0]
    rank = a_down.shape[1]
    quarter = ctx % 4

    groups = [[group_of(q, k, per_sequence, ctxs) for k in range(per_sequence)] for q in range(batch)]
    sequence_at, part_at = [0] * ctxs, [0] * ctxs
    for q in range(batch):
        for k in range(per_sequence):
            sequence_at[groups[q][k]] = q
            part_at[groups[q][k]] = k
    my_sequence = jnp.array(sequence_at, jnp.int32)[ctx]
    my_part = jnp.array(part_at, jnp.int32)[ctx]
    my_slot = my_sequence % seqs
    my_spot = (ctx % batch) // shards

    pairs = []
    for p in range(seqs):
        pairs.append([])
        for c in range(ctxs):
            for s in range(shards):
                k, local = c // batch, c % batch
                spot, owner = local // shards, local % shards
                to = groups[seqs * s + (p + spot) % seqs][k]
                pairs[p].append((c * shards + s, to * shards + owner))

    def to_groups(value):
        got = []
        for p in range(seqs):
            sent = lax.dynamic_index_in_dim(value, (p + my_spot) % seqs, 0, keepdims=False)
            got.append(lax.ppermute(sent, ("ctx", "shard"), pairs[p]))
        got = jnp.stack(got)
        return [
            lax.dynamic_index_in_dim(got, (my_slot - h) % seqs, 0, keepdims=False)
            for h in range(seqs)
        ]

    def from_groups(parts):
        stacked = jnp.stack(parts)
        got = []
        for p in range(seqs):
            sent = lax.dynamic_index_in_dim(stacked, (my_slot - p) % seqs, 0, keepdims=False)
            got.append(lax.ppermute(sent, ("ctx", "shard"), [(b, a) for a, b in pairs[p]]))
        got = jnp.stack(got)
        return jnp.stack(
            [
                lax.dynamic_index_in_dim(got, (j - my_spot) % seqs, 0, keepdims=False)
                for j in range(seqs)
            ]
        )

    def chunked(parts):
        if CHUNKS == 1:
            return [jnp.concatenate(parts, axis=0)]
        return parts

    def unchunked(chunks):
        if CHUNKS == 1:
            return [chunks[0][h * rows : (h + 1) * rows] for h in range(seqs)]
        return chunks

    token_rows = chunked(to_groups(tokens))
    index_pair = jnp.stack([adapter_index[:, 0], over_shard(adapter_index[:, 0], 2)])
    index_far = over_shard(index_pair, 1)
    index_all = jnp.concatenate(
        natural([index_pair[0], index_pair[1], index_far[0], index_far[1]], shard)
    )
    my_adapter = index_all[my_sequence]
    own_wide = lax.dynamic_index_in_dim(a_wide, my_adapter, 1, keepdims=False)
    own_down = lax.dynamic_index_in_dim(a_down, my_adapter, 0, keepdims=False)
    own_model = lax.dynamic_index_in_dim(b_model, my_adapter, 1, keepdims=False)
    own_hidden = lax.dynamic_index_in_dim(b_hidden, my_adapter, 1, keepdims=False)
    small = jnp.concatenate(
        [
            own_wide[:3].reshape(3 * rank, wide),
            own_wide[4:].reshape(2 * rank, wide),
            own_model[3:].reshape(2 * rank, wide),
            gains[2:],
        ]
    )
    small_pair = jnp.stack([small, over_shard(small, 2)])
    small_far = over_shard(small_pair, 1)
    small_all = jnp.concatenate(
        natural([small_pair[0], small_pair[1], small_far[0], small_far[1]], shard), axis=1
    )
    qkv_downs = small_all[: 3 * rank]
    gate_downs = small_all[3 * rank : 5 * rank]
    out_up = small_all[5 * rank : 6 * rank]
    feed_up = small_all[6 * rank : 7 * rank]
    attn_gain = small_all[7 * rank : 7 * rank + 1].astype(F32)
    feed_gain = small_all[7 * rank + 1 : 7 * rank + 2].astype(F32)

    w_qkv = relayout(w_attn[:3], shard, quarter)
    w_gate = relayout(w_gate_up[:1], shard, quarter)[0]
    w_up = relayout(w_gate_up[1:], shard, quarter)[0]
    w_out = w_attn[3]

    block_of_row = []
    positions = []
    span = rows * seqs // CHUNKS
    for h in range(CHUNKS):
        place = jnp.arange(span, dtype=jnp.int32)
        spots = h * (seqs // CHUNKS) + place // rows
        inner = place % rows
        for flip in FLIPS:
            positions.append(my_part * group_rows + (spots * shards + (shard ^ flip)) * rows + inner)
    positions = jnp.concatenate(positions)
    freqs = jnp.exp(jnp.arange(0, HD, 2, dtype=F32) * (-math.log(rope_base) / HD))
    angles = positions.astype(F32)[:, None] * freqs[None, :]
    cosine, sine = jnp.cos(angles)[:, None, :], jnp.sin(angles)[:, None, :]

    token_all = [gather_rows(x) for x in token_rows]
    token_full = jnp.concatenate(token_all) if len(token_all) > 1 else token_all[0]
    total_rows = token_full.shape[0]

    qkv_low = dot_nt(token_full, qkv_downs).astype(BF)
    lows = [qkv_low[:, p * rank : (p + 1) * rank] for p in range(3)]
    pre = [dot(token_full, w_qkv[p]) + dot(lows[p], own_model[p]) for p in range(3)]

    def over_all_heads(sums):
        shape = sums.shape
        sums = sums.reshape(shape[0], CHUNKS, 2, 2, -1)
        sums = sums + over_shard(sums, 1)[:, :, ::-1]
        sums = sums + over_shard(sums, 2)[:, :, :, ::-1]
        return sums.reshape(shape)

    squares = over_all_heads(
        jnp.stack([jnp.sum(pre[p] * pre[p], axis=-1) for p in range(2)])
    )
    scales = lax.rsqrt(squares / D + epsilon)[:, :, None]
    head_gain = gains[:2].astype(F32)

    def as_heads(value):
        return value.reshape(total_rows, heads, HD)

    queries, key_rows = [
        rotate(as_heads(pre[p] * scales[p] * head_gain[p]), cosine, sine).astype(BF)
        for p in range(2)
    ]
    values = as_heads(pre[2].astype(BF))

    def over_sequence(value):
        if per_sequence == 1:
            return value
        return lax.all_gather(value, "ctx", axis=0, tiled=True, axis_index_groups=groups)

    key_all, value_all = over_sequence(key_rows), over_sequence(values)
    key_block = over_sequence(positions // BLOCK)
    visible = key_block[None, :] <= (positions // BLOCK)[:, None]
    factor = 1.0 / math.sqrt(HD)
    scores = jnp.einsum("qhd,khd->hqk", queries, key_all, preferred_element_type=F32) * factor
    scores = jnp.where(visible, scores, far_below)
    weights = jnp.exp(scores - jnp.max(scores, axis=-1, keepdims=True))
    probs = weights / jnp.sum(weights, axis=-1, keepdims=True)
    probs_low = probs.astype(BF)
    mixed = jnp.einsum("hqk,khd->qhd", probs_low, value_all, preferred_element_type=F32)
    mixed = mixed.astype(BF).reshape(total_rows, wide)

    chunk_rows = total_rows // CHUNKS

    def chunk_of(value, h):
        return value[h * chunk_rows : (h + 1) * chunk_rows]

    cot_rows = chunked(to_groups(cotangent))
    output_rows, grad_resid_rows, grad_mixed_chunks = [], [], []
    down_a = gate_b = up_b = feed_b = gate_up_a = out_a = out_b = 0.0
    for h in range(CHUNKS):
        mix = chunk_of(mixed, h)
        out_low = dot_nt(mix, own_wide[3]).astype(BF)
        attn_pre = scatter_rows(dot(mix, w_out) + dot(out_low, out_up))
        attn_scale = rms_scale(attn_pre)
        resid = token_rows[h].astype(F32) + attn_pre * attn_scale * attn_gain
        resid_low = gather_rows(resid.astype(BF))
        gate_low = dot_nt(resid_low, gate_downs).astype(BF)
        gate_pre = dot(resid_low, w_gate) + dot(gate_low[:, :rank], own_hidden[0])
        up_pre = dot(resid_low, w_up) + dot(gate_low[:, rank:], own_hidden[1])
        gate_sig = jax.nn.sigmoid(gate_pre)
        activation = (gate_pre * gate_sig * up_pre).astype(BF)
        feed_low = dot_nt(activation, own_down).astype(BF)
        feed_pre = scatter_rows(dot(activation, w_down) + dot(feed_low, feed_up))
        feed_scale = rms_scale(feed_pre)
        output_rows.append((resid + feed_pre * feed_scale * feed_gain).astype(BF))

        cot = cot_rows[h].astype(F32)
        grad_feed = gather_rows(rms_back(feed_pre, feed_scale, feed_gain, cot).astype(BF))
        grad_feed_low = dot_nt(grad_feed, feed_up).astype(BF)
        grad_act = dot_nt(grad_feed, w_down) + dot(grad_feed_low, own_down)
        down_a += dot_tn(grad_feed_low, activation)
        feed_b += dot_tn(feed_low, grad_feed)
        grad_up = (grad_act * gate_pre * gate_sig).astype(BF)
        grad_gate = (
            grad_act * up_pre * gate_sig * (1.0 + gate_pre * (1.0 - gate_sig))
        ).astype(BF)
        gate_b += dot_tn(gate_low[:, :rank], grad_gate)
        up_b += dot_tn(gate_low[:, rank:], grad_up)
        grad_gate_low = jnp.concatenate(
            [dot_nt(grad_gate, own_hidden[0]), dot_nt(grad_up, own_hidden[1])], axis=1
        ).astype(BF)
        gate_up_a += dot_tn(grad_gate_low, resid_low)
        grad_resid = cot + scatter_rows(
            dot_nt(grad_gate, w_gate) + dot_nt(grad_up, w_up) + dot(grad_gate_low, gate_downs)
        )
        grad_resid_rows.append(grad_resid)
        grad_attn = gather_rows(rms_back(attn_pre, attn_scale, attn_gain, grad_resid).astype(BF))
        grad_out_low = dot_nt(grad_attn, out_up).astype(BF)
        out_a += dot_tn(grad_out_low, mix)
        out_b += dot_tn(out_low, grad_attn)
        grad_mixed_chunks.append(
            (dot_nt(grad_attn, w_out) + dot(grad_out_low, own_wide[3])).astype(BF)
        )
    output = from_groups(unchunked(output_rows))
    grad_mixed = jnp.concatenate(grad_mixed_chunks) if CHUNKS > 1 else grad_mixed_chunks[0]
    feed_gate = scatter_columns(jnp.concatenate([feed_b, gate_up_a]), shard)

    grad_heads = as_heads(grad_mixed)
    grad_probs = jnp.einsum("qhd,khd->hqk", grad_heads, value_all, preferred_element_type=F32)
    delta = jnp.sum(probs * grad_probs, axis=-1, keepdims=True)
    grad_scores = (probs * (grad_probs - delta)).astype(BF)
    grad_queries = factor * jnp.einsum(
        "hqk,khd->qhd", grad_scores, key_all, preferred_element_type=F32
    )
    grad_keys = factor * jnp.einsum(
        "hqk,qhd->khd", grad_scores, queries, preferred_element_type=F32
    )
    grad_values = jnp.einsum("hqk,qhd->khd", probs_low, grad_heads, preferred_element_type=F32)
    if per_sequence > 1:
        grad_keys, grad_values = [
            lax.psum_scatter(
                g.astype(BF), "ctx", scatter_dimension=0, tiled=True, axis_index_groups=groups
            ).astype(F32)
            for g in (grad_keys, grad_values)
        ]
    weighted = [
        rotate(g, cosine, -sine).reshape(total_rows, wide) * head_gain[p]
        for p, g in enumerate((grad_queries, grad_keys))
    ]
    inner = over_all_heads(jnp.stack([jnp.sum(weighted[p] * pre[p], axis=-1) for p in range(2)]))
    inner = (inner / D)[:, :, None]
    grad_pre = [
        (scales[p] * weighted[p] - pre[p] * (scales[p] * scales[p] * scales[p] * inner[p])).astype(BF)
        for p in range(2)
    ]
    grad_pre.append(grad_values.reshape(total_rows, wide).astype(BF))

    qkv_b = jnp.concatenate([dot_tn(lows[p], grad_pre[p]) for p in range(3)])
    grad_lows = jnp.concatenate(
        [dot_nt(grad_pre[p], own_model[p]) for p in range(3)], axis=1
    ).astype(BF)
    qkv_out = scatter_columns(jnp.concatenate([dot_tn(grad_lows, token_full), out_b]), shard)
    grad_tokens = dot(grad_lows, qkv_downs)
    for p in range(3):
        grad_tokens += dot_nt(grad_pre[p], w_qkv[p])
    input_rows = [
        grad_resid_rows[h] + scatter_rows(chunk_of(grad_tokens, h)) for h in range(CHUNKS)
    ]
    input_grad = from_groups([x.astype(BF) for x in unchunked(input_rows)]).astype(F32)

    narrow = jnp.concatenate(
        [
            qkv_out[: 3 * rank],
            out_a,
            feed_gate[rank:],
            qkv_b,
            qkv_out[3 * rank :],
            feed_gate[:rank],
        ]
    ).astype(BF)
    broad = jnp.concatenate([down_a, gate_b, up_b]).astype(BF)
    narrow_all = lax.all_gather(narrow, "ctx", axis=0)
    broad_all = lax.all_gather(broad, "ctx", axis=0)
    group_table = jnp.array(groups, jnp.int32)
    sequence_with = jnp.sum(
        jnp.where(
            index_all[None, :] == jnp.arange(adapters, dtype=jnp.int32)[:, None],
            jnp.arange(batch, dtype=jnp.int32)[None, :],
            0,
        ),
        axis=1,
    )

    def by_adapter(gathered):
        out = []
        for n in range(adapters):
            total = 0.0
            for k in range(per_sequence):
                total += lax.dynamic_index_in_dim(
                    gathered, group_table[sequence_with[n], k], 0, keepdims=False
                ).astype(F32)
            out.append(total)
        return jnp.stack(out, axis=0)

    narrow_out = by_adapter(narrow_all).reshape(adapters, 11, rank, wide).transpose(1, 0, 2, 3)
    broad_out = by_adapter(broad_all).reshape(adapters, 3, rank, -1).transpose(1, 0, 2, 3)
    return (
        output,
        input_grad,
        narrow_out[:6],
        broad_out[0],
        narrow_out[6:],
        broad_out[1:],
    )


def solution(mesh):
    return jax.shard_map(
        on_device,
        mesh=mesh,
        in_specs=(
            P("shard", "ctx", None),
            P("shard", "ctx", None),
            P("shard", None),
            P(None, "shard", None),
            P(None, "shard", None),
            P("shard", None),
            P(None, "shard"),
            P(None, None, None, "shard"),
            P(None, None, "shard"),
            P(None, None, None, "shard"),
            P(None, None, None, "shard"),
        ),
        out_specs=(
            P("shard", "ctx", None),
            P("shard", "ctx", None),
            P(None, None, None, "shard"),
            P(None, None, "shard"),
            P(None, None, None, "shard"),
            P(None, None, None, "shard"),
        ),
        check_vma=False,
    )
```

```python
import functools
import math

import jax
import jax.numpy as jnp
from jax import lax
from jax.experimental import pallas as pl
from jax.experimental.pallas import tpu as pltpu
from jax.sharding import PartitionSpec as P

D = 2048
HEADS = 16
HD = 128
BLOCK = 256

epsilon = 1e-06
rope_base = 500000.0
far_below = -1e30
BF = jnp.bfloat16
F32 = jnp.float32
VMEM_BYTES = 60 * 2**20


def dot(left, right):
    return lax.dot_general(left, right, (((1,), (0,)), ((), ())), preferred_element_type=F32)


def dot_nt(left, right):
    return lax.dot_general(left, right, (((1,), (1,)), ((), ())), preferred_element_type=F32)


def dot_tn(left, right):
    return lax.dot_general(left, right, (((0,), (0,)), ((), ())), preferred_element_type=F32)


def over_shard(value, flip):
    size = lax.axis_size("shard")
    return lax.ppermute(value, "shard", [(i, i ^ flip) for i in range(size)])


def after(value, *others):
    return jax.tree.map(lambda leaf: lax.optimization_barrier((leaf, others))[0], value)


def side_by_side(run, inputs, sends):
    inputs, values = lax.optimization_barrier((inputs, [value for _, value in sends]))
    got = [send(value) for (send, _), value in zip(sends, values)]
    out = run(inputs) if run else None
    return lax.optimization_barrier((out, got))


def over_ctx(value, flip):
    size = lax.axis_size("ctx")
    return lax.ppermute(value, "ctx", [(i, i ^ flip) for i in range(size)])


FLIPS = (0, 2, 1, 3)


def call(body, grid, args, in_specs, outs, scratch=(), scalars=(), flops=0):
    return pl.pallas_call(
        body,
        grid_spec=pltpu.PrefetchScalarGridSpec(
            num_scalar_prefetch=len(scalars),
            grid=grid,
            in_specs=in_specs,
            out_specs=[spec for _, spec in outs],
            scratch_shapes=scratch,
        ),
        out_shape=[shape for shape, _ in outs],
        compiler_params=pltpu.CompilerParams(vmem_limit_bytes=VMEM_BYTES),
        cost_estimate=pl.CostEstimate(flops=flops, bytes_accessed=0, transcendentals=0),
    )(*scalars, *args)


def shape_of(shape, kind):
    return jax.ShapeDtypeStruct(shape, kind)


def whole(value):
    zeros = (0,) * value.ndim
    return pl.BlockSpec(value.shape, lambda *_: zeros)


def spec(block, index):
    return pl.BlockSpec(block, lambda i, *_: index(i))


ANY = pl.BlockSpec(memory_space=pl.ANY)


def tile_of(width):
    return min(512, width)


def cut_body(places, near, far, cross, near_out, *far_outs):
    near_out[...] = near[...]
    for at, far_out in enumerate(far_outs):

        @pl.when((pl.program_id(0) == at) | (len(far_outs) == 1))
        def _():
            far_out[0] = far[...]
            far_out[1] = cross[...]


def cut(weight, first, count, shard, ctx, apart):
    depth, full = weight.shape[1:]
    width, slim = full // 4, depth // 4
    tile = tile_of(width)
    steps = width // tile
    places = jnp.stack([shard, ctx % 4]).astype(jnp.int32)

    def source(flip, rows, moves):
        def index(m, i, places):
            return first + m, places[1] if moves else 0, (places[0] ^ flip) * steps + i

        return pl.BlockSpec((1, rows, tile), index)

    if apart:
        far = [
            (
                shape_of((2, 1, slim, width), BF),
                pl.BlockSpec(
                    (2, 1, slim, tile),
                    lambda m, i, _, at=at: (0, 0, 0, jnp.where(m == at, i, jnp.where(m < at, 0, steps - 1))),
                ),
            )
            for at in range(count)
        ]
    else:
        far = [
            (
                shape_of((2, count, slim, width), BF),
                pl.BlockSpec((2, 1, slim, tile), lambda m, i, _: (0, m, 0, i)),
            )
        ]
    return call(
        cut_body,
        (count, steps),
        [weight] * 3,
        [source(1, depth, False), source(2, slim, True), source(3, slim, True)],
        [(shape_of((count, depth, width), BF), pl.BlockSpec((1, depth, tile), lambda m, i, _: (m, 0, i)))] + far,
        scalars=[places],
    )


def share(got):
    return jnp.stack([got[0], over_shard(got[1], 1)])


def beside(mine):
    return [over_ctx(mine, 1), over_ctx(mine, 2)]


def ends(from_x, from_z):
    return [from_z[0], from_x[1]]


def last(pieces):
    return [over_ctx(pieces[0], 1), over_ctx(pieces[1], 2)]


COPIES = 10
PARTS = 6


def copies_of(weight, first, count, parts, places, held, sems, columns, near_first=0):
    near, mine, from_x, from_z, *ends = parts
    depth, width = near.shape[1:]
    slim = depth // 4
    shard, quarter = places[0], places[1]
    own_columns = pl.ds(pl.multiple_of(shard * width + columns.start, columns.size), columns.size)

    def to(flip, rows, begin=0):
        start = pl.multiple_of((shard ^ flip) * depth + begin, slim)
        return held.at[:, pl.ds(start, rows), columns]

    pairs = [
        [(weight.at[pl.ds(first, count), :, own_columns], to(0, depth))],
        [(near.at[pl.ds(near_first, count), :, columns], to(1, depth))],
    ]
    for place, flip in enumerate((2, 3)):
        pairs.append(
            [
                (piece.at[place, :, :, columns], to(flip, slim, (quarter ^ turn) * slim))
                for turn, piece in enumerate((mine, from_x, from_z))
            ]
            + [(ends[place].at[:, :, columns], to(flip, slim, (quarter ^ 3) * slim))]
        )
    out, at = [], 0
    for group in pairs:
        out.append([])
        for source, target in group:
            out[-1].append(pltpu.make_async_copy(source, target, sems.at[at]))
            at += 1
    return out


def row_of(column):
    return jnp.transpose(jnp.broadcast_to(column, (column.shape[0], 128)))[:8]


def column_of(row):
    return jnp.transpose(jnp.broadcast_to(row[:1], (128, row.shape[1])))[:, :1]


def qkv_body(chunks, size, places, *refs):
    x_refs, refs = refs[:3], refs[3:]
    weight, weight_parts, (down, up, pre, low, sums, rows, held, sems) = refs[0], refs[1 : 1 + PARTS], refs[1 + PARTS :]
    step = pl.program_id(0)
    everything = pl.ds(0, held.shape[-1])

    def copies(p):
        own = [weight_parts[0]]
        own += [part.at[:, pl.ds(p, 1)] for part in weight_parts[1:4]]
        own += [part.at[pl.ds(p, 1)] for part in weight_parts[4:]]
        groups = copies_of(weight, p, 1, own, places, held.at[pl.ds(p, 1)], sems.at[p], everything, p)
        return [copy for group in groups for copy in group]

    @pl.when(step == 0)
    def _():
        for p in range(held.shape[0]):
            for copy in copies(p):
                copy.start()
        for h in range(chunks):
            rows[4 * h * size : 4 * (h + 1) * size] = load_parts(x_refs, h * size, size)

    lowrank = dot_nt(rows[...], down[...]).astype(BF)
    for copy in copies(step):
        copy.wait()
    value = dot(rows[...], held[step]) + dot(lowrank, up[0])
    pre[0] = value.astype(BF)
    low[0] = lowrank
    sums[...] = row_of(jnp.sum(value * value, axis=1, keepdims=True))


def qkv_forward(x_parts, chunks, size, weight, weight_parts, places, downs, ups):
    count, depth, width = weight_parts[0].shape
    full = x_parts[0].shape[1]
    total, rank = 4 * chunks * size, ups.shape[1]
    return call(
        functools.partial(qkv_body, chunks, size),
        (count,),
        [*x_parts, weight, *weight_parts, downs, ups],
        [whole(x) for x in x_parts]
        + [ANY] * (1 + PARTS)
        + [
            spec((rank, full), lambda p: (p, 0)),
            spec((1, rank, width), lambda p: (p, 0, 0)),
        ],
        [
            (shape_of((count, total, width), BF), spec((1, total, width), lambda p: (p, 0, 0))),
            (shape_of((count, total, rank), BF), spec((1, total, rank), lambda p: (p, 0, 0))),
            (shape_of((8 * count, total), F32), spec((8, total), lambda p: (p, 0))),
        ],
        [
            pltpu.VMEM((total, full), BF),
            pltpu.VMEM((count, full, width), BF),
            pltpu.SemaphoreType.DMA((count, COPIES)),
        ],
        [places],
    )


def aligned_sums(refs, which, chunks):
    total = refs[0].shape[1]
    block = total // (4 * chunks)
    out = 0.0
    for flip, ref in zip(FLIPS, refs):
        column = column_of(ref[8 * which : 8 * which + 8])
        if flip:
            order = [FLIPS.index(f ^ flip) for f in FLIPS]
            column = jnp.concatenate(
                [
                    column[(4 * h + i) * block : (4 * h + i + 1) * block]
                    for h in range(chunks)
                    for i in order
                ]
            )
        out = out + column
    return out


def attention_body(chunks, factor, *refs):
    (
        query_pre, key_pre, value, own, far, near, cross, cosine, sine, gains,
        query_out, key_out, mixed_out, logs_out, scale_rows,
    ) = refs
    total = query_pre.shape[1]
    size = total // chunks

    @pl.when(pl.program_id(0) == 0)
    def _():
        for p in range(2):
            sums = aligned_sums((own, far, near, cross), p, chunks)
            scale_rows[p] = jnp.broadcast_to(lax.rsqrt(sums / D + epsilon), (total, HD))

    def prepared(pre, p):
        value = pre[0].astype(F32) * scale_rows[p] * gains[p : p + 1]
        return (value * cosine[...] + pltpu.roll(value, HD // 2, 1) * sine[...]).astype(BF)

    query, key = prepared(query_pre, 0), prepared(key_pre, 1)
    query_out[...] = query
    key_out[...] = key
    logs = []
    for h in range(chunks):
        seen = (h + 1) * size
        scores = dot_nt(query[h * size : (h + 1) * size], key[:seen]) * factor
        top = jnp.max(scores, axis=1, keepdims=True)
        weights = jnp.exp(scores - top)
        sums = jnp.sum(weights, axis=1, keepdims=True)
        probs = (weights * (1.0 / sums)).astype(BF)
        mixed_out[h * size : (h + 1) * size] = dot(probs, value[0, :seen]).astype(BF)
        logs.append(top + jnp.log(sums))
    logs_out[...] = row_of(jnp.concatenate(logs))


def attention_forward(pre, sums, cosine, sine, gains, chunks):
    _, total, width = pre.shape
    heads = width // HD
    factor = 1.0 / math.sqrt(HD)

    def head(p):
        return spec((1, total, HD), lambda i: (p, 0, i))

    by_head = spec((total, HD), lambda i: (0, i))
    return call(
        functools.partial(attention_body, chunks, factor),
        (heads,),
        [pre, pre, pre, *sums, cosine, sine, gains],
        [head(0), head(1), head(2)]
        + [whole(s) for s in sums]
        + [whole(cosine), whole(sine), spec((gains.shape[0], HD), lambda i: (0, i))],
        [
            (shape_of((total, width), BF), by_head),
            (shape_of((total, width), BF), by_head),
            (shape_of((total, width), BF), by_head),
            (shape_of((8 * heads, total), F32), spec((8, total), lambda i: (i, 0))),
        ],
        [pltpu.VMEM((2, total, HD), F32)],
        flops=4 * total * total * width,
    )


def attention_back_body(chunks, factor, *refs):
    (
        query_in, key_in, query_pre, key_pre, value, grad_in, logs, cosine, sine, gains,
        query_out, key_out, value_out, inner_out, inner_rows,
    ) = refs
    total = query_in.shape[0]
    size = total // chunks
    head = pl.program_id(0)
    query, key, values, grad = query_in[...], key_in[...], value[0], grad_in[...]
    log_column = column_of(logs[...])
    grad_key = [0.0] * chunks
    grad_value = [0.0] * chunks
    grad_query = []
    for h in range(chunks):
        rows = slice(h * size, (h + 1) * size)
        grad_row = 0.0
        delta = 0.0
        kept = []
        for k in range(h + 1):
            keys = slice(k * size, (k + 1) * size)
            scores = dot_nt(query[rows], key[keys]) * factor
            probs = jnp.exp(scores - log_column[rows])
            grad_probs = dot_nt(grad[rows], values[keys])
            delta = delta + jnp.sum(probs * grad_probs, axis=1, keepdims=True)
            kept.append((probs, grad_probs))
        for k, (probs, grad_probs) in enumerate(kept):
            keys = slice(k * size, (k + 1) * size)
            grad_scores = (probs * (grad_probs - delta)).astype(BF)
            grad_row = grad_row + dot(grad_scores, key[keys])
            grad_key[k] = grad_key[k] + dot_tn(grad_scores, query[rows])
            grad_value[k] = grad_value[k] + dot_tn(probs.astype(BF), grad[rows])
        grad_query.append(grad_row)

    value_out[...] = jnp.concatenate(grad_value).astype(BF)
    for p, (pre, grads, out) in enumerate(
        ((query_pre, grad_query, query_out), (key_pre, grad_key, key_out))
    ):
        turned = jnp.concatenate(grads) * factor
        turned = turned * cosine[...] - pltpu.roll(turned, HD // 2, 1) * sine[...]
        turned = turned * gains[p : p + 1]
        out[...] = turned.astype(BF)
        inner = jnp.sum(turned * pre[0].astype(F32), axis=1, keepdims=True)
        inner = jnp.broadcast_to(inner, (total, 128))

        @pl.when(head == 0)
        def _():
            inner_rows[p] = inner

        @pl.when(head > 0)
        def _():
            inner_rows[p] += inner

    @pl.when(head == pl.num_programs(0) - 1)
    def _():
        for p in range(2):
            inner_out[8 * p : 8 * p + 8] = jnp.transpose(inner_rows[p])[:8]


def attention_back(queries, key_rows, pre, grad_mixed, logs, cosine, sine, gains, chunks):
    _, total, width = pre.shape
    heads = width // HD
    factor = 1.0 / math.sqrt(HD)

    def head(p):
        return spec((1, total, HD), lambda i: (p, 0, i))

    by_head = spec((total, HD), lambda i: (0, i))
    return call(
        functools.partial(attention_back_body, chunks, factor),
        (heads,),
        [queries, key_rows, pre, pre, pre, grad_mixed, logs, cosine, sine, gains],
        [by_head, by_head, head(0), head(1), head(2), by_head]
        + [spec((8, total), lambda i: (i, 0)), whole(cosine), whole(sine)]
        + [spec((gains.shape[0], HD), lambda i: (0, i))],
        [
            (shape_of((total, width), BF), by_head),
            (shape_of((total, width), BF), by_head),
            (shape_of((total, width), BF), by_head),
            (shape_of((16, total), F32), pl.BlockSpec((16, total), lambda *_: (0, 0))),
        ],
        [pltpu.VMEM((2, total, 128), F32)],
        flops=10 * total * total * width,
    )


def split_out(value, keep, send, columns=slice(None)):
    half = value.shape[0] // 2
    keep[:, columns] = value[:half].astype(BF)
    send[:, columns] = value[half:].astype(BF)


def back_columns(low, downs, x_refs, first, places, flip, depth):
    columns = pl.ds(pl.multiple_of((places[0] ^ flip) * depth, depth), depth)
    x = load_parts(x_refs, first, low.shape[0] // 4, columns)
    return columns, dot(low, downs[:, columns]), dot_tn(low, x)


def qkv_back_body(chunks, chunk, places, *refs):
    query_grad, key_grad, value_grad, query_pre, key_pre = refs[:5]
    squares, inners = refs[5:9], refs[9:13]
    x_refs = refs[13:16]
    weight, weight_parts, refs = refs[16], refs[17 : 17 + PARTS], refs[17 + PARTS :]
    low, downs, ups, keep, send, down_out, up_out, grads, lows, held, sems = refs
    rank = ups.shape[1]
    size = query_grad.shape[0]
    groups = copies_of(weight, 0, 3, weight_parts, places, held, sems, pl.ds(0, held.shape[-1]))
    for group in groups:
        for copy in group:
            copy.start()
    rows = slice(chunk * size, (chunk + 1) * size)
    for p, (grad, pre) in enumerate(((query_grad, query_pre), (key_grad, key_pre))):
        scale = lax.rsqrt(aligned_sums(squares, p, chunks)[rows] / D + epsilon)
        inner = aligned_sums(inners, p, chunks)[rows] * (scale * scale * scale / D)
        grads[p] = (grad[...].astype(F32) * scale - pre[0].astype(F32) * inner).astype(BF)
    grads[2] = value_grad[...]
    for p in range(3):
        lows[:, p * rank : (p + 1) * rank] = dot_nt(grads[p], ups[p]).astype(BF)
        up_out[p] = dot_tn(low[p], grads[p])

    depth = held.shape[1] // 4
    for flip, group in enumerate(groups):
        first = chunk * size // 4
        columns, value, down_out[:, columns] = back_columns(
            lows[...], downs, x_refs, first, places, flip, depth
        )
        for copy in group:
            copy.wait()
        for p in range(3):
            value += dot_nt(grads[p], held[p, columns])
        split_out(value, keep, send, columns)


def qkv_back(
    turned, grad_values, pre, squares, inners, x_parts, weight, weight_parts, places, low, downs, ups, chunks, chunk
):
    count, depth, width = weight_parts[0].shape
    total = pre.shape[1]
    size = total // chunks
    full = x_parts[0].shape[1]
    rank = ups.shape[1]
    rows = pl.BlockSpec((size, width), lambda *_: (chunk, 0))

    def pre_rows(p):
        return pl.BlockSpec((1, size, width), lambda *_: (p, chunk, 0))

    half = size // 2
    outs = [
        shape_of((half, full), BF),
        shape_of((half, full), BF),
        shape_of((count * rank, full), F32),
        shape_of((count, rank, width), F32),
    ]
    return call(
        functools.partial(qkv_back_body, chunks, chunk),
        (1,),
        [*turned, grad_values, pre, pre, *squares, *inners, *x_parts, weight, *weight_parts, low, downs, ups],
        [rows, rows, rows, pre_rows(0), pre_rows(1)]
        + [whole(v) for v in (*squares, *inners, *x_parts)]
        + [ANY] * (1 + PARTS)
        + [pl.BlockSpec((count, size, rank), lambda *_: (0, chunk, 0)), whole(downs), whole(ups)],
        [(o, whole(o)) for o in outs],
        [
            pltpu.VMEM((count, size, width), BF),
            pltpu.VMEM((size, count * rank), BF),
            pltpu.VMEM((count, full, width), BF),
            pltpu.SemaphoreType.DMA((COPIES,)),
        ],
        [places],
        flops=2 * size * full * width * count,
    )


def partial_body(*refs):
    x, weight, down, up, keep, send, low = refs

    @pl.when(pl.program_id(0) == 0)
    def _():
        low[...] = dot_nt(x[...], down[...]).astype(BF)

    tile = weight.reshape(weight.shape[-2:]) if weight.ndim == 3 else weight
    split_out(dot(x[...], tile[...]) + dot(low[...], up[...]), keep, send)


def partial_forward(x, chunk, chunks, weight, matrix, down, up):
    total, depth = x.shape
    size = total // chunks
    full = weight.shape[-1]
    tile = tile_of(full)
    half = size // 2
    rank = down.shape[0]
    if weight.ndim == 3:
        weight_spec = spec((1, depth, tile), lambda i: (matrix, 0, i))
    else:
        weight_spec = spec((depth, tile), lambda i: (0, i))
    return call(
        partial_body,
        (full // tile,),
        [x, weight, down, up],
        [
            pl.BlockSpec((size, depth), lambda *_: (chunk, 0)),
            weight_spec,
            whole(down),
            spec((rank, tile), lambda i: (0, i)),
        ],
        [
            (shape_of((half, full), BF), spec((half, tile), lambda i: (0, i))),
            (shape_of((half, full), BF), spec((half, tile), lambda i: (0, i))),
            (shape_of((size, rank), BF), pl.BlockSpec((size, rank), lambda *_: (0, 0))),
        ],
        flops=2 * size * depth * full,
    )


def gate_up_body(places, *refs):
    x_refs, weight, refs = refs[:3], refs[3], refs[4:]
    gate_parts, up_parts, refs = refs[:PARTS], refs[PARTS : 2 * PARTS], refs[2 * PARTS :]
    downs, ups, gate, upper, act, low, rows, gate_held, up_held, sems = refs
    rank = ups.shape[1]
    tile = gate.shape[1]
    step, steps = pl.program_id(0), pl.num_programs(0)

    def tile_columns(i):
        return pl.ds(pl.multiple_of(i * tile, tile), tile)

    def copies(i):
        columns = tile_columns(i)
        groups = copies_of(weight, 0, 1, gate_parts, places, gate_held, sems.at[0, i], columns)
        groups += copies_of(weight, 1, 1, up_parts, places, up_held, sems.at[1, i], columns, 1)
        return [copy for group in groups for copy in group]

    @pl.when(step == 0)
    def _():
        for copy in copies(0):
            copy.start()
        rows[...] = load_parts(x_refs)
        low[...] = dot_nt(rows[...], downs[...]).astype(BF)

    @pl.when(step + 1 < steps)
    def _():
        for copy in copies(step + 1):
            copy.start()

    for copy in copies(step):
        copy.wait()
    columns = tile_columns(step)
    gate_pre = dot(rows[...], gate_held[0, :, columns]) + dot(low[:, :rank], ups[0])
    upper_pre = dot(rows[...], up_held[0, :, columns]) + dot(low[:, rank:], ups[1])
    gate[...] = gate_pre.astype(BF)
    upper[...] = upper_pre.astype(BF)
    act[...] = (gate_pre * jax.nn.sigmoid(gate_pre) * upper_pre).astype(BF)


def gate_up_forward(x_parts, weight, gate_parts, up_parts, places, downs, ups):
    _, depth, width = gate_parts[0].shape
    full = x_parts[0].shape[1]
    size = 4 * x_parts[0].shape[0]
    rank = ups.shape[1]
    tile = tile_of(width)
    steps = width // tile
    out = (shape_of((size, width), BF), spec((size, tile), lambda i: (0, i)))
    return call(
        gate_up_body,
        (steps,),
        [*x_parts, weight, *gate_parts, *up_parts, downs, ups],
        [whole(x) for x in x_parts]
        + [ANY] * (1 + 2 * PARTS)
        + [whole(downs), spec((2, rank, tile), lambda i: (0, 0, i))],
        [
            out,
            out,
            out,
            (shape_of((size, 2 * rank), BF), pl.BlockSpec((size, 2 * rank), lambda *_: (0, 0))),
        ],
        [
            pltpu.VMEM((size, full), BF),
            pltpu.VMEM((1, full, width), BF),
            pltpu.VMEM((1, full, width), BF),
            pltpu.SemaphoreType.DMA((2, steps, COPIES)),
        ],
        [places],
        flops=4 * size * full * width,
    )


def feed_back_body(*refs):
    g_refs = refs[:3]
    weight, down, gate, upper, gate_low, feed_low, feed_up, ups = refs[3:11]
    gate_grad, upper_grad, low_out, down_a, feed_b, hidden_b, rows, low, lows = refs[11:]
    rank = down.shape[0]
    step = pl.program_id(0)

    @pl.when(step == 0)
    def _():
        rows[...] = load_parts(g_refs)
        low[...] = dot_nt(rows[...], feed_up[...]).astype(BF)
        feed_b[...] = dot_tn(feed_low[...], rows[...])
        lows[...] = jnp.zeros_like(lows)

    grad_act = dot_nt(rows[...], weight[...]) + dot(low[...], down[...])
    gate_pre, upper_pre = gate[...].astype(F32), upper[...].astype(F32)
    sig = jax.nn.sigmoid(gate_pre)
    silu = gate_pre * sig
    down_a[...] = dot_tn(low[...], (silu * upper_pre).astype(BF))
    grad_upper = (grad_act * silu).astype(BF)
    grad_gate = (grad_act * upper_pre * (sig + silu * (1.0 - sig))).astype(BF)
    gate_grad[...] = grad_gate
    upper_grad[...] = grad_upper
    hidden_b[0] = dot_tn(gate_low[:, :rank], grad_gate)
    hidden_b[1] = dot_tn(gate_low[:, rank:], grad_upper)
    lows[:, :rank] += dot_nt(grad_gate, ups[0])
    lows[:, rank:] += dot_nt(grad_upper, ups[1])

    @pl.when(step == pl.num_programs(0) - 1)
    def _():
        low_out[...] = lows[...].astype(BF)


def feed_back(g_parts, weight, down, gate, upper, gate_low, feed_low, feed_up, ups):
    width, depth = weight.shape
    size = 4 * g_parts[0].shape[0]
    rank = down.shape[0]
    tile = tile_of(width)
    by_tile = spec((size, tile), lambda i: (0, i))
    return call(
        feed_back_body,
        (width // tile,),
        [*g_parts, weight, down, gate, upper, gate_low, feed_low, feed_up, ups],
        [whole(g) for g in g_parts]
        + [
            spec((tile, depth), lambda i: (i, 0)),
            spec((rank, tile), lambda i: (0, i)),
            by_tile,
            by_tile,
            whole(gate_low),
            whole(feed_low),
            whole(feed_up),
            spec((2, rank, tile), lambda i: (0, 0, i)),
        ],
        [
            (shape_of((size, width), BF), by_tile),
            (shape_of((size, width), BF), by_tile),
            (shape_of((size, 2 * rank), BF), pl.BlockSpec((size, 2 * rank), lambda *_: (0, 0))),
            (shape_of((rank, width), F32), spec((rank, tile), lambda i: (0, i))),
            (shape_of((rank, depth), F32), pl.BlockSpec((rank, depth), lambda *_: (0, 0))),
            (shape_of((2, rank, width), F32), spec((2, rank, tile), lambda i: (0, 0, i))),
        ],
        [
            pltpu.VMEM((size, depth), BF),
            pltpu.VMEM((size, rank), BF),
            pltpu.VMEM((size, 2 * rank), F32),
        ],
        flops=2 * size * depth * width,
    )


def gate_up_back_body(places, *refs):
    gate_grad, upper_grad, weight, refs = refs[0], refs[1], refs[2], refs[3:]
    gate_parts, up_parts, refs = refs[:PARTS], refs[PARTS : 2 * PARTS], refs[2 * PARTS :]
    low, downs, x_refs, refs = refs[0], refs[1], refs[2:5], refs[5:]
    keep, send, down_out, gate_held, up_held, sems = refs
    everything = pl.ds(0, gate_held.shape[-1])
    gate_groups = copies_of(weight, 0, 1, gate_parts, places, gate_held, sems.at[0], everything)
    up_groups = copies_of(weight, 1, 1, up_parts, places, up_held, sems.at[1], everything, 1)
    groups = [gate_group + up_group for gate_group, up_group in zip(gate_groups, up_groups)]
    for group in groups:
        for copy in group:
            copy.start()
    depth = gate_held.shape[1] // 4
    for flip, group in enumerate(groups):
        columns, value, down_out[:, columns] = back_columns(
            low[...], downs, x_refs, 0, places, flip, depth
        )
        for copy in group:
            copy.wait()
        value += dot_nt(gate_grad[...], gate_held[0, columns])
        value += dot_nt(upper_grad[...], up_held[0, columns])
        split_out(value, keep, send, columns)


def gate_up_back(gate_grad, upper_grad, weight, gate_parts, up_parts, places, low, downs, x_parts):
    _, depth, width = gate_parts[0].shape
    full = x_parts[0].shape[1]
    size = gate_grad.shape[0]
    half = size // 2
    ranks = downs.shape[0]
    outs = [shape_of((half, full), BF), shape_of((half, full), BF), shape_of((ranks, full), F32)]
    return call(
        gate_up_back_body,
        (1,),
        [gate_grad, upper_grad, weight, *gate_parts, *up_parts, low, downs, *x_parts],
        [whole(gate_grad), whole(upper_grad)]
        + [ANY] * (1 + 2 * PARTS)
        + [whole(v) for v in (low, downs, *x_parts)],
        [(o, whole(o)) for o in outs],
        [
            pltpu.VMEM((1, full, width), BF),
            pltpu.VMEM((1, full, width), BF),
            pltpu.SemaphoreType.DMA((2, COPIES)),
        ],
        [places],
        flops=4 * size * full * width,
    )


def out_back_body(*refs):
    g_refs = refs[:3]
    weight, down, up, mixed, low, grad_mixed, down_out, up_out, rows, grad_low = refs[3:]

    @pl.when(pl.program_id(0) == 0)
    def _():
        rows[...] = load_parts(g_refs)
        grad_low[...] = dot_nt(rows[...], up[...]).astype(BF)
        up_out[...] = dot_tn(low[...], rows[...])

    grad_mixed[...] = (dot_nt(rows[...], weight[0]) + dot(grad_low[...], down[...])).astype(BF)
    down_out[...] = dot_tn(grad_low[...], mixed[...])


def out_back(g_parts, weight, matrix, down, up, mixed, low, chunk):
    _, width, depth = weight.shape
    size = 4 * g_parts[0].shape[0]
    rank = down.shape[0]
    tile = min(256, width)
    return call(
        out_back_body,
        (width // tile,),
        [*g_parts, weight, down, up, mixed, low],
        [whole(g) for g in g_parts]
        + [
            spec((1, tile, depth), lambda i: (matrix, i, 0)),
            spec((rank, tile), lambda i: (0, i)),
            whole(up),
            spec((size, tile), lambda i: (chunk, i)),
            whole(low),
        ],
        [
            (shape_of((size, width), BF), spec((size, tile), lambda i: (0, i))),
            (shape_of((rank, width), F32), spec((rank, tile), lambda i: (0, i))),
            (shape_of((rank, depth), F32), pl.BlockSpec((rank, depth), lambda *_: (0, 0))),
        ],
        [pltpu.VMEM((size, depth), BF), pltpu.VMEM((size, rank), BF)],
        flops=2 * size * depth * width,
    )


def gather_parts(own):
    far = over_shard(own, 2)
    near = over_shard(jnp.stack([own, far]), 1)
    return [own, far, near]


def load_parts(refs, first=0, count=None, columns=slice(None)):
    own, far, near = refs
    rows = slice(first, own.shape[0] if count is None else first + count)
    return jnp.concatenate(
        [own[rows, columns], far[rows, columns], near[0, rows, columns], near[1, rows, columns]]
    )


def scatter_parts(keep, send):
    got = over_shard(send, 1)
    rows = keep.shape[0] // 2
    far = (keep[rows:].astype(F32) + got[rows:].astype(F32)).astype(BF)
    far = over_shard(far, 2)
    return keep[:rows].astype(F32) + got[:rows].astype(F32) + far.astype(F32)


def ctx_flips():
    size = lax.axis_size("ctx")
    return [flip for flip in (2, 4, 8, 16, 1) if flip < size]


def gather_ctx(value):
    value = value[None]
    for flip in ctx_flips():
        value = jnp.concatenate([value, over_ctx(value, flip)])
    return value


def gathered_place(ctx, other):
    place = 0
    for at, flip in enumerate(ctx_flips()):
        place = place + (((ctx ^ other) // flip) % 2) * 2**at
    return place


def column_block(value, index, width):
    return lax.dynamic_slice_in_dim(value, index * width, width, value.ndim - 1)


def scatter_columns(partial, shard):
    width = partial.shape[-1] // 4
    blocks = [column_block(partial, shard ^ flip, width) for flip in FLIPS]
    got = over_shard(jnp.stack(blocks[2:]).astype(BF), 1).astype(F32)
    far = (blocks[1] + got[1]).astype(BF)
    return blocks[0] + got[0] + over_shard(far, 2).astype(F32)


def natural(parts, shard):
    out = []
    for index in range(4):
        value = parts[0]
        for flip, part in zip(FLIPS[1:], parts[1:]):
            value = jnp.where((shard ^ flip) == index, part, value)
        out.append(value)
    return out


def rms_scale(value):
    return lax.rsqrt(jnp.mean(value * value, axis=-1, keepdims=True) + epsilon)


def rms_back(value, scale, gain, grad):
    weighted = grad * gain
    return scale * weighted - value * (
        scale * scale * scale * jnp.mean(value * weighted, axis=-1, keepdims=True)
    )


def rotate(value, cosine, sine):
    half = value.shape[-1] // 2
    turned = jnp.concatenate([value[..., half:], value[..., :half]], axis=-1)
    return value * cosine[:, None, :] + turned * sine[:, None, :]


def realign(value, flip, chunks):
    shape = value.shape
    value = value.reshape(shape[0], chunks, 2, 2, -1)
    if flip & 1:
        value = value[:, :, ::-1]
    if flip & 2:
        value = value[:, :, :, ::-1]
    return value.reshape(shape)


def group_of(sequence, part, per_sequence, ctx_size):
    if per_sequence > 1:
        return sequence * per_sequence + part
    depth = sequence % (ctx_size // 2)
    return 2 * depth + (depth + sequence // (ctx_size // 2)) % 2


def wide_attention(pre, sums, cosine, sine, gains, chunks, positions, groups):
    _, total, width = pre.shape
    heads = width // HD
    pre = pre.astype(F32)
    squares = sum(realign(s[::8], flip, chunks) for flip, s in zip(FLIPS, sums))
    scales = lax.rsqrt(squares[:2] / D + epsilon)[:, :, None]

    def as_heads(value):
        return value.reshape(total, heads, HD)

    queries, key_rows = [
        rotate(as_heads(pre[p] * scales[p] * gains[p]), cosine, sine).astype(BF) for p in range(2)
    ]

    def over_sequence(value):
        return lax.all_gather(value, "ctx", axis=0, tiled=True, axis_index_groups=groups)

    key_all, value_all = over_sequence(key_rows), over_sequence(as_heads(pre[2].astype(BF)))
    visible = over_sequence(positions // BLOCK)[None, :] <= (positions // BLOCK)[:, None]
    factor = 1.0 / math.sqrt(HD)
    scores = jnp.einsum("qhd,khd->hqk", queries, key_all, preferred_element_type=F32) * factor
    scores = jnp.where(visible, scores, far_below)
    weights = jnp.exp(scores - jnp.max(scores, axis=-1, keepdims=True))
    probs = weights / jnp.sum(weights, axis=-1, keepdims=True)
    mixed = jnp.einsum("hqk,khd->qhd", probs.astype(BF), value_all, preferred_element_type=F32)
    mixed = mixed.astype(BF).reshape(total, width)

    def back(grad_mixed):
        grad = as_heads(grad_mixed)
        grad_probs = jnp.einsum("qhd,khd->hqk", grad, value_all, preferred_element_type=F32)
        delta = jnp.sum(probs * grad_probs, axis=-1, keepdims=True)
        grad_scores = (probs * (grad_probs - delta)).astype(BF)
        grad_queries = jnp.einsum("hqk,khd->qhd", grad_scores, key_all, preferred_element_type=F32)
        grad_keys = jnp.einsum("hqk,qhd->khd", grad_scores, queries, preferred_element_type=F32)
        grad_values = jnp.einsum("hqk,qhd->khd", probs.astype(BF), grad, preferred_element_type=F32)
        grad_keys, grad_values = [
            lax.psum_scatter(
                g.astype(BF), "ctx", scatter_dimension=0, tiled=True, axis_index_groups=groups
            ).astype(F32)
            for g in (grad_keys * factor, grad_values)
        ]
        turned = [
            rotate(g, cosine, -sine).reshape(total, width) * gains[p]
            for p, g in enumerate((grad_queries * factor, grad_keys))
        ]
        inner = jnp.stack([jnp.sum(turned[p] * pre[p], axis=-1) for p in range(2)])
        inner = jnp.repeat(inner, 8, axis=0)
        values = grad_values.reshape(total, width).astype(BF)
        return turned[0].astype(BF), turned[1].astype(BF), values, inner

    return mixed, back


def choose_body(place, *refs):
    wide, down, model, hidden, gains, wide_out, down_out, model_out, hidden_out, small = refs
    wide_out[...] = wide[:, 0]
    down_out[...] = down[0]
    model_out[...] = model[:, 0]
    hidden_out[...] = hidden[:, 0]
    count, _, rank, width = wide.shape
    shared = [wide[p, 0] for p in (0, 1, 2, 4, 5)] + [model[p, 0] for p in (3, 4)]
    last = jnp.concatenate([gains[2:], jnp.zeros((rank - 2, width), BF)])
    for at, value in enumerate([*shared, last]):
        column = at // 2 * width
        small[at % 2 * rank : (at % 2 + 1) * rank, column : column + width] = value


def choose(place, a_wide, a_down, b_model, b_hidden, gains):
    rank, width = a_wide.shape[2:]
    shapes = [a_wide.shape[:1] + a_wide.shape[2:], a_down.shape[1:]]
    shapes += [b_model.shape[:1] + b_model.shape[2:], b_hidden.shape[:1] + b_hidden.shape[2:]]
    shapes.append((2 * rank, 4 * width))
    outs = [shape_of(s, BF) for s in shapes]
    return call(
        choose_body,
        (1,),
        [a_wide, a_down, b_model, b_hidden, gains],
        [
            pl.BlockSpec((a_wide.shape[0], 1, rank, width), lambda _, n: (0, n[0], 0, 0)),
            pl.BlockSpec((1,) + a_down.shape[1:], lambda _, n: (n[0], 0, 0)),
            pl.BlockSpec((b_model.shape[0], 1) + b_model.shape[2:], lambda _, n: (0, n[0], 0, 0)),
            pl.BlockSpec((b_hidden.shape[0], 1) + b_hidden.shape[2:], lambda _, n: (0, n[0], 0, 0)),
            whole(gains),
        ],
        [(o, whole(o)) for o in outs],
        scalars=[place],
    )


def place_body(rank, count, plan, at, *refs):
    sources, outs = refs[:count], refs[count:]
    for out, maps in zip(outs, plan):
        for n in range(out.shape[1]):
            for p, (source, place) in enumerate(maps):
                out[p, n] = sources[source][at[n], place * rank : (place + 1) * rank].astype(F32)


def on_device(
    tokens,
    cotangent,
    adapter_index,
    w_attn,
    w_gate_up,
    w_down,
    gains,
    a_wide,
    a_down,
    b_model,
    b_hidden,
):
    seqs, rows = tokens.shape[0], tokens.shape[1]
    shards, ctxs = lax.axis_size("shard"), lax.axis_size("ctx")
    shard, ctx = lax.axis_index("shard"), lax.axis_index("ctx")
    batch = seqs * shards
    per_sequence = ctxs // batch
    group_rows = batch * rows
    chunks = seqs
    chunk_rows = shards * rows
    wide = HEADS // shards * HD
    adapters, rank = a_down.shape[:2]

    groups = [[group_of(q, k, per_sequence, ctxs) for k in range(per_sequence)] for q in range(batch)]
    sequence_at, part_at = [0] * ctxs, [0] * ctxs
    for q in range(batch):
        for k in range(per_sequence):
            sequence_at[groups[q][k]] = q
            part_at[groups[q][k]] = k
    my_sequence = jnp.array(sequence_at, jnp.int32)[ctx]
    my_part = jnp.array(part_at, jnp.int32)[ctx]
    my_slot = my_sequence % seqs
    my_spot = (ctx % batch) // shards

    pairs = []
    for p in range(seqs):
        pairs.append([])
        for c in range(ctxs):
            for s in range(shards):
                k, local = c // batch, c % batch
                spot, owner = local // shards, local % shards
                to = groups[seqs * s + (p + spot) % seqs][k]
                pairs[p].append((c * shards + s, to * shards + owner))

    def pick(parts, index):
        value = parts[0]
        for at in range(1, len(parts)):
            value = jnp.where(index == at, parts[at], value)
        return value

    def cut_rows(*values):
        return [
            jnp.concatenate(
                [
                    lax.dynamic_index_in_dim(value, (p + my_spot) % seqs, 0, keepdims=False)
                    for value in values
                ]
            )
            for p in range(seqs)
        ]

    def send_rows(cuts):
        return [lax.ppermute(cut, ("ctx", "shard"), pairs[p]) for p, cut in enumerate(cuts)]

    def chunk_order(got):
        return [pick(got, (my_slot - h) % seqs) for h in range(seqs)]

    def return_cuts(parts):
        return [pick(parts, (my_slot - p) % seqs) for p in range(seqs)]

    def return_rows(cuts):
        return [
            lax.ppermute(cut, ("ctx", "shard"), [(b, a) for a, b in pairs[p]]) for p, cut in enumerate(cuts)
        ]

    def return_order(got):
        return jnp.stack([pick(got, (j - my_spot) % seqs) for j in range(seqs)])

    index_own = adapter_index[:, 0]
    index_all = jnp.concatenate(
        natural([index_own] + [over_shard(index_own, flip) for flip in FLIPS[1:]], shard)
    )
    qkv_near, qkv_far = cut(w_attn, 0, 3, shard, ctx, False)

    ready = (index_all, qkv_far)
    token_cuts = cut_rows(after(tokens, ready))
    qkv_got = over_shard(after(qkv_far, ready), 2)
    token_got = send_rows(token_cuts)
    qkv_near = over_shard(after(qkv_near, ready), 1)
    own_wide, own_down, own_model, own_hidden, small = choose(
        after(index_all[my_sequence], token_cuts)[None], a_wide, a_down, b_model, b_hidden, gains
    )
    gate_up_near, gate_far, up_far = cut(after(w_gate_up, small), 0, 2, shard, ctx, True)

    ready = (qkv_got, token_got, qkv_near, gate_far, up_far)
    qkv_mine = share(after(qkv_got, ready))
    qkv_beside = beside(qkv_mine)
    token_rows = chunk_order(after(token_got, ready))
    token_own = jnp.concatenate([*token_rows, small])
    token_far = over_shard(token_own, 2)
    gate_got = over_shard(after(gate_far, token_far), 2)
    ready = (qkv_beside, token_far)
    token_parts = [token_own, token_far, over_shard(jnp.stack([token_own, after(token_far, ready)]), 1)]
    qkv_last = last(ends(*after(qkv_beside, ready)))
    ready = (token_parts[2], qkv_last, gate_got)
    gate_mine = share(after(gate_got, ready))
    gate_beside = beside(gate_mine)
    up_got = over_shard(after(up_far, gate_mine), 2)
    gate_up_near = over_shard(after(gate_up_near, gate_mine), 1)
    w_qkv = [qkv_near, qkv_mine, *qkv_beside, *qkv_last]
    small_parts = [part[..., seqs * rows :, :] for part in token_parts]
    small_parts = [small_parts[0], small_parts[1], small_parts[2][0], small_parts[2][1]]
    small_all = jnp.concatenate(
        natural(
            [
                jnp.concatenate([part[:, at * wide : (at + 1) * wide] for at in range(4)])
                for part in small_parts
            ],
            shard,
        ),
        axis=1,
    )
    qkv_downs = small_all[: 3 * rank]
    gate_downs = small_all[3 * rank : 5 * rank]
    out_up = small_all[5 * rank : 6 * rank]
    feed_up = small_all[6 * rank : 7 * rank]
    attn_gain = small_all[7 * rank : 7 * rank + 1].astype(F32)
    feed_gain = small_all[7 * rank + 1 : 7 * rank + 2].astype(F32)
    head_gains = gains[:2].astype(F32)
    places = jnp.stack([shard, ctx % 4]).astype(jnp.int32)
    qkv_downs = after(qkv_downs, gate_mine)

    pre, qkv_low, squares = qkv_forward(
        token_parts,
        chunks,
        rows,
        w_attn,
        w_qkv,
        places,
        qkv_downs,
        own_model,
    )

    def from_all(sums):
        return [sums] + [over_shard(sums, flip) for flip in FLIPS[1:]]

    squares = from_all(squares[:16])
    place = after(jnp.arange(rows, dtype=jnp.int32), pre)
    positions = jnp.concatenate(
        [
            my_part * group_rows + (h * shards + (shard ^ flip)) * rows + place
            for h in range(chunks)
            for flip in FLIPS
        ]
    )
    freqs = jnp.exp(jnp.arange(0, HD, 2, dtype=F32) * (-math.log(rope_base) / HD))
    angles = positions.astype(F32)[:, None] * freqs[None, :]
    cosine, sine = jnp.cos(angles), jnp.sin(angles)
    cosine = jnp.concatenate([cosine, cosine], axis=1)
    sine = jnp.concatenate([-sine, sine], axis=1)
    up_mine = share(up_got)
    up_beside = beside(up_mine)
    gate_ends = ends(*gate_beside)
    gate_last = last(gate_ends)
    pre = after(pre, cosine, sine, gate_beside, up_mine)
    simple = per_sequence == 1 and chunk_rows == BLOCK
    if simple:
        queries, key_rows, mixed, logs = attention_forward(
            pre, squares, cosine, sine, head_gains, chunks
        )
    else:
        mixed, attention_grads = wide_attention(
            pre, squares, cosine, sine, head_gains, chunks, positions, groups
        )

    every = range(chunks)
    assert chunks == 2
    mid = rows

    def core(value):
        return over_shard(value, 1)

    def chip(value):
        return over_shard(value, 2)

    def half_sums(keep, got):
        own = keep[:mid].astype(F32) + got[:mid].astype(F32)
        return own, (keep[mid:].astype(F32) + got[mid:].astype(F32)).astype(BF)

    def project_out(x, h):
        return partial_forward(x, h, chunks, w_attn, 3, own_wide[3], out_up)

    def attention_rows(h, own, got, *ready):
        value = own + got.astype(F32)
        scale = rms_scale(value)
        resid = after(token_rows[h], ready).astype(F32) + value * scale * attn_gain
        return value, scale, resid, resid.astype(BF)

    def feed_rows(h, own, got):
        value = own + got.astype(F32)
        scale = rms_scale(value)
        grad = rms_back(value, scale, feed_gain, cot[h]).astype(BF)
        return (resid[h] + value * scale * feed_gain).astype(BF), grad

    def back_rows(h, own, got):
        grad = cot[h] + own + got.astype(F32)
        return grad, rms_back(attn_pre[h], attn_scale[h], attn_gain, grad).astype(BF)

    def up_gate(parts):
        return gate_up_forward(parts, w_gate_up, w_gate, w_up, places, gate_downs, own_hidden)

    def down(act):
        return partial_forward(act, 0, 1, w_down, None, own_down, feed_up)

    def back_down(h, parts):
        return feed_back(
            parts, w_down, own_down, hidden[h][0], hidden[h][1], hidden[h][3], feed_parts[h][2], feed_up, own_hidden
        )

    def back_up_gate(h, gate_grad, upper_grad):
        return gate_up_back(
            gate_grad, upper_grad, w_gate_up, w_gate, w_up, places, hidden_grads[h][2], gate_downs, resid_parts[h]
        )

    def back_out(h, parts):
        return out_back(parts, w_attn, 3, own_wide[3], out_up, mixed, out_parts[h][2], h)

    attn_pre, attn_scale, resid, resid_low = [None] * 2, [None] * 2, [None] * 2, [None] * 2
    resid_parts, hidden, feed_parts, output = [None] * 2, [None] * 2, [None] * 2, [None] * 2
    hidden_grads, resid_grads, grad_resid, out_grads = [None] * 2, [None] * 2, [None] * 2, [None] * 2
    out_parts = [project_out(after(mixed, gate_last), 0), None]
    out_parts[1], [got] = side_by_side(
        lambda x: project_out(x, 1), after(mixed, out_parts[0][2]), [(core, out_parts[0][1])]
    )
    own0, far0 = half_sums(out_parts[0][0], got)
    _, [got0, got] = side_by_side(None, None, [(chip, far0), (core, out_parts[1][1])])
    own1, far1 = half_sums(out_parts[1][0], got)
    attn_pre[0], attn_scale[0], resid[0], resid_low[0] = attention_rows(0, own0, got0, up_beside)
    up_last = last(ends(*up_beside))
    w_gate = [gate_up_near, gate_mine, *gate_beside, *gate_last]
    w_up = [gate_up_near, up_mine, *up_beside, *up_last]
    _, [resid_far] = side_by_side(None, None, [(chip, resid_low[0])])
    _, [resid_near] = side_by_side(None, None, [(core, jnp.stack([resid_low[0], resid_far]))])
    resid_parts[0] = [resid_low[0], resid_far, resid_near]
    hidden[0], [got1, cot_got] = side_by_side(
        up_gate, resid_parts[0], [(chip, far1), (send_rows, cut_rows(after(cotangent, resid_far)))]
    )
    cot = [x.astype(F32) for x in chunk_order(cot_got)]
    attn_pre[1], attn_scale[1], resid[1], resid_low[1] = attention_rows(1, own1, got1)
    feed_parts[0], [resid_far] = side_by_side(down, hidden[0][2], [(chip, resid_low[1])])
    _, [resid_near, got] = side_by_side(
        None, None, [(core, jnp.stack([resid_low[1], resid_far])), (core, feed_parts[0][1])]
    )
    resid_parts[1] = [resid_low[1], resid_far, resid_near]
    own0, far0 = half_sums(feed_parts[0][0], got)
    hidden[1], [got0] = side_by_side(up_gate, resid_parts[1], [(chip, far0)])
    output[0], grad0 = feed_rows(0, own0, got0)
    feed_parts[1], [grad_far] = side_by_side(down, hidden[1][2], [(chip, grad0)])
    _, [grad_near, got] = side_by_side(
        None, None, [(core, jnp.stack([grad0, grad_far])), (core, feed_parts[1][1])]
    )
    own1, far1 = half_sums(feed_parts[1][0], got)
    hidden_grads[0], [got1] = side_by_side(
        lambda x: back_down(0, x), [grad0, grad_far, grad_near], [(chip, far1)]
    )
    output[1], grad1 = feed_rows(1, own1, got1)
    resid_grads[0], [grad_far] = side_by_side(
        lambda x: back_up_gate(0, *x), hidden_grads[0][:2], [(chip, grad1)]
    )
    _, [grad_near, got] = side_by_side(
        None, None, [(core, jnp.stack([grad1, grad_far])), (core, resid_grads[0][1])]
    )
    own0, far0 = half_sums(resid_grads[0][0], got)
    hidden_grads[1], [got0] = side_by_side(
        lambda x: back_down(1, x), [grad1, grad_far, grad_near], [(chip, far0)]
    )
    grad_resid[0], grad0 = back_rows(0, own0, got0)
    resid_grads[1], [grad_far, output_got] = side_by_side(
        lambda x: back_up_gate(1, *x), hidden_grads[1][:2], [(chip, grad0), (return_rows, return_cuts(output))]
    )
    output = return_order(output_got)
    _, [grad_near, got] = side_by_side(
        None, None, [(core, jnp.stack([grad0, grad_far])), (core, resid_grads[1][1])]
    )
    own1, far1 = half_sums(resid_grads[1][0], got)
    out_grads[0], [got1] = side_by_side(
        lambda x: back_out(0, x), [grad0, grad_far, grad_near], [(chip, far1)]
    )
    grad_resid[1], grad1 = back_rows(1, own1, got1)
    _, [grad_far] = side_by_side(None, None, [(chip, grad1)])
    _, [grad_near] = side_by_side(None, None, [(core, jnp.stack([grad1, grad_far]))])
    out_grads[1] = back_out(1, [grad1, grad_far, grad_near])
    grad_mixed = jnp.concatenate([g[0] for g in out_grads])

    broad = jnp.concatenate(
        [
            sum(g[3] for g in hidden_grads),
            sum(g[5] for g in hidden_grads).reshape(2 * rank, -1),
        ]
    ).astype(BF)
    broad_all = gather_ctx(broad)
    feed_gate = scatter_columns(
        jnp.concatenate([sum(g[4] for g in hidden_grads), sum(g[2] for g in resid_grads)]), shard
    )

    if simple:
        query_turned, key_turned, grad_values, inner = attention_back(
            queries, key_rows, pre, grad_mixed, logs, cosine, sine, head_gains, chunks
        )
    else:
        query_turned, key_turned, grad_values, inner = attention_grads(grad_mixed)
    inners = from_all(inner)
    qkv_grads = [
        qkv_back(
            [query_turned, key_turned],
            grad_values,
            pre,
            squares,
            inners,
            token_parts,
            w_attn,
            w_qkv,
            places,
            qkv_low,
            qkv_downs,
            own_model[:3],
            chunks,
            h,
        )
        for h in every
    ]
    qkv_out = scatter_columns(
        jnp.concatenate([sum(g[2] for g in qkv_grads), sum(g[2] for g in out_grads)]), shard
    )
    input_rows = [
        grad_resid[h] + scatter_parts(qkv_grads[h][0], qkv_grads[h][1]) for h in every
    ]
    input_grad = return_order(return_rows(return_cuts([x.astype(BF) for x in input_rows]))).astype(F32)

    early_all = gather_ctx(
        jnp.concatenate([sum(g[1] for g in out_grads), feed_gate[rank:], feed_gate[:rank]]).astype(BF)
    )
    late_all = gather_ctx(
        jnp.concatenate([qkv_out, sum(g[3] for g in qkv_grads).reshape(3 * rank, -1)]).astype(BF)
    )
    sequence_with = jnp.sum(
        jnp.where(
            index_all[None, :] == jnp.arange(adapters, dtype=jnp.int32)[:, None],
            jnp.arange(batch, dtype=jnp.int32)[None, :],
            0,
        ),
        axis=1,
    )
    table = jnp.array(groups, jnp.int32)
    if per_sequence > 1:

        def summed(gathered):
            order = gathered_place(ctx, table)
            return jnp.sum(gathered.astype(F32)[order], axis=1)

        broad_all, early_all, late_all = summed(broad_all), summed(early_all), summed(late_all)
        where = sequence_with
    else:
        where = gathered_place(ctx, table[sequence_with, 0])

    def placed(sources, counts, plan):
        width = sources[0].shape[-1]
        outs = [shape_of((count, adapters, rank, width), F32) for count in counts]
        return call(
            functools.partial(place_body, rank, len(sources), plan),
            (1,),
            sources,
            [whole(x) for x in sources],
            [(o, whole(o)) for o in outs],
            scalars=[where],
        )

    grad_wide, grad_model = placed(
        [early_all, late_all],
        (6, 5),
        (((1, 0), (1, 1), (1, 2), (0, 0), (0, 1), (0, 2)), ((1, 4), (1, 5), (1, 6), (1, 3), (0, 3))),
    )
    grad_down, grad_hidden = placed([broad_all], (1, 2), (((0, 0),), ((0, 1), (0, 2))))
    return (output, input_grad, grad_wide, grad_down[0], grad_model, grad_hidden)


def solution(mesh):
    return jax.shard_map(
        on_device,
        mesh=mesh,
        in_specs=(
            P("shard", "ctx", None),
            P("shard", "ctx", None),
            P("shard", None),
            P(None, "shard", None),
            P(None, "shard", None),
            P("shard", None),
            P(None, "shard"),
            P(None, None, None, "shard"),
            P(None, None, "shard"),
            P(None, None, None, "shard"),
            P(None, None, None, "shard"),
        ),
        out_specs=(
            P("shard", "ctx", None),
            P("shard", "ctx", None),
            P(None, None, None, "shard"),
            P(None, None, "shard"),
            P(None, None, None, "shard"),
            P(None, None, None, "shard"),
        ),
        check_vma=False,
    )
```

```python
import functools
import math

import jax
import jax.numpy as jnp
from jax import lax
from jax.experimental import pallas as pl
from jax.experimental.pallas import tpu as pltpu
from jax.sharding import PartitionSpec as P

D = 2048
HEADS = 16
HD = 128
BLOCK = 256

epsilon = 1e-06
rope_base = 500000.0
far_below = -1e30
BF = jnp.bfloat16
F32 = jnp.float32
VMEM_BYTES = 16 * 2**20


def dot(left, right):
    return lax.dot_general(left, right, (((1,), (0,)), ((), ())), preferred_element_type=F32)


def dot_nt(left, right):
    return lax.dot_general(left, right, (((1,), (1,)), ((), ())), preferred_element_type=F32)


def dot_tn(left, right):
    return lax.dot_general(left, right, (((0,), (0,)), ((), ())), preferred_element_type=F32)


def over_shard(value, flip):
    size = lax.axis_size("shard")
    return lax.ppermute(value, "shard", [(i, i ^ flip) for i in range(size)])


class Windows:
    def __init__(self):
        self.carried = []

    def side_by_side(self, run, inputs, sends):
        values = [value for _, value in sends]
        inputs, values, self.carried = lax.optimization_barrier((inputs, values, self.carried))
        got = [send(value) for (send, _), value in zip(sends, values)]
        out = run(inputs) if run else None
        out, got, self.carried = lax.optimization_barrier((out, got, self.carried))
        return out, got


def over_ctx(value, flip):
    size = lax.axis_size("ctx")
    return lax.ppermute(value, "ctx", [(i, i ^ flip) for i in range(size)])


FLIPS = (0, 2, 1, 3)


def call(body, grid, args, in_specs, outs, scratch=(), scalars=(), flops=0, aliases={}):
    placed = []
    for arg, spec in zip(args, in_specs):
        if spec.memory_space == pltpu.VMEM:
            arg = pltpu.with_memory_space_constraint(arg, pltpu.VMEM)
        elif spec.memory_space == pltpu.HBM:
            arg = pltpu.with_memory_space_constraint(arg, pltpu.HBM)
        placed.append(arg)
    return pl.pallas_call(
        body,
        grid_spec=pltpu.PrefetchScalarGridSpec(
            num_scalar_prefetch=len(scalars),
            grid=grid,
            in_specs=in_specs,
            out_specs=[spec for _, spec in outs],
            scratch_shapes=scratch,
        ),
        out_shape=[shape for shape, _ in outs],
        input_output_aliases=aliases,
        compiler_params=pltpu.CompilerParams(vmem_limit_bytes=VMEM_BYTES),
        cost_estimate=pl.CostEstimate(flops=flops, bytes_accessed=0, transcendentals=0),
    )(*scalars, *placed)


def shape_of(shape, kind):
    return jax.ShapeDtypeStruct(shape, kind)


def whole(value):
    zeros = (0,) * value.ndim
    return pl.BlockSpec(value.shape, lambda *_: zeros)


def spec(block, index):
    return pl.BlockSpec(block, lambda i, *_: index(i))


def column_spec(value, tile):
    zeros = (0,) * (value.ndim - 1)
    return pl.BlockSpec(value.shape[:-1] + (tile,), lambda i, *_: (*zeros, i))


HBM = pl.BlockSpec(memory_space=pltpu.HBM)
VMEM = pl.BlockSpec(memory_space=pltpu.VMEM)


def tile_of(width):
    return min(512, width)


def run_copies(copies):
    for copy in copies:
        copy.start()
    for copy in copies:
        copy.wait()


def cut_body(first, kinds, places, weight, near, *refs):
    fars, sems = refs[:-1], refs[-1]
    step = pl.program_id(0)
    width = near.shape[2]
    slim = fars[0].shape[2]

    def columns(flip):
        return pl.ds(pl.multiple_of((places[0] ^ flip) * width, width), width)

    def copies(which):
        sources = [(slice(None), columns(1), near.at[0])]
        for far, turn in which:
            rows = pl.ds(pl.multiple_of((places[1] ^ turn) * slim, slim), slim)
            sources += [(rows, columns(2), far.at[0, 0]), (rows, columns(3), far.at[1, 0])]
        return [
            pltpu.make_async_copy(weight.at[first + step, r, c], to, sems.at[i])
            for i, (r, c, to) in enumerate(sources)
        ]

    if kinds is None:
        run_copies(copies([(fars[0], 0)]))
    else:
        for matrix in range(len({kind[0] for kind in kinds})):
            which = [(far, turn) for far, (at, turn) in zip(fars, kinds) if at == matrix]
            pl.when(step == matrix)(functools.partial(lambda which: run_copies(copies(which)), which))


def cut(weight, first, count, places, kinds=None):
    depth, full = weight.shape[1:]
    width, slim = full // 4, depth // 4
    if kinds:
        far = (shape_of((2, 1, slim, width), BF), pl.BlockSpec((2, 1, slim, width), lambda *_: (0, 0, 0, 0)))
    else:
        far = (shape_of((2, count, slim, width), BF), pl.BlockSpec((2, 1, slim, width), lambda m, _: (0, m, 0, 0)))
    return call(
        functools.partial(cut_body, first, kinds),
        (count,),
        [weight],
        [HBM],
        [(shape_of((count, depth, width), BF), pl.BlockSpec((1, depth, width), lambda m, _: (m, 0, 0)))]
        + [far] * (len(kinds) if kinds else 1),
        [pltpu.SemaphoreType.DMA((5,))],
        scalars=[places],
    )


COPIES = 10
PARTS = 6


def copies_of(weight, matrix, parts, near_at, at, places, held, sems):
    near, mine, from_x, from_z, *last_parts = parts
    width = held.shape[1]
    depth = held.shape[0] // 4
    slim = depth // 4
    shard, quarter = places[0], places[1]

    def to(flip, rows, begin=0):
        start = pl.multiple_of((shard ^ flip) * depth + begin, slim)
        return held.at[pl.ds(start, rows), :]

    pairs = []
    if weight is not None:
        own_columns = pl.ds(pl.multiple_of(shard * width, width), width)
        pairs.append((weight.at[matrix, :, own_columns], to(0, depth)))
    if near is not None:
        pairs.append((near.at[near_at], to(1, depth)))
    for place, flip in enumerate((2, 3)):
        for turn, piece in enumerate((mine, from_x, from_z)):
            if piece is not None:
                source = piece[place].at[at] if isinstance(piece, list) else piece.at[place, at]
                pairs.append((source, to(flip, slim, (quarter ^ turn) * slim)))
        if last_parts[place] is not None:
            pairs.append((last_parts[place].at[at], to(flip, slim, (quarter ^ 3) * slim)))
    return [pltpu.make_async_copy(source, target, sems.at[i]) for i, (source, target) in enumerate(pairs)]


DONE = (shape_of((8, 128), F32), pl.BlockSpec((8, 128), lambda *_: (0, 0)))


def load_plain_body(attn, out_held, done, sem):
    run_copies([pltpu.make_async_copy(attn.at[attn.shape[0] - 1], out_held, sem)])
    done[...] = jnp.zeros_like(done)


def load_plain(w_attn):
    return call(
        load_plain_body,
        (1,),
        [w_attn],
        [HBM],
        [(pltpu.VMEM(w_attn.shape[1:], BF), VMEM), DONE],
        [pltpu.SemaphoreType.DMA],
    )


def load_early_body(places, weight, near, *refs):
    gate_parts, (held, done, sems) = refs[: PARTS - 1], refs[PARTS - 1 :]
    copies = copies_of(weight, 0, [near, *gate_parts], 0, 0, places, held.at[0], sems.at[0])
    copies += copies_of(weight, 1, [near] + [None] * (PARTS - 1), 1, 0, places, held.at[1], sems.at[1])
    run_copies(copies)
    done[...] = jnp.zeros_like(done)


def load_early(weight, near, gate_parts, places):
    depth, full = weight.shape[1:]
    return call(
        load_early_body,
        (1,),
        [weight, near, *gate_parts],
        [HBM] * (1 + PARTS),
        [(pltpu.VMEM((2, 4 * depth, full // 4), BF), VMEM), DONE],
        [pltpu.SemaphoreType.DMA((2, COPIES))],
        [places],
    )


def load_late_body(places, *refs):
    mine, x0, x1, z0, z1, last0, last1, _, held, done, sems = refs
    parts = [None, mine, [x0, x1], [z0, z1], last0, last1]
    run_copies(copies_of(None, 1, parts, 0, 0, places, held.at[1], sems))
    done[...] = jnp.zeros_like(done)


def load_late(held, up_parts, places):
    return call(
        load_late_body,
        (1,),
        [*up_parts, held],
        [HBM] * len(up_parts) + [VMEM],
        [(pltpu.VMEM(held.shape, BF), VMEM), DONE],
        [pltpu.SemaphoreType.DMA((COPIES,))],
        [places],
        aliases={1 + len(up_parts): 0},
    )


def row_of(column):
    return jnp.transpose(jnp.broadcast_to(column, (column.shape[0], 128)))[:8]


def column_of(row):
    return jnp.transpose(jnp.broadcast_to(row[:1], (128, row.shape[1])))[:, :1]


def qkv_body(chunks, size, places, *refs):
    x_refs, refs = refs[:3], refs[3:]
    weight, weight_parts, refs = refs[0], refs[1 : 1 + PARTS], refs[1 + PARTS :]
    down, up, pre, low, sums, kept, held, rows, sems, keep_sems = refs
    step = pl.program_id(0)

    def copies(p):
        return copies_of(weight, p, weight_parts, p, p, places, held.at[p], sems.at[p])

    @pl.when(step == 0)
    def _():
        for p in range(held.shape[0]):
            for copy in copies(p):
                copy.start()
        for h in range(chunks):
            rows[4 * h * size : 4 * (h + 1) * size] = load_parts(x_refs, h * size, size)

    lowrank = dot_nt(rows[...], down[...]).astype(BF)
    for copy in copies(step):
        copy.wait()
    keep = [pltpu.make_async_copy(held.at[p], kept.at[p], keep_sems.at[p]) for p in range(held.shape[0])]
    for p, copy in enumerate(keep):
        pl.when(step == p)(copy.start)
    value = dot(rows[...], held[step]) + dot(lowrank, up[0])
    pre[0] = value.astype(BF)
    low[0] = lowrank
    sums[...] = row_of(jnp.sum(value * value, axis=1, keepdims=True))

    @pl.when(step == held.shape[0] - 1)
    def _():
        for copy in keep:
            copy.wait()


def qkv_forward(x_parts, chunks, size, weight, weight_parts, places, downs, ups):
    count, depth, width = weight_parts[0].shape
    full = x_parts[0].shape[1]
    total, rank = 4 * chunks * size, ups.shape[1]
    return call(
        functools.partial(qkv_body, chunks, size),
        (count,),
        [*x_parts, weight, *weight_parts, downs, ups],
        [whole(x) for x in x_parts]
        + [HBM] * (1 + PARTS)
        + [
            spec((rank, full), lambda p: (p, 0)),
            spec((1, rank, width), lambda p: (p, 0, 0)),
        ],
        [
            (shape_of((count, total, width), BF), spec((1, total, width), lambda p: (p, 0, 0))),
            (shape_of((count, total, rank), BF), spec((1, total, rank), lambda p: (p, 0, 0))),
            (shape_of((8 * count, total), F32), spec((8, total), lambda p: (p, 0))),
            (pltpu.HBM((count, full, width), BF), HBM),
        ],
        [
            pltpu.VMEM((count, full, width), BF),
            pltpu.VMEM((total, full), BF),
            pltpu.SemaphoreType.DMA((count, COPIES)),
            pltpu.SemaphoreType.DMA((count,)),
        ],
        [places],
        flops=2 * total * full * width * count,
    )


def aligned_sums(refs, which, chunks):
    total = refs[0].shape[1]
    block = total // (4 * chunks)
    out = 0.0
    for flip, ref in zip(FLIPS, refs):
        column = column_of(ref[8 * which : 8 * which + 8])
        if flip:
            order = [FLIPS.index(f ^ flip) for f in FLIPS]
            column = jnp.concatenate(
                [
                    column[(4 * h + i) * block : (4 * h + i + 1) * block]
                    for h in range(chunks)
                    for i in order
                ]
            )
        out = out + column
    return out


def attention_body(chunks, factor, *refs):
    (
        query_pre, key_pre, value, own, far, near, cross, cosine, sine, gains,
        query_out, key_out, mixed_out, logs_out, scale_rows,
    ) = refs
    total = query_pre.shape[1]
    size = total // chunks

    @pl.when(pl.program_id(0) == 0)
    def _():
        for p in range(2):
            sums = aligned_sums((own, far, near, cross), p, chunks)
            scale_rows[p] = jnp.broadcast_to(lax.rsqrt(sums / D + epsilon), (total, HD))

    def prepared(pre, p):
        value = pre[0].astype(F32) * scale_rows[p] * gains[p : p + 1]
        return (value * cosine[...] + pltpu.roll(value, HD // 2, 1) * sine[...]).astype(BF)

    query, key = prepared(query_pre, 0), prepared(key_pre, 1)
    query_out[...] = query
    key_out[...] = key
    logs = []
    for h in range(chunks):
        seen = (h + 1) * size
        scores = dot_nt(query[h * size : (h + 1) * size], key[:seen]) * factor
        top = jnp.max(scores, axis=1, keepdims=True)
        weights = jnp.exp(scores - top)
        sums = jnp.sum(weights, axis=1, keepdims=True)
        probs = (weights * (1.0 / sums)).astype(BF)
        mixed_out[h * size : (h + 1) * size] = dot(probs, value[0, :seen]).astype(BF)
        logs.append(top + jnp.log(sums))
    logs_out[...] = row_of(jnp.concatenate(logs))


def attention_forward(pre, sums, cosine, sine, gains, chunks):
    _, total, width = pre.shape
    heads = width // HD
    factor = 1.0 / math.sqrt(HD)

    def head(p):
        return spec((1, total, HD), lambda i: (p, 0, i))

    by_head = spec((total, HD), lambda i: (0, i))
    return call(
        functools.partial(attention_body, chunks, factor),
        (heads,),
        [pre, pre, pre, *sums, cosine, sine, gains],
        [head(0), head(1), head(2)]
        + [whole(s) for s in sums]
        + [whole(cosine), whole(sine), spec((gains.shape[0], HD), lambda i: (0, i))],
        [
            (shape_of((total, width), BF), by_head),
            (shape_of((total, width), BF), by_head),
            (shape_of((total, width), BF), by_head),
            (shape_of((8 * heads, total), F32), spec((8, total), lambda i: (i, 0))),
        ],
        [pltpu.VMEM((2, total, HD), F32)],
        flops=4 * total * total * width,
    )


def attention_back_body(chunks, factor, *refs):
    (
        query_in, key_in, query_pre, key_pre, value, grad_in, logs, cosine, sine, gains,
        query_out, key_out, value_out, inner_out, inner_rows,
    ) = refs
    total = query_in.shape[0]
    size = total // chunks
    head = pl.program_id(0)
    query, key, values, grad = query_in[...], key_in[...], value[0], grad_in[...]
    log_column = column_of(logs[...])
    grad_key = [0.0] * chunks
    grad_value = [0.0] * chunks
    grad_query = []
    for h in range(chunks):
        rows = slice(h * size, (h + 1) * size)
        grad_row = 0.0
        delta = 0.0
        kept = []
        for k in range(h + 1):
            keys = slice(k * size, (k + 1) * size)
            scores = dot_nt(query[rows], key[keys]) * factor
            probs = jnp.exp(scores - log_column[rows])
            grad_probs = dot_nt(grad[rows], values[keys])
            delta = delta + jnp.sum(probs * grad_probs, axis=1, keepdims=True)
            kept.append((probs, grad_probs))
        for k, (probs, grad_probs) in enumerate(kept):
            keys = slice(k * size, (k + 1) * size)
            grad_scores = (probs * (grad_probs - delta)).astype(BF)
            grad_row = grad_row + dot(grad_scores, key[keys])
            grad_key[k] = grad_key[k] + dot_tn(grad_scores, query[rows])
            grad_value[k] = grad_value[k] + dot_tn(probs.astype(BF), grad[rows])
        grad_query.append(grad_row)

    value_out[...] = jnp.concatenate(grad_value).astype(BF)
    for p, (pre, grads, out) in enumerate(
        ((query_pre, grad_query, query_out), (key_pre, grad_key, key_out))
    ):
        turned = jnp.concatenate(grads) * factor
        turned = turned * cosine[...] - pltpu.roll(turned, HD // 2, 1) * sine[...]
        turned = turned * gains[p : p + 1]
        out[...] = turned.astype(BF)
        inner = jnp.sum(turned * pre[0].astype(F32), axis=1, keepdims=True)
        inner = jnp.broadcast_to(inner, (total, 128))

        @pl.when(head == 0)
        def _():
            inner_rows[p] = inner

        @pl.when(head > 0)
        def _():
            inner_rows[p] += inner

    @pl.when(head == pl.num_programs(0) - 1)
    def _():
        for p in range(2):
            inner_out[8 * p : 8 * p + 8] = jnp.transpose(inner_rows[p])[:8]


def attention_back(queries, key_rows, pre, grad_mixed, logs, cosine, sine, gains, chunks):
    _, total, width = pre.shape
    heads = width // HD
    factor = 1.0 / math.sqrt(HD)

    def head(p):
        return spec((1, total, HD), lambda i: (p, 0, i))

    by_head = spec((total, HD), lambda i: (0, i))
    return call(
        functools.partial(attention_back_body, chunks, factor),
        (heads,),
        [queries, key_rows, pre, pre, pre, grad_mixed, logs, cosine, sine, gains],
        [by_head, by_head, head(0), head(1), head(2), by_head]
        + [spec((8, total), lambda i: (i, 0)), whole(cosine), whole(sine)]
        + [spec((gains.shape[0], HD), lambda i: (0, i))],
        [
            (shape_of((total, width), BF), by_head),
            (shape_of((total, width), BF), by_head),
            (shape_of((total, width), BF), by_head),
            (shape_of((16, total), F32), pl.BlockSpec((16, total), lambda *_: (0, 0))),
        ],
        [pltpu.VMEM((2, total, 128), F32)],
        flops=10 * total * total * width,
    )


def split_out(value, keep, send, columns=slice(None)):
    half = value.shape[0] // 2
    keep[:, columns] = value[:half].astype(BF)
    send[:, columns] = value[half:].astype(BF)


def qkv_grads_body(chunks, *refs):
    query_grad, key_grad, value_grad, query_pre, key_pre = refs[:5]
    squares, inners, x_refs = refs[5:9], refs[9:13], refs[13:16]
    low, ups, grads, lows, down_out, up_out = refs[16:]
    rank = ups.shape[1]
    total = query_grad.shape[0]
    for p, (grad, pre) in enumerate(((query_grad, query_pre), (key_grad, key_pre))):
        scale = lax.rsqrt(aligned_sums(squares, p, chunks) / D + epsilon)
        inner = aligned_sums(inners, p, chunks) * (scale * scale * scale / D)
        grads[p] = (grad[...].astype(F32) * scale - pre[0].astype(F32) * inner).astype(BF)
    grads[2] = value_grad[...]
    for p in range(3):
        lows[:, p * rank : (p + 1) * rank] = dot_nt(grads[p], ups[p]).astype(BF)
        up_out[p] = dot_tn(low[p], grads[p])
    size = total // chunks
    down = 0.0
    for h in range(chunks):
        x = load_parts(x_refs, h * size // 4, size // 4)
        down += dot_tn(lows[h * size : (h + 1) * size], x)
    down_out[...] = down


def qkv_grads(turned, grad_values, pre, squares, inners, x_parts, low, ups, chunks):
    count, total, width = pre.shape
    rank = ups.shape[1]
    full = x_parts[0].shape[1]

    def pre_rows(p):
        return pl.BlockSpec((1, total, width), lambda *_: (p, 0, 0))

    outs = [
        shape_of((count, total, width), BF),
        shape_of((total, count * rank), BF),
        shape_of((count * rank, full), F32),
        shape_of((count, rank, width), F32),
    ]
    return call(
        functools.partial(qkv_grads_body, chunks),
        (1,),
        [*turned, grad_values, pre, pre, *squares, *inners, *x_parts, low, ups],
        [whole(turned[0]), whole(turned[1]), whole(grad_values), pre_rows(0), pre_rows(1)]
        + [whole(v) for v in (*squares, *inners, *x_parts, low)]
        + [pl.BlockSpec((count, rank, width), lambda *_: (0, 0, 0))],
        [(o, whole(o)) for o in outs],
        flops=2 * total * width * 512,
    )


def qkv_back_body(_, grads, lows, weight, downs, keep, send):
    value = dot(lows[...], downs[...])
    for p in range(3):
        value += dot_nt(grads[p], weight[p])
    split_out(value, keep, send)


def qkv_back(grads, lows, weight, downs, chunks, chunk):
    count, full, width = weight.shape
    total = grads.shape[1]
    size = total // chunks
    tile = tile_of(full)
    half = size // 2
    return call(
        qkv_back_body,
        (full // tile,),
        [grads, lows, weight, downs],
        [
            pl.BlockSpec((count, size, width), lambda i, c: (0, c[0], 0)),
            pl.BlockSpec((size, lows.shape[1]), lambda i, c: (c[0], 0)),
            spec((count, tile, width), lambda i: (0, i, 0)),
            spec((downs.shape[0], tile), lambda i: (0, i)),
        ],
        [
            (shape_of((half, full), BF), spec((half, tile), lambda i: (0, i))),
            (shape_of((half, full), BF), spec((half, tile), lambda i: (0, i))),
        ],
        scalars=[chunk],
        flops=2 * size * full * width * count,
    )


def partial_body(streamed, beside, x, weight, down, up, *refs):
    keep, send, low, *scratch = refs[beside:]
    step = pl.program_id(0)
    tile = keep.shape[1]

    def columns(i):
        return pl.ds(pl.multiple_of(i * tile, tile), tile)

    def copy(i):
        held, sems = scratch
        return pltpu.make_async_copy(weight.at[:, columns(i)], held.at[:, columns(i)], sems.at[i])

    @pl.when(step == 0)
    def _():
        if streamed:
            for i in range(weight.shape[1] // tile):
                copy(i).start()
        low[...] = dot_nt(x[...], down[...]).astype(BF)

    if streamed:
        copy(step).wait()
        held = scratch[0]
    else:
        held = weight
    split_out(dot(x[...], held[:, columns(step)]) + dot(low[...], up[...]), keep, send)


def partial_forward(x, chunk, chunks, weight, down, up, streamed, beside=()):
    total, depth = x.shape
    size = total // chunks
    full = weight.shape[-1]
    tile = tile_of(full)
    half = size // 2
    rank = down.shape[0]
    scratch = [pltpu.VMEM(weight.shape, BF), pltpu.SemaphoreType.DMA((full // tile,))]
    return call(
        functools.partial(partial_body, streamed, len(beside)),
        (full // tile,),
        [x, weight, down, up, *beside],
        [
            pl.BlockSpec((size, depth), lambda *_: (chunk, 0)),
            HBM if streamed else VMEM,
            whole(down),
            spec((rank, tile), lambda i: (0, i)),
            *[VMEM] * len(beside),
        ],
        [
            (shape_of((half, full), BF), spec((half, tile), lambda i: (0, i))),
            (shape_of((half, full), BF), spec((half, tile), lambda i: (0, i))),
            (shape_of((size, rank), BF), pl.BlockSpec((size, rank), lambda *_: (0, 0))),
        ],
        scratch if streamed else (),
        flops=2 * size * depth * full,
    )


def gate_up_body(*refs):
    x_refs, (weight, downs, ups, gate, upper, act, low, rows) = refs[:3], refs[3:]
    rank = ups.shape[1]
    tile = gate.shape[1]
    step = pl.program_id(0)

    @pl.when(step == 0)
    def _():
        rows[...] = load_parts(x_refs)
        low[...] = dot_nt(rows[...], downs[...]).astype(BF)

    columns = pl.ds(pl.multiple_of(step * tile, tile), tile)
    gate_pre = dot(rows[...], weight[0, :, columns]) + dot(low[:, :rank], ups[0])
    upper_pre = dot(rows[...], weight[1, :, columns]) + dot(low[:, rank:], ups[1])
    gate[...] = gate_pre.astype(BF)
    upper[...] = upper_pre.astype(BF)
    act[...] = (gate_pre * jax.nn.sigmoid(gate_pre) * upper_pre).astype(BF)


def gate_up_forward(x_parts, weight, downs, ups):
    _, full, width = weight.shape
    size = 4 * x_parts[0].shape[0]
    rank = ups.shape[1]
    tile = tile_of(width)
    out = (shape_of((size, width), BF), spec((size, tile), lambda i: (0, i)))
    return call(
        gate_up_body,
        (width // tile,),
        [*x_parts, weight, downs, ups],
        [whole(x) for x in x_parts] + [VMEM, whole(downs), spec((2, rank, tile), lambda i: (0, 0, i))],
        [
            out,
            out,
            out,
            (shape_of((size, 2 * rank), BF), pl.BlockSpec((size, 2 * rank), lambda *_: (0, 0))),
        ],
        [pltpu.VMEM((size, full), BF)],
        flops=4 * size * full * width,
    )


def feed_back_body(*refs):
    g_refs = refs[:3]
    weight, down, gate, upper, gate_low, feed_low, feed_up, ups, _ = refs[3:12]
    gate_grad, upper_grad, low_out, down_a, feed_b, hidden_b, rows, low, lows = refs[12:]
    rank = down.shape[0]
    step = pl.program_id(0)
    @pl.when(step == 0)
    def _():
        rows[...] = load_parts(g_refs)
        low[...] = dot_nt(rows[...], feed_up[...]).astype(BF)
        feed_b[...] = dot_tn(feed_low[...], rows[...])
        lows[...] = jnp.zeros_like(lows)

    grad_act = dot_nt(rows[...], weight[...]) + dot(low[...], down[...])
    gate_pre, upper_pre = gate[...].astype(F32), upper[...].astype(F32)
    sig = jax.nn.sigmoid(gate_pre)
    silu = gate_pre * sig
    down_a[...] = dot_tn(low[...], (silu * upper_pre).astype(BF))
    grad_upper = (grad_act * silu).astype(BF)
    grad_gate = (grad_act * upper_pre * (sig + silu * (1.0 - sig))).astype(BF)
    gate_grad[...] = grad_gate
    upper_grad[...] = grad_upper
    hidden_b[0] = dot_tn(gate_low[:, :rank], grad_gate)
    hidden_b[1] = dot_tn(gate_low[:, rank:], grad_upper)
    lows[:, :rank] += dot_nt(grad_gate, ups[0])
    lows[:, rank:] += dot_nt(grad_upper, ups[1])

    @pl.when(step == pl.num_programs(0) - 1)
    def _():
        low_out[...] = lows[...].astype(BF)


def feed_back(g_parts, weight, down, gate, upper, gate_low, feed_low, feed_up, ups, beside):
    width, depth = weight.shape
    size = 4 * g_parts[0].shape[0]
    rank = down.shape[0]
    tile = tile_of(width)
    weight = pltpu.with_memory_space_constraint(weight, pltpu.HBM)
    by_tile = spec((size, tile), lambda i: (0, i))
    return call(
        feed_back_body,
        (width // tile,),
        [*g_parts, weight, down, gate, upper, gate_low, feed_low, feed_up, ups, beside],
        [whole(g) for g in g_parts]
        + [
            spec((tile, depth), lambda i: (i, 0)),
            spec((rank, tile), lambda i: (0, i)),
            by_tile,
            by_tile,
            whole(gate_low),
            whole(feed_low),
            whole(feed_up),
            spec((2, rank, tile), lambda i: (0, 0, i)),
            VMEM,
        ],
        [
            (shape_of((size, width), BF), by_tile),
            (shape_of((size, width), BF), by_tile),
            (shape_of((size, 2 * rank), BF), pl.BlockSpec((size, 2 * rank), lambda *_: (0, 0))),
            (shape_of((rank, width), F32), spec((rank, tile), lambda i: (0, i))),
            (shape_of((rank, depth), F32), pl.BlockSpec((rank, depth), lambda *_: (0, 0))),
            (shape_of((2, rank, width), F32), spec((2, rank, tile), lambda i: (0, 0, i))),
        ],
        [
            pltpu.VMEM((size, depth), BF),
            pltpu.VMEM((size, rank), BF),
            pltpu.VMEM((size, 2 * rank), F32),
        ],
        flops=2 * size * depth * width,
    )


def gate_up_back_body(gate_grad, upper_grad, weight, low, downs, own, far, near, keep, send, down_out):
    tile = keep.shape[1]
    held_rows = pl.ds(pl.multiple_of(pl.program_id(0) * tile, tile), tile)
    value = dot_nt(gate_grad[...], weight[0, held_rows]) + dot_nt(upper_grad[...], weight[1, held_rows])
    split_out(value + dot(low[...], downs[...]), keep, send)
    down_out[...] = dot_tn(low[...], load_parts((own, far, near)))


def gate_up_back(gate_grad, upper_grad, weight, low, downs, x_parts):
    _, full, width = weight.shape
    size = gate_grad.shape[0]
    half = size // 2
    ranks = downs.shape[0]
    tile = tile_of(full)
    return call(
        gate_up_back_body,
        (full // tile,),
        [gate_grad, upper_grad, weight, low, downs, *x_parts],
        [whole(gate_grad), whole(upper_grad), VMEM, whole(low), spec((ranks, tile), lambda i: (0, i))]
        + [column_spec(x, tile) for x in x_parts],
        [
            (shape_of((half, full), BF), spec((half, tile), lambda i: (0, i))),
            (shape_of((half, full), BF), spec((half, tile), lambda i: (0, i))),
            (shape_of((ranks, full), F32), spec((ranks, tile), lambda i: (0, i))),
        ],
        flops=4 * size * full * width,
    )


def out_back_body(*refs):
    g_refs = refs[:3]
    weight, down, up, mixed, low, grad_mixed, down_out, up_out, rows, grad_low = refs[3:]

    @pl.when(pl.program_id(0) == 0)
    def _():
        rows[...] = load_parts(g_refs)
        grad_low[...] = dot_nt(rows[...], up[...]).astype(BF)
        up_out[...] = dot_tn(low[...], rows[...])

    tile = grad_mixed.shape[1]
    held_rows = pl.ds(pl.multiple_of(pl.program_id(0) * tile, tile), tile)
    grad_mixed[...] = (dot_nt(rows[...], weight[held_rows]) + dot(grad_low[...], down[...])).astype(BF)
    down_out[...] = dot_tn(grad_low[...], mixed[...])


def out_back(g_parts, weight, down, up, mixed, low, chunk):
    width, depth = weight.shape
    size = 4 * g_parts[0].shape[0]
    rank = down.shape[0]
    tile = min(256, width)
    return call(
        out_back_body,
        (width // tile,),
        [*g_parts, weight, down, up, mixed, low],
        [whole(g) for g in g_parts]
        + [
            VMEM,
            spec((rank, tile), lambda i: (0, i)),
            whole(up),
            spec((size, tile), lambda i: (chunk, i)),
            whole(low),
        ],
        [
            (shape_of((size, width), BF), spec((size, tile), lambda i: (0, i))),
            (shape_of((rank, width), F32), spec((rank, tile), lambda i: (0, i))),
            (shape_of((rank, depth), F32), pl.BlockSpec((rank, depth), lambda *_: (0, 0))),
        ],
        [pltpu.VMEM((size, depth), BF), pltpu.VMEM((size, rank), BF)],
        flops=2 * size * depth * width,
    )


def load_parts(refs, first=0, count=None, columns=slice(None)):
    own, far, near = refs
    rows = slice(first, own.shape[0] if count is None else first + count)
    return jnp.concatenate(
        [own[rows, columns], far[rows, columns], near[0, rows, columns], near[1, rows, columns]]
    )


def ctx_flips():
    size = lax.axis_size("ctx")
    return [flip for flip in (2, 4, 8, 16, 1) if flip < size]


def ctx_step(at):
    return lambda value: over_ctx(value, ctx_flips()[at])


def gathered_place(ctx, other):
    place = 0
    for at, flip in enumerate(ctx_flips()):
        place = place + (((ctx ^ other) // flip) % 2) * 2**at
    return place


def column_cuts(partial, starts):
    width = partial.shape[-1] // 4
    zero = jnp.uint32(0)
    blocks = [lax.dynamic_slice(partial, (zero, start), (partial.shape[0], width)) for start in starts]
    return blocks[0], blocks[1], jnp.stack(blocks[2:]).astype(BF)


def natural(parts, shard):
    out = []
    for index in range(4):
        value = parts[0]
        for flip, part in zip(FLIPS[1:], parts[1:]):
            value = jnp.where((shard ^ flip) == index, part, value)
        out.append(value)
    return out


def rms_scale(value):
    return lax.rsqrt(jnp.mean(value * value, axis=-1, keepdims=True) + epsilon)


def rms_back(value, scale, gain, grad):
    weighted = grad * gain
    return scale * weighted - value * (
        scale * scale * scale * jnp.mean(value * weighted, axis=-1, keepdims=True)
    )


def rotate(value, cosine, sine):
    half = value.shape[-1] // 2
    turned = jnp.concatenate([value[..., half:], value[..., :half]], axis=-1)
    return value * cosine[:, None, :] + turned * sine[:, None, :]


def realign(value, flip, chunks):
    shape = value.shape
    value = value.reshape(shape[0], chunks, 2, 2, -1)
    if flip & 1:
        value = value[:, :, ::-1]
    if flip & 2:
        value = value[:, :, :, ::-1]
    return value.reshape(shape)


def group_of(sequence, part, per_sequence, ctx_size):
    if per_sequence > 1:
        return sequence * per_sequence + part
    depth = sequence % (ctx_size // 2)
    return 2 * depth + (depth + sequence // (ctx_size // 2)) % 2


def sequence_of(ctx, per_sequence, ctx_size):
    if per_sequence > 1:
        return ctx // per_sequence, ctx % per_sequence
    depth = ctx // 2
    return depth + ctx_size // 2 * ((ctx + depth) % 2), 0 * ctx


def wide_attention(pre, sums, cosine, sine, gains, chunks, positions, groups):
    _, total, width = pre.shape
    heads = width // HD
    pre = pre.astype(F32)
    squares = sum(realign(s[::8], flip, chunks) for flip, s in zip(FLIPS, sums))
    scales = lax.rsqrt(squares[:2] / D + epsilon)[:, :, None]

    def as_heads(value):
        return value.reshape(total, heads, HD)

    queries, key_rows = [
        rotate(as_heads(pre[p] * scales[p] * gains[p]), cosine, sine).astype(BF) for p in range(2)
    ]

    def over_sequence(value):
        return lax.all_gather(value, "ctx", axis=0, tiled=True, axis_index_groups=groups)

    key_all, value_all = over_sequence(key_rows), over_sequence(as_heads(pre[2].astype(BF)))
    visible = over_sequence(positions // BLOCK)[None, :] <= (positions // BLOCK)[:, None]
    factor = 1.0 / math.sqrt(HD)
    scores = jnp.einsum("qhd,khd->hqk", queries, key_all, preferred_element_type=F32) * factor
    scores = jnp.where(visible, scores, far_below)
    weights = jnp.exp(scores - jnp.max(scores, axis=-1, keepdims=True))
    probs = weights / jnp.sum(weights, axis=-1, keepdims=True)
    mixed = jnp.einsum("hqk,khd->qhd", probs.astype(BF), value_all, preferred_element_type=F32)
    mixed = mixed.astype(BF).reshape(total, width)

    def back(grad_mixed):
        grad = as_heads(grad_mixed)
        grad_probs = jnp.einsum("qhd,khd->hqk", grad, value_all, preferred_element_type=F32)
        delta = jnp.sum(probs * grad_probs, axis=-1, keepdims=True)
        grad_scores = (probs * (grad_probs - delta)).astype(BF)
        grad_queries = jnp.einsum("hqk,khd->qhd", grad_scores, key_all, preferred_element_type=F32)
        grad_keys = jnp.einsum("hqk,qhd->khd", grad_scores, queries, preferred_element_type=F32)
        grad_values = jnp.einsum("hqk,qhd->khd", probs.astype(BF), grad, preferred_element_type=F32)
        grad_keys, grad_values = [
            lax.psum_scatter(
                g.astype(BF), "ctx", scatter_dimension=0, tiled=True, axis_index_groups=groups
            ).astype(F32)
            for g in (grad_keys * factor, grad_values)
        ]
        turned = [
            rotate(g, cosine, -sine).reshape(total, width) * gains[p]
            for p, g in enumerate((grad_queries * factor, grad_keys))
        ]
        inner = jnp.stack([jnp.sum(turned[p] * pre[p], axis=-1) for p in range(2)])
        inner = jnp.repeat(inner, 8, axis=0)
        values = grad_values.reshape(total, width).astype(BF)
        return turned[0].astype(BF), turned[1].astype(BF), values, inner

    return mixed, back


def choose_body(place, wide, down, model, hidden, gains, wide_out, down_out, model_out, hidden_out, small, sems):
    at = place[0]
    sources = [(wide.at[:, at], wide_out), (down.at[at], down_out)]
    sources += [(model.at[:, at], model_out), (hidden.at[:, at], hidden_out)]
    run_copies([pltpu.make_async_copy(source, to, sems.at[i]) for i, (source, to) in enumerate(sources)])
    rank, width = wide_out.shape[1:]
    shared = [wide_out[p] for p in (0, 1, 2, 4, 5)] + [model_out[p] for p in (3, 4)]
    last = jnp.concatenate([gains[2:], jnp.zeros((rank - 2, width), BF)])
    for at, value in enumerate([*shared, last]):
        column = at // 2 * width
        small[at % 2 * rank : (at % 2 + 1) * rank, column : column + width] = value


def choose(place, a_wide, a_down, b_model, b_hidden, gains):
    rank, width = a_wide.shape[2:]
    shapes = [a_wide.shape[:1] + a_wide.shape[2:], a_down.shape[1:]]
    shapes += [b_model.shape[:1] + b_model.shape[2:], b_hidden.shape[:1] + b_hidden.shape[2:]]
    shapes.append((2 * rank, 4 * width))
    outs = [shape_of(s, BF) for s in shapes]
    return call(
        choose_body,
        (1,),
        [a_wide, a_down, b_model, b_hidden, gains],
        [HBM] * 4 + [whole(gains)],
        [(o, whole(o)) for o in outs],
        [pltpu.SemaphoreType.DMA((4,))],
        scalars=[place],
    )


def place_body(rank, count, unused, plan, at, *refs):
    sources, outs = refs[:count], refs[count + unused :]
    for out, maps in zip(outs, plan):
        for n in range(out.shape[1]):
            for p, pieces in enumerate(maps):
                begin = 0
                for source, place in pieces:
                    value = sources[source][at[n], place * rank : (place + 1) * rank].astype(F32)
                    out[p, n, :, begin : begin + value.shape[-1]] = value
                    begin += value.shape[-1]


def on_device(
    tokens,
    cotangent,
    adapter_index,
    w_attn,
    w_gate_up,
    w_down,
    gains,
    a_wide,
    a_down,
    b_model,
    b_hidden,
):
    seqs, rows = tokens.shape[0], tokens.shape[1]
    shards, ctxs = lax.axis_size("shard"), lax.axis_size("ctx")
    shard, ctx = lax.axis_index("shard"), lax.axis_index("ctx")
    batch = seqs * shards
    per_sequence = ctxs // batch
    group_rows = batch * rows
    chunks = seqs
    chunk_rows = shards * rows
    wide = HEADS // shards * HD
    adapters, rank = a_down.shape[:2]

    groups = [[group_of(q, k, per_sequence, ctxs) for k in range(per_sequence)] for q in range(batch)]
    my_sequence, my_part = sequence_of(ctx, per_sequence, ctxs)
    my_slot = my_sequence % seqs
    my_spot = (ctx % batch) // shards

    pairs = []
    for p in range(seqs):
        pairs.append([])
        for c in range(ctxs):
            for s in range(shards):
                k, local = c // batch, c % batch
                spot, owner = local // shards, local % shards
                to = groups[seqs * s + (p + spot) % seqs][k]
                pairs[p].append((c * shards + s, to * shards + owner))

    windows = Windows()
    side_by_side = windows.side_by_side

    def is_place(index):
        return [index % seqs == at for at in range(1, seqs)]

    flags = {
        "cut": [((p + my_spot) % seqs).astype(jnp.uint32) for p in range(seqs)],
        "chunk": [is_place(my_slot - h) for h in range(seqs)],
        "return": [is_place(my_slot - p) for p in range(seqs)],
        "order": [is_place(j - my_spot) for j in range(seqs)],
        "columns": [((shard ^ flip) * wide).astype(jnp.uint32) for flip in FLIPS],
        "places": jnp.stack([shard, ctx % 4]).astype(jnp.int32),
        "turn": [((my_slot - p) % seqs)[None].astype(jnp.int32) for p in range(seqs)],
    }

    def pick(parts, is_it):
        value = parts[0]
        for part, flag in zip(parts[1:], is_it):
            value = jnp.where(flag, part, value)
        return value

    def cut_rows(*values):
        return [
            jnp.concatenate(
                [
                    lax.dynamic_index_in_dim(value, flags["cut"][p], 0, keepdims=False)
                    for value in values
                ]
            )
            for p in range(seqs)
        ]

    def send_row(p):
        return lambda cut: lax.ppermute(cut, ("ctx", "shard"), pairs[p])

    def chunk_order(got):
        return [pick(got, flags["chunk"][h]) for h in range(seqs)]

    def return_cuts(parts):
        return [pick(parts, flags["return"][p]) for p in range(seqs)]

    def return_row(p):
        return lambda cut: lax.ppermute(cut, ("ctx", "shard"), [(b, a) for a, b in pairs[p]])

    def return_order(got):
        return jnp.stack([pick(got, flags["order"][j]) for j in range(seqs)])

    def core(value):
        return over_shard(value, 1)

    def chip(value):
        return over_shard(value, 2)

    def by_x(value):
        return over_ctx(value, 1)

    def by_z(value):
        return over_ctx(value, 2)

    def to_all(value):
        return [(functools.partial(over_shard, flip=flip), value) for flip in FLIPS[1:]]

    index_own = adapter_index[:, 0]
    (qkv_near, qkv_far, flags), index_got = side_by_side(
        lambda x: (*cut(x[0], 0, 3, x[1]["places"]), x[1]), [w_attn, flags], to_all(index_own)
    )
    places = flags["places"]
    index_all = jnp.concatenate(natural([index_own, *index_got], shard))
    sequence_with = jnp.sum(
        jnp.where(
            index_all[None, :] == jnp.arange(adapters, dtype=jnp.int32)[:, None],
            jnp.arange(batch, dtype=jnp.int32)[None, :],
            0,
        ),
        axis=1,
    )
    table = jnp.array(groups, jnp.int32)
    if per_sequence > 1:
        where = sequence_with
    else:
        group_with = jnp.sum(
            jnp.where(
                sequence_with[:, None] == jnp.arange(batch, dtype=jnp.int32)[None, :], table[:, 0][None, :], 0
            ),
            axis=1,
        )
        where = gathered_place(ctx, group_with)
    row_cuts = cut_rows(tokens)

    def rope_tables(place):
        shape = (chunks, shards, rows, HD)
        spot, turn, row, lane = [lax.broadcasted_iota(jnp.int32, shape, axis) for axis in range(4)]
        owner = place ^ (turn // 2 + turn % 2 * 2)
        position = my_part * group_rows + (spot * shards + owner) * rows + row
        freqs = jnp.exp((lane % (HD // 2)).astype(F32) * (-2.0 * math.log(rope_base) / HD))
        angles = position.astype(F32) * freqs
        sine = jnp.sin(angles) * jnp.where(lane < HD // 2, -1.0, 1.0)
        return position[..., 0].reshape(-1), jnp.cos(angles).reshape(-1, HD), sine.reshape(-1, HD)

    def prepare(x):
        chosen = choose(x[0], a_wide, a_down, b_model, b_hidden, gains)
        return chosen, cut(x[1], 0, 2, x[2], ((0, 0), (1, 0), (1, 3))), x[3], rope_tables(x[2][0])

    (chosen, gate_up_cuts, where, (positions, cosine, sine)), [qkv_got, row_got0, row_got1, qkv_near] = side_by_side(
        prepare,
        [index_all[my_sequence][None], w_gate_up, places, where],
        [(chip, qkv_far), (send_row(0), row_cuts[0]), (send_row(1), row_cuts[1]), (core, qkv_near)],
    )
    own_wide, own_down, own_model, own_hidden, small = chosen
    gate_up_near, gate_far, up_far, up_far_last = gate_up_cuts

    token_rows = chunk_order([row_got0, row_got1])
    token_own, [got] = side_by_side(
        lambda x: jnp.concatenate(x), [*token_rows, small], [(core, qkv_got[1])]
    )
    qkv_mine = jnp.stack([qkv_got[0], got])
    held = {}

    def load_out(weight):
        held["out"], done = load_plain(weight)
        return done

    row_cuts = cut_rows(cotangent)
    done, [qkv_x, qkv_z, gate_got, *row_got] = side_by_side(
        load_out,
        w_attn,
        [
            (by_x, qkv_mine),
            (by_z, qkv_mine),
            (chip, gate_far),
            (send_row(0), row_cuts[0]),
            (send_row(1), row_cuts[1]),
        ],
    )
    cot_rows = chunk_order(row_got)
    _, [token_far, last0, last1, got] = side_by_side(
        None, None, [(chip, token_own), (by_x, qkv_z[0]), (by_z, qkv_x[1]), (core, gate_got[1])]
    )
    windows.carried.append(done)
    gate_mine = jnp.stack([gate_got[0], got])
    w_qkv = [qkv_near, qkv_mine, qkv_x, qkv_z, last0, last1]
    _, [token_near] = side_by_side(None, None, [(core, jnp.stack([token_own, token_far]))])
    token_parts = [token_own, token_far, token_near]
    small_parts = [part[..., seqs * rows :, :] for part in token_parts]
    small_parts = [small_parts[0], small_parts[1], small_parts[2][0], small_parts[2][1]]
    small_all = jnp.concatenate(
        natural(
            [
                jnp.concatenate([part[:, at * wide : (at + 1) * wide] for at in range(4)])
                for part in small_parts
            ],
            shard,
        ),
        axis=1,
    )
    qkv_downs = small_all[: 3 * rank]
    gate_downs = small_all[3 * rank : 5 * rank]
    out_up = small_all[5 * rank : 6 * rank]
    feed_up = small_all[6 * rank : 7 * rank]
    attn_gain = small_all[7 * rank : 7 * rank + 1].astype(F32)
    feed_gain = small_all[7 * rank + 1 : 7 * rank + 2].astype(F32)
    head_gains = gains[:2].astype(F32)

    (pre, qkv_low, squares, qkv_held), [gate_x, gate_z, up_got, gate_up_near] = side_by_side(
        lambda x: qkv_forward(x, chunks, rows, w_attn, w_qkv, places, qkv_downs, own_model),
        token_parts,
        [(by_x, gate_mine), (by_z, gate_mine), (chip, up_far), (core, gate_up_near)],
    )

    def from_all(sums, others):
        _, got = side_by_side(None, None, to_all(sums) + others)
        return [sums, *got[:3]], got[3:]

    squares, [got] = from_all(squares[:16], [(core, up_got[1])])
    up_mine = jnp.stack([up_got[0], got])
    simple = per_sequence == 1 and chunk_rows == BLOCK
    attention_sends = [(by_x, gate_z[0]), (by_z, gate_x[1]), (chip, up_far_last[0])]
    if simple:
        (queries, key_rows, mixed, logs), got = side_by_side(
            lambda x: attention_forward(x[0], x[1], x[2], x[3], head_gains, chunks),
            [pre, squares, cosine, sine],
            attention_sends,
        )
    else:
        mixed, attention_grads = wide_attention(
            pre, squares, cosine, sine, head_gains, chunks, positions, groups
        )
        got = [send(value) for send, value in attention_sends]
    gate_last, up_last0 = got[:2], got[2]

    every = range(chunks)
    assert chunks == 2
    mid = rows

    def half_sums(keep, got):
        own = keep[:mid].astype(F32) + got[:mid].astype(F32)
        return own, (keep[mid:].astype(F32) + got[mid:].astype(F32)).astype(BF)

    def project_out(x, h):
        return partial_forward(x, h, chunks, held["out"], own_wide[3], out_up, False)

    def attention_rows(h, own, got):
        value = own + got.astype(F32)
        scale = rms_scale(value)
        resid = token_rows[h].astype(F32) + value * scale * attn_gain
        return value, scale, resid, resid.astype(BF)

    def feed_rows(h, own, got):
        value = own + got.astype(F32)
        scale = rms_scale(value)
        grad = rms_back(value, scale, feed_gain, cot[h]).astype(BF)
        return (resid[h] + value * scale * feed_gain).astype(BF), grad

    def back_rows(h, own, got):
        grad = cot[h] + own + got.astype(F32)
        return grad, rms_back(attn_pre[h], attn_scale[h], attn_gain, grad).astype(BF)

    def up_gate(parts):
        return gate_up_forward(parts, gate_up_held, gate_downs, own_hidden)

    def down(act):
        return partial_forward(act, 0, 1, w_down, own_down, feed_up, True, [gate_up_held])

    def back_down(h, parts):
        return feed_back(
            parts, w_down, own_down, hidden[h][0], hidden[h][1], hidden[h][3], feed_parts[h][2], feed_up, own_hidden, gate_up_held
        )

    def back_up_gate(h, gate_grad, upper_grad):
        return gate_up_back(
            gate_grad, upper_grad, gate_up_held, hidden_grads[h][2], gate_downs, resid_parts[h]
        )

    def back_out(h, parts):
        return out_back(parts, held["out"], own_wide[3], out_up, mixed, out_parts[h][2], h)

    def project_both(x):
        outs = [project_out(x[0], h) for h in every]
        held["gate_up"], done = load_early(w_gate_up, x[1], x[2:], places)
        return outs, done

    def load_rest(parts):
        held["gate_up"], done = load_late(held["gate_up"], parts, places)
        return done

    attn_pre, attn_scale, resid, resid_low = [None] * 2, [None] * 2, [None] * 2, [None] * 2
    resid_parts, hidden, feed_parts, output = [None] * 2, [None] * 2, [None] * 2, [None] * 2
    hidden_grads, resid_grads, grad_resid, out_grads = [None] * 2, [None] * 2, [None] * 2, [None] * 2
    (out_parts, done), [up_x0, up_z0, got] = side_by_side(
        project_both,
        [mixed, gate_up_near, gate_mine, gate_x, gate_z, *gate_last],
        [(by_x, up_mine[0]), (by_z, up_mine[0]), (chip, up_far_last[1])],
    )
    windows.carried.append(done)
    _, [got0, got1, up_last1] = side_by_side(
        None, None, [(core, out_parts[0][1]), (core, out_parts[1][1]), (core, got)]
    )
    own0, far0 = half_sums(out_parts[0][0], got0)
    own1, far1 = half_sums(out_parts[1][0], got1)
    _, [got0, up_x1, up_z1] = side_by_side(
        None, None, [(chip, far0), (by_x, up_mine[1]), (by_z, up_mine[1])]
    )
    attn_pre[0], attn_scale[0], resid[0], resid_low[0] = attention_rows(0, own0, got0)
    done, [resid_far] = side_by_side(
        load_rest, [up_mine, up_x0, up_x1, up_z0, up_z1, up_last0, up_last1], [(chip, resid_low[0])]
    )
    windows.carried.append(done)
    gate_up_held = held["gate_up"]
    _, [resid_near] = side_by_side(None, None, [(core, jnp.stack([resid_low[0], resid_far]))])
    resid_parts[0] = [resid_low[0], resid_far, resid_near]
    hidden[0], [got1] = side_by_side(up_gate, resid_parts[0], [(chip, far1)])
    cot = [x.astype(F32) for x in cot_rows]
    attn_pre[1], attn_scale[1], resid[1], resid_low[1] = attention_rows(1, own1, got1)
    feed_parts[0], [resid_far] = side_by_side(down, hidden[0][2], [(chip, resid_low[1])])
    _, [resid_near, got] = side_by_side(
        None, None, [(core, jnp.stack([resid_low[1], resid_far])), (core, feed_parts[0][1])]
    )
    resid_parts[1] = [resid_low[1], resid_far, resid_near]
    own0, far0 = half_sums(feed_parts[0][0], got)
    hidden[1], [got0] = side_by_side(up_gate, resid_parts[1], [(chip, far0)])
    output[0], grad0 = feed_rows(0, own0, got0)
    feed_parts[1], [grad_far] = side_by_side(down, hidden[1][2], [(chip, grad0)])
    _, [grad_near, got] = side_by_side(
        None, None, [(core, jnp.stack([grad0, grad_far])), (core, feed_parts[1][1])]
    )
    own1, far1 = half_sums(feed_parts[1][0], got)
    hidden_grads[0], [got1] = side_by_side(
        lambda x: back_down(0, x), [grad0, grad_far, grad_near], [(chip, far1)]
    )
    output[1], grad1 = feed_rows(1, own1, got1)
    output = return_cuts(output)
    resid_grads[0], [grad_far, output0] = side_by_side(
        lambda x: back_up_gate(0, *x), hidden_grads[0][:2], [(chip, grad1), (return_row(0), output[0])]
    )
    _, [grad_near, got] = side_by_side(
        None, None, [(core, jnp.stack([grad1, grad_far])), (core, resid_grads[0][1])]
    )
    own0, far0 = half_sums(resid_grads[0][0], got)
    hidden_grads[1], [got0, output1] = side_by_side(
        lambda x: back_down(1, x), [grad1, grad_far, grad_near], [(chip, far0), (return_row(1), output[1])]
    )
    output = return_order([output0, output1])
    grad_resid[0], grad0 = back_rows(0, own0, got0)

    broad = jnp.concatenate(
        [sum(g[3] for g in hidden_grads), sum(g[5] for g in hidden_grads).reshape(2 * rank, -1)]
    ).astype(BF)
    broad = [x[None] for x in jnp.split(broad, 2, axis=1)]
    step0, step1, step2 = [ctx_step(at) for at in range(3)]

    def grown(value, got):
        return jnp.concatenate([value, got])

    resid_grads[1], [grad_far, *got] = side_by_side(
        lambda x: back_up_gate(1, *x),
        hidden_grads[1][:2],
        [(chip, grad0), (step0, broad[0]), (step0, broad[1])],
    )
    broad = [grown(*pair) for pair in zip(broad, got)]
    own_early, far_early, cuts = column_cuts(
        jnp.concatenate([sum(g[4] for g in hidden_grads), sum(g[2] for g in resid_grads)]), flags["columns"]
    )
    _, [grad_near, got, got_early] = side_by_side(
        None, None, [(core, jnp.stack([grad0, grad_far])), (core, resid_grads[1][1]), (core, cuts)]
    )
    own1, far1 = half_sums(resid_grads[1][0], got)
    own_early = own_early + got_early[0].astype(F32)
    far_early = (far_early + got_early[1].astype(F32)).astype(BF)
    out_grads[0], [got1, got_early, got] = side_by_side(
        lambda x: back_out(0, x),
        [grad0, grad_far, grad_near],
        [(chip, far1), (chip, far_early), (step1, broad[0])],
    )
    broad[0] = grown(broad[0], got)
    early = (own_early + got_early.astype(F32)).astype(BF)[None]
    grad_resid[1], grad1 = back_rows(1, own1, got1)
    _, [grad_far, got, got_early] = side_by_side(
        None, None, [(chip, grad1), (step2, broad[0]), (step0, early)]
    )
    broad[0] = grown(broad[0], got)
    early = grown(early, got_early)
    _, [grad_near] = side_by_side(None, None, [(core, jnp.stack([grad1, grad_far]))])
    out_grads[1] = back_out(1, [grad1, grad_far, grad_near])
    grad_mixed = jnp.concatenate([g[0] for g in out_grads])

    attention_sends = [(step1, broad[1])]
    if simple:
        (query_turned, key_turned, grad_values, inner), [got] = side_by_side(
            lambda x: attention_back(
                queries, key_rows, pre, x, logs, cosine, sine, head_gains, chunks
            ),
            grad_mixed,
            attention_sends,
        )
    else:
        query_turned, key_turned, grad_values, inner = attention_grads(grad_mixed)
        [got] = [send(value) for send, value in attention_sends]
    broad[1] = grown(broad[1], got)
    inners, [got] = from_all(inner, [(step1, early)])
    early = grown(early, got)
    (grads, lows, down_late, up_late), [got] = side_by_side(
        lambda x: qkv_grads(x[:2], x[2], pre, squares, x[3:], token_parts, qkv_low, own_model, chunks),
        [query_turned, key_turned, grad_values, *inners],
        [(step2, early)],
    )
    early = grown(early, got)
    own_late, far_late, cuts = column_cuts(
        jnp.concatenate([down_late, sum(g[2] for g in out_grads)]), flags["columns"]
    )

    def rest_of(value):
        for at in range(3, len(ctx_flips())):
            value = grown(value, ctx_step(at)(value))
        if per_sequence > 1:
            value = jnp.sum(value.astype(F32)[gathered_place(ctx, table)], axis=1)
        return value

    def placed(sources, counts, plan, carried=()):
        width = sum(sources[piece[0]].shape[-1] for piece in plan[0][0])
        outs = [shape_of((count, adapters, rank, width), F32) for count in counts]
        return call(
            functools.partial(place_body, rank, len(sources), len(carried), plan),
            (1,),
            [*sources, *carried],
            [whole(x) for x in (*sources, *carried)],
            [(o, whole(o)) for o in outs],
            scalars=[where],
        )

    def back_qkv(x, p):
        return qkv_back(x, lows, qkv_held, qkv_downs, chunks, flags["turn"][p])

    def input_rows(p, own, got):
        return (pick(grad_resid, flags["return"][p]) + own + got.astype(F32)).astype(BF)

    def place_broad(x):
        return placed([rest_of(value) for value in x], (1, 2), ((((0, 0), (1, 0)),), (((0, 1), (1, 1)), ((0, 2), (1, 2)))))

    parts0, [got_late] = side_by_side(lambda x: back_qkv(x, 0), grads, [(core, cuts)])
    own_late = own_late + got_late[0].astype(F32)
    far_late = (far_late + got_late[1].astype(F32)).astype(BF)
    parts1, [got_late, got0] = side_by_side(
        lambda x: back_qkv(x, 1), grads, [(chip, far_late), (core, parts0[1])]
    )
    late = jnp.concatenate(
        [
            own_late + got_late.astype(F32),
            up_late.reshape(3 * rank, -1),
            sum(g[1] for g in out_grads),
        ]
    ).astype(BF)[None]
    own0, far0 = half_sums(parts0[0], got0)
    _, [got0, got1, got_late, got] = side_by_side(
        None, None, [(chip, far0), (core, parts1[1]), (step0, late), (step2, broad[1])]
    )
    broad[1] = grown(broad[1], got)
    late = grown(late, got_late)
    own1, far1 = half_sums(parts1[0], got1)
    (grad_down, grad_hidden), [got1, input0, got_late] = side_by_side(
        place_broad, broad, [(chip, far1), (return_row(0), input_rows(0, own0, got0)), (step1, late)]
    )
    late = grown(late, got_late)
    _, [input1, got_late] = side_by_side(
        None, None, [(return_row(1), input_rows(1, own1, got1)), (step2, late)]
    )
    input_grad = return_order([input0, input1]).astype(F32)
    late = rest_of(grown(late, got_late))
    early = rest_of(early)
    grad_wide, grad_model = placed(
        [early, late],
        (6, 5),
        (
            (((1, 0),), ((1, 1),), ((1, 2),), ((1, 7),), ((0, 1),), ((0, 2),)),
            (((1, 4),), ((1, 5),), ((1, 6),), ((1, 3),), ((0, 0),)),
        ),
        windows.carried,
    )
    return (output, input_grad, grad_wide, grad_down[0], grad_model, grad_hidden)


def solution(mesh):
    return jax.shard_map(
        on_device,
        mesh=mesh,
        in_specs=(
            P("shard", "ctx", None),
            P("shard", "ctx", None),
            P("shard", None),
            P(None, "shard", None),
            P(None, "shard", None),
            P("shard", None),
            P(None, "shard"),
            P(None, None, None, "shard"),
            P(None, None, "shard"),
            P(None, None, None, "shard"),
            P(None, None, None, "shard"),
        ),
        out_specs=(
            P("shard", "ctx", None),
            P("shard", "ctx", None),
            P(None, None, None, "shard"),
            P(None, None, "shard"),
            P(None, None, None, "shard"),
            P(None, None, None, "shard"),
        ),
        check_vma=False,
    )
```

```python
import functools
import math

import jax
import jax.numpy as jnp
from jax import lax
from jax.experimental import pallas as pl
from jax.experimental.pallas import tpu as pltpu
from jax.sharding import PartitionSpec as P

D = 2048
HEADS = 16
HD = 128
BLOCK = 256

epsilon = 1e-06
rope_base = 500000.0
far_below = -1e30
BF = jnp.bfloat16
F32 = jnp.float32
VMEM_BYTES = 16 * 2**20


def dot(left, right):
    return lax.dot_general(left, right, (((1,), (0,)), ((), ())), preferred_element_type=F32)


def dot_nt(left, right):
    return lax.dot_general(left, right, (((1,), (1,)), ((), ())), preferred_element_type=F32)


def dot_tn(left, right):
    return lax.dot_general(left, right, (((0,), (0,)), ((), ())), preferred_element_type=F32)


def over_shard(value, flip):
    size = lax.axis_size("shard")
    return lax.ppermute(value, "shard", [(i, i ^ flip) for i in range(size)])


class Windows:
    def __init__(self):
        self.carried = []

    def side_by_side(self, run, inputs, sends):
        values = [value for _, value in sends]
        inputs, values, self.carried = lax.optimization_barrier((inputs, values, self.carried))
        got = [send(value) for (send, _), value in zip(sends, values)]
        out = run(inputs) if run else None
        out, got, self.carried = lax.optimization_barrier((out, got, self.carried))
        return out, got


def over_ctx(value, flip):
    size = lax.axis_size("ctx")
    return lax.ppermute(value, "ctx", [(i, i ^ flip) for i in range(size)])


FLIPS = (0, 2, 1, 3)


def call(body, grid, args, in_specs, outs, scratch=(), scalars=(), flops=0, aliases={}):
    placed = []
    for arg, spec in zip(args, in_specs):
        if spec.memory_space == pltpu.VMEM:
            arg = pltpu.with_memory_space_constraint(arg, pltpu.VMEM)
        elif spec.memory_space == pltpu.HBM:
            arg = pltpu.with_memory_space_constraint(arg, pltpu.HBM)
        placed.append(arg)
    return pl.pallas_call(
        body,
        grid_spec=pltpu.PrefetchScalarGridSpec(
            num_scalar_prefetch=len(scalars),
            grid=grid,
            in_specs=in_specs,
            out_specs=[spec for _, spec in outs],
            scratch_shapes=scratch,
        ),
        out_shape=[shape for shape, _ in outs],
        input_output_aliases=aliases,
        compiler_params=pltpu.CompilerParams(vmem_limit_bytes=VMEM_BYTES),
        cost_estimate=pl.CostEstimate(flops=flops, bytes_accessed=0, transcendentals=0),
    )(*scalars, *placed)


def shape_of(shape, kind):
    return jax.ShapeDtypeStruct(shape, kind)


def whole(value):
    zeros = (0,) * value.ndim
    return pl.BlockSpec(value.shape, lambda *_: zeros)


def spec(block, index):
    return pl.BlockSpec(block, lambda i, *_: index(i))


def column_spec(value, tile):
    zeros = (0,) * (value.ndim - 1)
    return pl.BlockSpec(value.shape[:-1] + (tile,), lambda i, *_: (*zeros, i))


HBM = pl.BlockSpec(memory_space=pltpu.HBM)
ANY = pl.BlockSpec(memory_space=pl.ANY)
VMEM = pl.BlockSpec(memory_space=pltpu.VMEM)


def tile_of(width):
    return min(512, width)


def run_copies(copies):
    for copy in copies:
        copy.start()
    for copy in copies:
        copy.wait()


def cut_body(first, apart, places, weight, near, *refs):
    fars, sems = refs[:-1], refs[-1]
    step = pl.program_id(0)
    width = near.shape[2]
    slim = fars[0].shape[1]
    rows = pl.ds(pl.multiple_of(places[1] * slim, slim), slim)

    def columns(flip):
        return pl.ds(pl.multiple_of((places[0] ^ flip) * width, width), width)

    def copies(far, cross):
        sources = [(slice(None), columns(1), near), (rows, columns(2), far), (rows, columns(3), cross)]
        return [
            pltpu.make_async_copy(weight.at[first + step, r, c], to.at[0], sems.at[i])
            for i, (r, c, to) in enumerate(sources)
        ]

    if apart:
        for matrix in range(len(fars) // 2):
            pair = fars[2 * matrix : 2 * matrix + 2]
            pl.when(step == matrix)(functools.partial(lambda pair: run_copies(copies(*pair)), pair))
    else:
        run_copies(copies(*fars))


def cut(weight, first, count, places, apart):
    depth, full = weight.shape[1:]
    width, slim = full // 4, depth // 4
    if apart:
        far = (shape_of((1, slim, width), BF), pl.BlockSpec((1, slim, width), lambda *_: (0, 0, 0)))
    else:
        far = (shape_of((count, slim, width), BF), pl.BlockSpec((1, slim, width), lambda m, _: (m, 0, 0)))
    return call(
        functools.partial(cut_body, first, apart),
        (count,),
        [weight],
        [HBM],
        [(shape_of((count, depth, width), BF), pl.BlockSpec((1, depth, width), lambda m, _: (m, 0, 0)))]
        + [far] * (2 * count if apart else 2),
        [pltpu.SemaphoreType.DMA((3,))],
        scalars=[places],
    )


COPIES = 10
PARTS = 8


def copies_of(weight, matrix, near, near_at, parts, at, places, held, sems):
    width = held.shape[1]
    depth = held.shape[0] // 4
    slim = depth // 4
    shard, quarter = places[0], places[1]

    def to(flip, rows, begin=0):
        start = pl.multiple_of((shard ^ flip) * depth + begin, slim)
        return held.at[pl.ds(start, rows), :]

    pairs = []
    if weight is not None:
        own_columns = pl.ds(pl.multiple_of(shard * width, width), width)
        pairs.append((weight.at[matrix, :, own_columns], to(0, depth)))
    if near is not None:
        pairs.append((near.at[near_at], to(1, depth)))
    for i, part in enumerate(parts):
        if part is not None:
            pairs.append((part.at[at], to(2 + i % 2, slim, (quarter ^ (i // 2)) * slim)))
    return [pltpu.make_async_copy(source, target, sems.at[i]) for i, (source, target) in enumerate(pairs)]


DONE = (shape_of((8, 128), F32), pl.BlockSpec((8, 128), lambda *_: (0, 0)))


def load_plain_body(attn, out_held, done, sem):
    run_copies([pltpu.make_async_copy(attn.at[attn.shape[0] - 1], out_held, sem)])
    done[...] = jnp.zeros_like(done)


def load_plain(w_attn):
    return call(
        load_plain_body,
        (1,),
        [w_attn],
        [HBM],
        [(pltpu.VMEM(w_attn.shape[1:], BF), VMEM), DONE],
        [pltpu.SemaphoreType.DMA],
    )


def load_body(first, there, places, *refs):
    refs = list(refs)
    weight, near = (refs.pop(0), refs.pop(0)) if first else (None, None)
    parts = [[refs.pop(0) if is_there else None for is_there in matrix] for matrix in there]
    held, done, sems = refs[-3:]
    copies = []
    for m, matrix_parts in enumerate(parts):
        copies += copies_of(weight, m, near, m, matrix_parts, 0, places, held.at[m], sems.at[m])
    run_copies(copies)
    done[...] = jnp.zeros_like(done)


def load(parts, places, weight=None, near=None, held=None):
    there = [[part is not None for part in matrix] for matrix in parts]
    arrays = [part for matrix in parts for part in matrix if part is not None]
    arrays = ([weight, near] if held is None else []) + arrays
    depth, full = (weight if held is None else held).shape[1:]
    shape = (2, 4 * depth, full // 4) if held is None else held.shape
    return call(
        functools.partial(load_body, held is None, there),
        (1,),
        arrays + ([] if held is None else [held]),
        ([HBM] + [ANY] * (len(arrays) - 1) if held is None else [ANY] * len(arrays) + [VMEM]),
        [(pltpu.VMEM(shape, BF), VMEM), DONE],
        [pltpu.SemaphoreType.DMA((2, COPIES))],
        [places],
        aliases={} if held is None else {1 + len(arrays): 0},
    )


def row_of(column):
    return jnp.transpose(jnp.broadcast_to(column, (column.shape[0], 128)))[:8]


def column_of(row):
    return jnp.transpose(jnp.broadcast_to(row[:1], (128, row.shape[1])))[:, :1]


def qkv_body(chunks, size, places, *refs):
    x_refs, refs = refs[:3], refs[3:]
    weight, near, weight_parts, refs = refs[0], refs[1], refs[2 : 2 + PARTS], refs[2 + PARTS :]
    down, up, pre, low, sums, kept, held, rows, sems, keep_sems = refs
    step = pl.program_id(0)

    def copies(p):
        return copies_of(weight, p, near, p, weight_parts, p, places, held.at[p], sems.at[p])

    @pl.when(step == 0)
    def _():
        for p in range(held.shape[0]):
            for copy in copies(p):
                copy.start()
        for h in range(chunks):
            rows[4 * h * size : 4 * (h + 1) * size] = load_parts(x_refs, h * size, size)

    lowrank = dot_nt(rows[...], down[...]).astype(BF)
    for copy in copies(step):
        copy.wait()
    keep = [pltpu.make_async_copy(held.at[p], kept.at[p], keep_sems.at[p]) for p in range(held.shape[0])]
    for p, copy in enumerate(keep):
        pl.when(step == p)(copy.start)
    value = dot(rows[...], held[step]) + dot(lowrank, up[0])
    pre[0] = value.astype(BF)
    low[0] = lowrank
    sums[...] = row_of(jnp.sum(value * value, axis=1, keepdims=True))

    @pl.when(step == held.shape[0] - 1)
    def _():
        for copy in keep:
            copy.wait()


def qkv_forward(x_parts, chunks, size, weight, weight_parts, places, downs, ups):
    count, depth, width = weight_parts[0].shape
    full = x_parts[0].shape[1]
    total, rank = 4 * chunks * size, ups.shape[1]
    return call(
        functools.partial(qkv_body, chunks, size),
        (count,),
        [*x_parts, weight, *weight_parts, downs, ups],
        [whole(x) for x in x_parts]
        + [HBM] * (2 + PARTS)
        + [
            spec((rank, full), lambda p: (p, 0)),
            spec((1, rank, width), lambda p: (p, 0, 0)),
        ],
        [
            (shape_of((count, total, width), BF), spec((1, total, width), lambda p: (p, 0, 0))),
            (shape_of((count, total, rank), BF), spec((1, total, rank), lambda p: (p, 0, 0))),
            (shape_of((8 * count, total), F32), spec((8, total), lambda p: (p, 0))),
            (pltpu.HBM((count, full, width), BF), HBM),
        ],
        [
            pltpu.VMEM((count, full, width), BF),
            pltpu.VMEM((total, full), BF),
            pltpu.SemaphoreType.DMA((count, COPIES)),
            pltpu.SemaphoreType.DMA((count,)),
        ],
        [places],
        flops=2 * total * full * width * count,
    )


def aligned_sums(refs, which, chunks):
    total = refs[0].shape[1]
    block = total // (4 * chunks)
    out = 0.0
    for flip, ref in zip(FLIPS, refs):
        column = column_of(ref[8 * which : 8 * which + 8])
        if flip:
            order = [FLIPS.index(f ^ flip) for f in FLIPS]
            column = jnp.concatenate(
                [
                    column[(4 * h + i) * block : (4 * h + i + 1) * block]
                    for h in range(chunks)
                    for i in order
                ]
            )
        out = out + column
    return out


def attention_body(chunks, factor, *refs):
    (
        query_pre, key_pre, value, own, far, near, cross, cosine, sine, gains,
        query_out, key_out, mixed_out, logs_out, scale_rows,
    ) = refs
    total = query_pre.shape[1]
    size = total // chunks

    @pl.when(pl.program_id(0) == 0)
    def _():
        for p in range(2):
            sums = aligned_sums((own, far, near, cross), p, chunks)
            scale_rows[p] = jnp.broadcast_to(lax.rsqrt(sums / D + epsilon), (total, HD))

    def prepared(pre, p):
        value = pre[0].astype(F32) * scale_rows[p] * gains[p : p + 1]
        return (value * cosine[...] + pltpu.roll(value, HD // 2, 1) * sine[...]).astype(BF)

    query, key = prepared(query_pre, 0), prepared(key_pre, 1)
    query_out[...] = query
    key_out[...] = key
    logs = []
    for h in range(chunks):
        seen = (h + 1) * size
        scores = dot_nt(query[h * size : (h + 1) * size], key[:seen]) * factor
        top = jnp.max(scores, axis=1, keepdims=True)
        weights = jnp.exp(scores - top)
        sums = jnp.sum(weights, axis=1, keepdims=True)
        probs = (weights * (1.0 / sums)).astype(BF)
        mixed_out[h * size : (h + 1) * size] = dot(probs, value[0, :seen]).astype(BF)
        logs.append(top + jnp.log(sums))
    logs_out[...] = row_of(jnp.concatenate(logs))


def attention_forward(pre, sums, cosine, sine, gains, chunks):
    _, total, width = pre.shape
    heads = width // HD
    factor = 1.0 / math.sqrt(HD)

    def head(p):
        return spec((1, total, HD), lambda i: (p, 0, i))

    by_head = spec((total, HD), lambda i: (0, i))
    return call(
        functools.partial(attention_body, chunks, factor),
        (heads,),
        [pre, pre, pre, *sums, cosine, sine, gains],
        [head(0), head(1), head(2)]
        + [whole(s) for s in sums]
        + [whole(cosine), whole(sine), spec((gains.shape[0], HD), lambda i: (0, i))],
        [
            (shape_of((total, width), BF), by_head),
            (shape_of((total, width), BF), by_head),
            (shape_of((total, width), BF), by_head),
            (shape_of((8 * heads, total), F32), spec((8, total), lambda i: (i, 0))),
        ],
        [pltpu.VMEM((2, total, HD), F32)],
        flops=4 * total * total * width,
    )


def attention_back_body(chunks, factor, *refs):
    (
        query_in, key_in, query_pre, key_pre, value, grad_in, logs, cosine, sine, gains,
        query_out, key_out, value_out, inner_out, inner_rows,
    ) = refs
    total = query_in.shape[0]
    size = total // chunks
    head = pl.program_id(0)
    query, key, values, grad = query_in[...], key_in[...], value[0], grad_in[...]
    log_column = column_of(logs[...])
    grad_key = [0.0] * chunks
    grad_value = [0.0] * chunks
    grad_query = []
    for h in range(chunks):
        rows = slice(h * size, (h + 1) * size)
        grad_row = 0.0
        delta = 0.0
        kept = []
        for k in range(h + 1):
            keys = slice(k * size, (k + 1) * size)
            scores = dot_nt(query[rows], key[keys]) * factor
            probs = jnp.exp(scores - log_column[rows])
            grad_probs = dot_nt(grad[rows], values[keys])
            delta = delta + jnp.sum(probs * grad_probs, axis=1, keepdims=True)
            kept.append((probs, grad_probs))
        for k, (probs, grad_probs) in enumerate(kept):
            keys = slice(k * size, (k + 1) * size)
            grad_scores = (probs * (grad_probs - delta)).astype(BF)
            grad_row = grad_row + dot(grad_scores, key[keys])
            grad_key[k] = grad_key[k] + dot_tn(grad_scores, query[rows])
            grad_value[k] = grad_value[k] + dot_tn(probs.astype(BF), grad[rows])
        grad_query.append(grad_row)

    value_out[...] = jnp.concatenate(grad_value).astype(BF)
    for p, (pre, grads, out) in enumerate(
        ((query_pre, grad_query, query_out), (key_pre, grad_key, key_out))
    ):
        turned = jnp.concatenate(grads) * factor
        turned = turned * cosine[...] - pltpu.roll(turned, HD // 2, 1) * sine[...]
        turned = turned * gains[p : p + 1]
        out[...] = turned.astype(BF)
        inner = jnp.sum(turned * pre[0].astype(F32), axis=1, keepdims=True)
        inner = jnp.broadcast_to(inner, (total, 128))

        @pl.when(head == 0)
        def _():
            inner_rows[p] = inner

        @pl.when(head > 0)
        def _():
            inner_rows[p] += inner

    @pl.when(head == pl.num_programs(0) - 1)
    def _():
        for p in range(2):
            inner_out[8 * p : 8 * p + 8] = jnp.transpose(inner_rows[p])[:8]


def attention_back(queries, key_rows, pre, grad_mixed, logs, cosine, sine, gains, chunks):
    _, total, width = pre.shape
    heads = width // HD
    factor = 1.0 / math.sqrt(HD)

    def head(p):
        return spec((1, total, HD), lambda i: (p, 0, i))

    by_head = spec((total, HD), lambda i: (0, i))
    return call(
        functools.partial(attention_back_body, chunks, factor),
        (heads,),
        [queries, key_rows, pre, pre, pre, grad_mixed, logs, cosine, sine, gains],
        [by_head, by_head, head(0), head(1), head(2), by_head]
        + [spec((8, total), lambda i: (i, 0)), whole(cosine), whole(sine)]
        + [spec((gains.shape[0], HD), lambda i: (0, i))],
        [
            (shape_of((total, width), BF), by_head),
            (shape_of((total, width), BF), by_head),
            (shape_of((total, width), BF), by_head),
            (shape_of((16, total), F32), pl.BlockSpec((16, total), lambda *_: (0, 0))),
        ],
        [pltpu.VMEM((2, total, 128), F32)],
        flops=10 * total * total * width,
    )


def split_out(value, keep, send, columns=slice(None)):
    half = value.shape[0] // 2
    keep[:, columns] = value[:half].astype(BF)
    send[:, columns] = value[half:].astype(BF)


def qkv_grads_body(chunks, *refs):
    query_grad, key_grad, value_grad, query_pre, key_pre = refs[:5]
    squares, inners, x_refs = refs[5:9], refs[9:13], refs[13:16]
    low, ups, grads, lows, down_out, up_out = refs[16:]
    rank = ups.shape[1]
    total = query_grad.shape[0]
    for p, (grad, pre) in enumerate(((query_grad, query_pre), (key_grad, key_pre))):
        scale = lax.rsqrt(aligned_sums(squares, p, chunks) / D + epsilon)
        inner = aligned_sums(inners, p, chunks) * (scale * scale * scale / D)
        grads[p] = (grad[...].astype(F32) * scale - pre[0].astype(F32) * inner).astype(BF)
    grads[2] = value_grad[...]
    for p in range(3):
        lows[:, p * rank : (p + 1) * rank] = dot_nt(grads[p], ups[p]).astype(BF)
        up_out[p] = dot_tn(low[p], grads[p])
    size = total // chunks
    down = 0.0
    for h in range(chunks):
        x = load_parts(x_refs, h * size // 4, size // 4)
        down += dot_tn(lows[h * size : (h + 1) * size], x)
    down_out[...] = down


def qkv_grads(turned, grad_values, pre, squares, inners, x_parts, low, ups, chunks):
    count, total, width = pre.shape
    rank = ups.shape[1]
    full = x_parts[0].shape[1]

    def pre_rows(p):
        return pl.BlockSpec((1, total, width), lambda *_: (p, 0, 0))

    outs = [
        shape_of((count, total, width), BF),
        shape_of((total, count * rank), BF),
        shape_of((count * rank, full), F32),
        shape_of((count, rank, width), F32),
    ]
    return call(
        functools.partial(qkv_grads_body, chunks),
        (1,),
        [*turned, grad_values, pre, pre, *squares, *inners, *x_parts, low, ups],
        [whole(turned[0]), whole(turned[1]), whole(grad_values), pre_rows(0), pre_rows(1)]
        + [whole(v) for v in (*squares, *inners, *x_parts, low)]
        + [pl.BlockSpec((count, rank, width), lambda *_: (0, 0, 0))],
        [(o, whole(o)) for o in outs],
        flops=2 * total * width * 512,
    )


def qkv_back_body(_, grads, lows, weight, downs, keep, send):
    value = dot(lows[...], downs[...])
    for p in range(3):
        value += dot_nt(grads[p], weight[p])
    split_out(value, keep, send)


def qkv_back(grads, lows, weight, downs, chunks, chunk):
    count, full, width = weight.shape
    total = grads.shape[1]
    size = total // chunks
    tile = tile_of(full)
    half = size // 2
    return call(
        qkv_back_body,
        (full // tile,),
        [grads, lows, weight, downs],
        [
            pl.BlockSpec((count, size, width), lambda i, c: (0, c[0], 0)),
            pl.BlockSpec((size, lows.shape[1]), lambda i, c: (c[0], 0)),
            spec((count, tile, width), lambda i: (0, i, 0)),
            spec((downs.shape[0], tile), lambda i: (0, i)),
        ],
        [
            (shape_of((half, full), BF), spec((half, tile), lambda i: (0, i))),
            (shape_of((half, full), BF), spec((half, tile), lambda i: (0, i))),
        ],
        scalars=[chunk],
        flops=2 * size * full * width * count,
    )


def partial_body(streamed, beside, x, weight, down, up, *refs):
    keep, send, low, *scratch = refs[beside:]
    step = pl.program_id(0)
    tile = keep.shape[1]

    def columns(i):
        return pl.ds(pl.multiple_of(i * tile, tile), tile)

    def copy(i):
        held, sems = scratch
        return pltpu.make_async_copy(weight.at[:, columns(i)], held.at[:, columns(i)], sems.at[i])

    @pl.when(step == 0)
    def _():
        if streamed:
            for i in range(weight.shape[1] // tile):
                copy(i).start()
        low[...] = dot_nt(x[...], down[...]).astype(BF)

    if streamed:
        copy(step).wait()
        held = scratch[0]
    else:
        held = weight
    split_out(dot(x[...], held[:, columns(step)]) + dot(low[...], up[...]), keep, send)


def partial_forward(x, chunk, chunks, weight, down, up, streamed, beside=()):
    total, depth = x.shape
    size = total // chunks
    full = weight.shape[-1]
    tile = tile_of(full)
    half = size // 2
    rank = down.shape[0]
    scratch = [pltpu.VMEM(weight.shape, BF), pltpu.SemaphoreType.DMA((full // tile,))]
    return call(
        functools.partial(partial_body, streamed, len(beside)),
        (full // tile,),
        [x, weight, down, up, *beside],
        [
            pl.BlockSpec((size, depth), lambda *_: (chunk, 0)),
            HBM if streamed else VMEM,
            whole(down),
            spec((rank, tile), lambda i: (0, i)),
            *[VMEM] * len(beside),
        ],
        [
            (shape_of((half, full), BF), spec((half, tile), lambda i: (0, i))),
            (shape_of((half, full), BF), spec((half, tile), lambda i: (0, i))),
            (shape_of((size, rank), BF), pl.BlockSpec((size, rank), lambda *_: (0, 0))),
        ],
        scratch if streamed else (),
        flops=2 * size * depth * full,
    )


def gate_up_body(*refs):
    x_refs, (weight, downs, ups, gate, upper, act, low, rows) = refs[:4], refs[4:]
    rank = ups.shape[1]
    tile = gate.shape[1]
    step = pl.program_id(0)

    @pl.when(step == 0)
    def _():
        rows[...] = load_parts(x_refs)
        low[...] = dot_nt(rows[...], downs[...]).astype(BF)

    columns = pl.ds(pl.multiple_of(step * tile, tile), tile)
    gate_pre = dot(rows[...], weight[0, :, columns]) + dot(low[:, :rank], ups[0])
    upper_pre = dot(rows[...], weight[1, :, columns]) + dot(low[:, rank:], ups[1])
    gate[...] = gate_pre.astype(BF)
    upper[...] = upper_pre.astype(BF)
    act[...] = (gate_pre * jax.nn.sigmoid(gate_pre) * upper_pre).astype(BF)


def gate_up_forward(x_parts, weight, downs, ups):
    _, full, width = weight.shape
    size = 4 * x_parts[0].shape[0]
    rank = ups.shape[1]
    tile = tile_of(width)
    out = (shape_of((size, width), BF), spec((size, tile), lambda i: (0, i)))
    return call(
        gate_up_body,
        (width // tile,),
        [*x_parts, weight, downs, ups],
        [whole(x) for x in x_parts] + [VMEM, whole(downs), spec((2, rank, tile), lambda i: (0, 0, i))],
        [
            out,
            out,
            out,
            (shape_of((size, 2 * rank), BF), pl.BlockSpec((size, 2 * rank), lambda *_: (0, 0))),
        ],
        [pltpu.VMEM((size, full), BF)],
        flops=4 * size * full * width,
    )


def feed_back_body(*refs):
    g_refs = refs[:4]
    weight, down, gate, upper, gate_low, feed_low, feed_up, ups, _ = refs[4:13]
    gate_grad, upper_grad, low_out, down_a, feed_b, hidden_b, rows, low, lows = refs[13:]
    rank = down.shape[0]
    step = pl.program_id(0)
    @pl.when(step == 0)
    def _():
        rows[...] = load_parts(g_refs)
        low[...] = dot_nt(rows[...], feed_up[...]).astype(BF)
        feed_b[...] = dot_tn(feed_low[...], rows[...])
        lows[...] = jnp.zeros_like(lows)

    grad_act = dot_nt(rows[...], weight[...]) + dot(low[...], down[...])
    gate_pre, upper_pre = gate[...].astype(F32), upper[...].astype(F32)
    sig = jax.nn.sigmoid(gate_pre)
    silu = gate_pre * sig
    down_a[...] = dot_tn(low[...], (silu * upper_pre).astype(BF))
    grad_upper = (grad_act * silu).astype(BF)
    grad_gate = (grad_act * upper_pre * (sig + silu * (1.0 - sig))).astype(BF)
    gate_grad[...] = grad_gate
    upper_grad[...] = grad_upper
    hidden_b[0] = dot_tn(gate_low[:, :rank], grad_gate)
    hidden_b[1] = dot_tn(gate_low[:, rank:], grad_upper)
    lows[:, :rank] += dot_nt(grad_gate, ups[0])
    lows[:, rank:] += dot_nt(grad_upper, ups[1])

    @pl.when(step == pl.num_programs(0) - 1)
    def _():
        low_out[...] = lows[...].astype(BF)


def feed_back(g_parts, weight, down, gate, upper, gate_low, feed_low, feed_up, ups, beside):
    width, depth = weight.shape
    size = 4 * g_parts[0].shape[0]
    rank = down.shape[0]
    tile = tile_of(width)
    weight = pltpu.with_memory_space_constraint(weight, pltpu.HBM)
    by_tile = spec((size, tile), lambda i: (0, i))
    return call(
        feed_back_body,
        (width // tile,),
        [*g_parts, weight, down, gate, upper, gate_low, feed_low, feed_up, ups, beside],
        [whole(g) for g in g_parts]
        + [
            spec((tile, depth), lambda i: (i, 0)),
            spec((rank, tile), lambda i: (0, i)),
            by_tile,
            by_tile,
            whole(gate_low),
            whole(feed_low),
            whole(feed_up),
            spec((2, rank, tile), lambda i: (0, 0, i)),
            VMEM,
        ],
        [
            (shape_of((size, width), BF), by_tile),
            (shape_of((size, width), BF), by_tile),
            (shape_of((size, 2 * rank), BF), pl.BlockSpec((size, 2 * rank), lambda *_: (0, 0))),
            (shape_of((rank, width), F32), spec((rank, tile), lambda i: (0, i))),
            (shape_of((rank, depth), F32), pl.BlockSpec((rank, depth), lambda *_: (0, 0))),
            (shape_of((2, rank, width), F32), spec((2, rank, tile), lambda i: (0, 0, i))),
        ],
        [
            pltpu.VMEM((size, depth), BF),
            pltpu.VMEM((size, rank), BF),
            pltpu.VMEM((size, 2 * rank), F32),
        ],
        flops=2 * size * depth * width,
    )


def gate_up_back_body(gate_grad, upper_grad, weight, low, downs, *refs):
    x_refs, (keep, send, down_out) = refs[:4], refs[4:]
    tile = keep.shape[1]
    held_rows = pl.ds(pl.multiple_of(pl.program_id(0) * tile, tile), tile)
    value = dot_nt(gate_grad[...], weight[0, held_rows]) + dot_nt(upper_grad[...], weight[1, held_rows])
    split_out(value + dot(low[...], downs[...]), keep, send)
    down_out[...] = dot_tn(low[...], load_parts(x_refs))


def gate_up_back(gate_grad, upper_grad, weight, low, downs, x_parts):
    _, full, width = weight.shape
    size = gate_grad.shape[0]
    half = size // 2
    ranks = downs.shape[0]
    tile = tile_of(full)
    return call(
        gate_up_back_body,
        (full // tile,),
        [gate_grad, upper_grad, weight, low, downs, *x_parts],
        [whole(gate_grad), whole(upper_grad), VMEM, whole(low), spec((ranks, tile), lambda i: (0, i))]
        + [column_spec(x, tile) for x in x_parts],
        [
            (shape_of((half, full), BF), spec((half, tile), lambda i: (0, i))),
            (shape_of((half, full), BF), spec((half, tile), lambda i: (0, i))),
            (shape_of((ranks, full), F32), spec((ranks, tile), lambda i: (0, i))),
        ],
        flops=4 * size * full * width,
    )


def out_back_body(*refs):
    g_refs = refs[:4]
    weight, down, up, mixed, low, grad_mixed, down_out, up_out, rows, grad_low = refs[4:]

    @pl.when(pl.program_id(0) == 0)
    def _():
        rows[...] = load_parts(g_refs)
        grad_low[...] = dot_nt(rows[...], up[...]).astype(BF)
        up_out[...] = dot_tn(low[...], rows[...])

    tile = grad_mixed.shape[1]
    held_rows = pl.ds(pl.multiple_of(pl.program_id(0) * tile, tile), tile)
    grad_mixed[...] = (dot_nt(rows[...], weight[held_rows]) + dot(grad_low[...], down[...])).astype(BF)
    down_out[...] = dot_tn(grad_low[...], mixed[...])


def out_back(g_parts, weight, down, up, mixed, low, chunk):
    width, depth = weight.shape
    size = 4 * g_parts[0].shape[0]
    rank = down.shape[0]
    tile = min(256, width)
    return call(
        out_back_body,
        (width // tile,),
        [*g_parts, weight, down, up, mixed, low],
        [whole(g) for g in g_parts]
        + [
            VMEM,
            spec((rank, tile), lambda i: (0, i)),
            whole(up),
            spec((size, tile), lambda i: (chunk, i)),
            whole(low),
        ],
        [
            (shape_of((size, width), BF), spec((size, tile), lambda i: (0, i))),
            (shape_of((rank, width), F32), spec((rank, tile), lambda i: (0, i))),
            (shape_of((rank, depth), F32), pl.BlockSpec((rank, depth), lambda *_: (0, 0))),
        ],
        [pltpu.VMEM((size, depth), BF), pltpu.VMEM((size, rank), BF)],
        flops=2 * size * depth * width,
    )


def load_parts(refs, first=0, count=None, columns=slice(None)):
    own, far, *near = refs
    if len(near) == 1:
        near = near[0].at[0], near[0].at[1]
    rows = slice(first, own.shape[0] if count is None else first + count)
    return jnp.concatenate([ref[rows, columns] for ref in (own, far, *near)])


def ctx_flips():
    size = lax.axis_size("ctx")
    return [flip for flip in (2, 4, 8, 16, 1) if flip < size]


def ctx_step(at):
    return lambda value: over_ctx(value, ctx_flips()[at])


def gathered_place(ctx, other):
    place = 0
    for at, flip in enumerate(ctx_flips()):
        place = place + (((ctx ^ other) // flip) % 2) * 2**at
    return place


def column_cuts(partial, starts):
    width = partial.shape[-1] // 4
    zero = jnp.uint32(0)
    blocks = [lax.dynamic_slice(partial, (zero, start), (partial.shape[0], width)) for start in starts]
    return blocks[0], blocks[1], jnp.stack(blocks[2:]).astype(BF)


def natural(parts, shard):
    out = []
    for index in range(4):
        value = parts[0]
        for flip, part in zip(FLIPS[1:], parts[1:]):
            value = jnp.where((shard ^ flip) == index, part, value)
        out.append(value)
    return out


def row_sum(keep, near, got):
    rows = got.shape[0]
    return keep[:rows].astype(F32) + near[:rows].astype(F32) + got[...].astype(F32)


def rms_scale(value):
    return lax.rsqrt(jnp.mean(value * value, axis=-1, keepdims=True) + epsilon)


def rms_back(value, scale, gain, grad):
    weighted = grad * gain
    return scale * weighted - value * (
        scale * scale * scale * jnp.mean(value * weighted, axis=-1, keepdims=True)
    )


def far_body(keep, near, far):
    rows = far.shape[0]
    far[...] = (keep[rows:].astype(F32) + near[rows:].astype(F32)).astype(BF)


def attention_rows_body(keep, near, got, token, gain, value_out, resid_out, low_out):
    value = row_sum(keep, near, got)
    resid = token[...].astype(F32) + value * rms_scale(value) * gain[...]
    value_out[...] = value
    resid_out[...] = resid
    low_out[...] = resid.astype(BF)


def feed_rows_body(keep, near, got, resid, cot, gain, output, grad):
    value = row_sum(keep, near, got)
    scale = rms_scale(value)
    output[...] = (resid[...] + value * scale * gain[...]).astype(BF)
    grad[...] = rms_back(value, scale, gain[...], cot[...].astype(F32)).astype(BF)


def back_rows_body(keep, near, got, value, cot, gain, grad_out, low_out):
    grad = cot[...].astype(F32) + row_sum(keep, near, got)
    grad_out[...] = grad
    value = value[...]
    low_out[...] = rms_back(value, rms_scale(value), gain[...], grad).astype(BF)


def input_rows_body(order, keep, near, got, first, second, out):
    value = row_sum(keep, near, got)

    @pl.when(order[0] == 0)
    def _():
        out[...] = (value + first[...]).astype(BF)

    @pl.when(order[0] != 0)
    def _():
        out[...] = (value + second[...]).astype(BF)


def by_rows(body, args, kinds, scalars=()):
    rows = args[0].shape[0] // 2
    outs = [shape_of((rows, args[0].shape[1]), kind) for kind in kinds]
    return call(body, (1,), args, [whole(x) for x in args], [(o, whole(o)) for o in outs], scalars=scalars)


def rotate(value, cosine, sine):
    half = value.shape[-1] // 2
    turned = jnp.concatenate([value[..., half:], value[..., :half]], axis=-1)
    return value * cosine[:, None, :] + turned * sine[:, None, :]


def realign(value, flip, chunks):
    shape = value.shape
    value = value.reshape(shape[0], chunks, 2, 2, -1)
    if flip & 1:
        value = value[:, :, ::-1]
    if flip & 2:
        value = value[:, :, :, ::-1]
    return value.reshape(shape)


def group_of(sequence, part, per_sequence, ctx_size):
    if per_sequence > 1:
        return sequence * per_sequence + part
    depth = sequence % (ctx_size // 2)
    return 2 * depth + (depth + sequence // (ctx_size // 2)) % 2


def sequence_of(ctx, per_sequence, ctx_size):
    if per_sequence > 1:
        return ctx // per_sequence, ctx % per_sequence
    depth = ctx // 2
    return depth + ctx_size // 2 * ((ctx + depth) % 2), 0 * ctx


def wide_attention(pre, sums, cosine, sine, gains, chunks, positions, groups):
    _, total, width = pre.shape
    heads = width // HD
    pre = pre.astype(F32)
    squares = sum(realign(s[::8], flip, chunks) for flip, s in zip(FLIPS, sums))
    scales = lax.rsqrt(squares[:2] / D + epsilon)[:, :, None]

    def as_heads(value):
        return value.reshape(total, heads, HD)

    queries, key_rows = [
        rotate(as_heads(pre[p] * scales[p] * gains[p]), cosine, sine).astype(BF) for p in range(2)
    ]

    def over_sequence(value):
        return lax.all_gather(value, "ctx", axis=0, tiled=True, axis_index_groups=groups)

    key_all, value_all = over_sequence(key_rows), over_sequence(as_heads(pre[2].astype(BF)))
    visible = over_sequence(positions // BLOCK)[None, :] <= (positions // BLOCK)[:, None]
    factor = 1.0 / math.sqrt(HD)
    scores = jnp.einsum("qhd,khd->hqk", queries, key_all, preferred_element_type=F32) * factor
    scores = jnp.where(visible, scores, far_below)
    weights = jnp.exp(scores - jnp.max(scores, axis=-1, keepdims=True))
    probs = weights / jnp.sum(weights, axis=-1, keepdims=True)
    mixed = jnp.einsum("hqk,khd->qhd", probs.astype(BF), value_all, preferred_element_type=F32)
    mixed = mixed.astype(BF).reshape(total, width)

    def back(grad_mixed):
        grad = as_heads(grad_mixed)
        grad_probs = jnp.einsum("qhd,khd->hqk", grad, value_all, preferred_element_type=F32)
        delta = jnp.sum(probs * grad_probs, axis=-1, keepdims=True)
        grad_scores = (probs * (grad_probs - delta)).astype(BF)
        grad_queries = jnp.einsum("hqk,khd->qhd", grad_scores, key_all, preferred_element_type=F32)
        grad_keys = jnp.einsum("hqk,qhd->khd", grad_scores, queries, preferred_element_type=F32)
        grad_values = jnp.einsum("hqk,qhd->khd", probs.astype(BF), grad, preferred_element_type=F32)
        grad_keys, grad_values = [
            lax.psum_scatter(
                g.astype(BF), "ctx", scatter_dimension=0, tiled=True, axis_index_groups=groups
            ).astype(F32)
            for g in (grad_keys * factor, grad_values)
        ]
        turned = [
            rotate(g, cosine, -sine).reshape(total, width) * gains[p]
            for p, g in enumerate((grad_queries * factor, grad_keys))
        ]
        inner = jnp.stack([jnp.sum(turned[p] * pre[p], axis=-1) for p in range(2)])
        inner = jnp.repeat(inner, 8, axis=0)
        values = grad_values.reshape(total, width).astype(BF)
        return turned[0].astype(BF), turned[1].astype(BF), values, inner

    return mixed, back


def choose_body(place, wide, down, model, hidden, gains, wide_out, down_out, model_out, hidden_out, small, sems):
    at = place[0]
    sources = [(wide.at[:, at], wide_out), (down.at[at], down_out)]
    sources += [(model.at[:, at], model_out), (hidden.at[:, at], hidden_out)]
    run_copies([pltpu.make_async_copy(source, to, sems.at[i]) for i, (source, to) in enumerate(sources)])
    rank, width = wide_out.shape[1:]
    shared = [wide_out[p] for p in (0, 1, 2, 4, 5)] + [model_out[p] for p in (3, 4)]
    last = jnp.concatenate([gains[2:], jnp.zeros((rank - 2, width), BF)])
    for at, value in enumerate([*shared, last]):
        column = at // 2 * width
        small[at % 2 * rank : (at % 2 + 1) * rank, column : column + width] = value


def choose(place, a_wide, a_down, b_model, b_hidden, gains):
    rank, width = a_wide.shape[2:]
    shapes = [a_wide.shape[:1] + a_wide.shape[2:], a_down.shape[1:]]
    shapes += [b_model.shape[:1] + b_model.shape[2:], b_hidden.shape[:1] + b_hidden.shape[2:]]
    shapes.append((2 * rank, 4 * width))
    outs = [shape_of(s, BF) for s in shapes]
    return call(
        choose_body,
        (1,),
        [a_wide, a_down, b_model, b_hidden, gains],
        [HBM] * 4 + [whole(gains)],
        [(o, whole(o)) for o in outs],
        [pltpu.SemaphoreType.DMA((4,))],
        scalars=[place],
    )


def place_body(rank, count, unused, plan, at, *refs):
    sources, outs = refs[:count], refs[count + unused :]
    for out, maps in zip(outs, plan):
        for n in range(out.shape[1]):
            for p, pieces in enumerate(maps):
                begin = 0
                for source, place in pieces:
                    value = sources[source][at[n], place * rank : (place + 1) * rank].astype(F32)
                    out[p, n, :, begin : begin + value.shape[-1]] = value
                    begin += value.shape[-1]


def on_device(
    tokens,
    cotangent,
    adapter_index,
    w_attn,
    w_gate_up,
    w_down,
    gains,
    a_wide,
    a_down,
    b_model,
    b_hidden,
):
    seqs, rows = tokens.shape[0], tokens.shape[1]
    shards, ctxs = lax.axis_size("shard"), lax.axis_size("ctx")
    shard, ctx = lax.axis_index("shard"), lax.axis_index("ctx")
    batch = seqs * shards
    per_sequence = ctxs // batch
    group_rows = batch * rows
    chunks = seqs
    chunk_rows = shards * rows
    wide = HEADS // shards * HD
    adapters, rank = a_down.shape[:2]

    groups = [[group_of(q, k, per_sequence, ctxs) for k in range(per_sequence)] for q in range(batch)]
    my_sequence, my_part = sequence_of(ctx, per_sequence, ctxs)
    my_slot = my_sequence % seqs
    my_spot = (ctx % batch) // shards

    pairs = []
    for p in range(seqs):
        pairs.append([])
        for c in range(ctxs):
            for s in range(shards):
                k, local = c // batch, c % batch
                spot, owner = local // shards, local % shards
                to = groups[seqs * s + (p + spot) % seqs][k]
                pairs[p].append((c * shards + s, to * shards + owner))

    windows = Windows()
    side_by_side = windows.side_by_side

    def is_place(index):
        return [index % seqs == at for at in range(1, seqs)]

    flags = {
        "cut": [((p + my_spot) % seqs).astype(jnp.uint32) for p in range(seqs)],
        "chunk": [is_place(my_slot - h) for h in range(seqs)],
        "return": [is_place(my_slot - p) for p in range(seqs)],
        "order": [is_place(j - my_spot) for j in range(seqs)],
        "columns": [((shard ^ flip) * wide).astype(jnp.uint32) for flip in FLIPS],
        "places": jnp.stack([shard, ctx % 4]).astype(jnp.int32),
        "turn": [((my_slot - p) % seqs)[None].astype(jnp.int32) for p in range(seqs)],
    }

    def pick(parts, is_it):
        value = parts[0]
        for part, flag in zip(parts[1:], is_it):
            value = jnp.where(flag, part, value)
        return value

    def cut_rows(*values):
        return [
            jnp.concatenate(
                [
                    lax.dynamic_index_in_dim(value, flags["cut"][p], 0, keepdims=False)
                    for value in values
                ]
            )
            for p in range(seqs)
        ]

    def send_row(p):
        return lambda cut: lax.ppermute(cut, ("ctx", "shard"), pairs[p])

    def chunk_order(got):
        return [pick(got, flags["chunk"][h]) for h in range(seqs)]

    def return_cuts(parts):
        return [pick(parts, flags["return"][p]) for p in range(seqs)]

    def return_row(p):
        return lambda cut: lax.ppermute(cut, ("ctx", "shard"), [(b, a) for a, b in pairs[p]])

    def return_order(got):
        return jnp.stack([pick(got, flags["order"][j]) for j in range(seqs)])

    def core(value):
        return over_shard(value, 1)

    def chip(value):
        return over_shard(value, 2)

    def across(value):
        return over_shard(value, 3)

    def by_x(value):
        return over_ctx(value, 1)

    def by_z(value):
        return over_ctx(value, 2)

    def to_all(value):
        return [(functools.partial(over_shard, flip=flip), value) for flip in FLIPS[1:]]

    index_own = adapter_index[:, 0]
    (qkv_near, qkv_far, qkv_cross, flags), index_got = side_by_side(
        lambda x: (*cut(x[0], 0, 3, x[1]["places"], False), x[1]), [w_attn, flags], to_all(index_own)
    )
    places = flags["places"]
    index_all = jnp.concatenate(natural([index_own, *index_got], shard))
    sequence_with = jnp.sum(
        jnp.where(
            index_all[None, :] == jnp.arange(adapters, dtype=jnp.int32)[:, None],
            jnp.arange(batch, dtype=jnp.int32)[None, :],
            0,
        ),
        axis=1,
    )
    table = jnp.array(groups, jnp.int32)
    if per_sequence > 1:
        where = sequence_with
    else:
        group_with = jnp.sum(
            jnp.where(
                sequence_with[:, None] == jnp.arange(batch, dtype=jnp.int32)[None, :], table[:, 0][None, :], 0
            ),
            axis=1,
        )
        where = gathered_place(ctx, group_with)
    row_cuts = cut_rows(tokens)

    def rope_tables(place):
        shape = (chunks, shards, rows, HD)
        spot, turn, row, lane = [lax.broadcasted_iota(jnp.int32, shape, axis) for axis in range(4)]
        owner = place ^ (turn // 2 + turn % 2 * 2)
        position = my_part * group_rows + (spot * shards + owner) * rows + row
        freqs = jnp.exp((lane % (HD // 2)).astype(F32) * (-2.0 * math.log(rope_base) / HD))
        angles = position.astype(F32) * freqs
        sine = jnp.sin(angles) * jnp.where(lane < HD // 2, -1.0, 1.0)
        return position[..., 0].reshape(-1), jnp.cos(angles).reshape(-1, HD), sine.reshape(-1, HD)

    def prepare(x):
        chosen = choose(x[0], a_wide, a_down, b_model, b_hidden, gains)
        return chosen, cut(x[1], 0, 2, x[2], True), x[3], rope_tables(x[2][0])

    (chosen, gate_up_cuts, where, (positions, cosine, sine)), [qkv_a, qkv_b, *row_got, qkv_near] = side_by_side(
        prepare,
        [index_all[my_sequence][None], w_gate_up, places, where],
        [
            (chip, qkv_far),
            (across, qkv_cross),
            (send_row(0), row_cuts[0]),
            (send_row(1), row_cuts[1]),
            (core, qkv_near),
        ],
    )
    own_wide, own_down, own_model, own_hidden, small = chosen
    near, gate_far, gate_cross, up_far, up_cross = gate_up_cuts

    token_rows = chunk_order(row_got)
    token_own = jnp.concatenate([*token_rows, small])
    held = {}

    def load_out(weight):
        held["out"], done = load_plain(weight)
        return done

    done, [qkv_xa, qkv_xb, qkv_za, qkv_zb, token_far] = side_by_side(
        load_out,
        w_attn,
        [(by_x, qkv_a), (by_x, qkv_b), (by_z, qkv_a), (by_z, qkv_b), (chip, token_own)],
    )
    windows.carried.append(done)
    _, [last_a, last_b, token_near, gate_a] = side_by_side(
        None,
        None,
        [
            (by_x, qkv_za),
            (by_z, qkv_xb),
            (core, jnp.stack([token_own, token_far])),
            (chip, gate_far),
        ],
    )
    w_qkv = [qkv_near, qkv_a, qkv_b, qkv_xa, qkv_xb, qkv_za, qkv_zb, last_a, last_b]
    token_parts = [token_own, token_far, token_near]
    small_parts = [part[..., seqs * rows :, :] for part in token_parts]
    small_parts = [small_parts[0], small_parts[1], small_parts[2][0], small_parts[2][1]]
    small_all = jnp.concatenate(
        natural(
            [
                jnp.concatenate([part[:, at * wide : (at + 1) * wide] for at in range(4)])
                for part in small_parts
            ],
            shard,
        ),
        axis=1,
    )
    qkv_downs = small_all[: 3 * rank]
    gate_downs = small_all[3 * rank : 5 * rank]
    out_up = small_all[5 * rank : 6 * rank]
    feed_up = small_all[6 * rank : 7 * rank]
    attn_gain = small_all[7 * rank : 7 * rank + 1].astype(F32)
    feed_gain = small_all[7 * rank + 1 : 7 * rank + 2].astype(F32)
    head_gains = gains[:2].astype(F32)

    (pre, qkv_low, squares, qkv_held), [gate_b, gate_xa, gate_za, near] = side_by_side(
        lambda x: qkv_forward(x, chunks, rows, w_attn, w_qkv, places, qkv_downs, own_model),
        token_parts,
        [(across, gate_cross), (by_x, gate_a), (by_z, gate_a), (core, near)],
    )

    def from_all(sums, others):
        _, got = side_by_side(None, None, to_all(sums) + others)
        return [sums, *got[:3]], got[3:]

    squares, _ = from_all(squares[:16], [])
    simple = per_sequence == 1 and chunk_rows == BLOCK
    attention_sends = [(chip, up_far), (by_x, gate_b), (by_z, gate_b)]
    if simple:
        (queries, key_rows, mixed, logs), got = side_by_side(
            lambda x: attention_forward(x[0], x[1], x[2], x[3], head_gains, chunks),
            [pre, squares, cosine, sine],
            attention_sends,
        )
    else:
        mixed, attention_grads = wide_attention(
            pre, squares, cosine, sine, head_gains, chunks, positions, groups
        )
        got = [send(value) for send, value in attention_sends]
    up_a, gate_xb, gate_zb = got

    every = range(chunks)
    assert chunks == 2
    def far_sum(keep, near):
        return by_rows(far_body, [keep, near], [BF])[0]

    def project_out(x, h):
        return partial_forward(x, h, chunks, held["out"], own_wide[3], out_up, False)

    def attention_rows(h, keep, near, got):
        return by_rows(attention_rows_body, [keep, near, got, token_rows[h], attn_gain], [F32, F32, BF])

    def feed_rows(h, keep, near, got):
        return by_rows(feed_rows_body, [keep, near, got, resid[h], cot[h], feed_gain], [BF, BF])

    def back_rows(h, keep, near, got):
        return by_rows(back_rows_body, [keep, near, got, attn_pre[h], cot[h], attn_gain], [F32, BF])

    def up_gate(parts):
        return gate_up_forward(parts, gate_up_held, gate_downs, own_hidden)

    def down(act):
        return partial_forward(act, 0, 1, w_down, own_down, feed_up, True, [gate_up_held])

    def back_down(h, parts):
        return feed_back(
            parts, w_down, own_down, hidden[h][0], hidden[h][1], hidden[h][3], feed_parts[h][2], feed_up, own_hidden, gate_up_held
        )

    def back_up_gate(h, gate_grad, upper_grad):
        return gate_up_back(
            gate_grad, upper_grad, gate_up_held, hidden_grads[h][2], gate_downs, resid_parts[h]
        )

    def back_out(h, parts):
        return out_back(parts, held["out"], own_wide[3], out_up, mixed, out_parts[h][2], h)

    none = [None] * PARTS

    def load_first(x):
        gate = [*x, None, None]
        held["gate_up"], done = load([gate, none], places, w_gate_up, near)
        return done

    def load_more(x):
        gate = none[:6] + x[:2]
        up = [*x[2:], None, None]
        held["gate_up"], done = load([gate, up], places, held=held["gate_up"])
        return done

    def load_last(x):
        held["gate_up"], done = load([none, none[:6] + x], places, held=held["gate_up"])
        return done

    attn_pre, resid, resid_low = [None] * 2, [None] * 2, [None] * 2
    resid_parts, hidden, feed_parts, output = [None] * 2, [None] * 2, [None] * 2, [None] * 2
    hidden_grads, resid_grads, grad_resid, out_grads = [None] * 2, [None] * 2, [None] * 2, [None] * 2
    out_parts, [up_b, up_xa, up_za] = side_by_side(
        lambda x: [project_out(x, h) for h in every], mixed, [(across, up_cross), (by_x, up_a), (by_z, up_a)]
    )
    _, [core0, core1] = side_by_side(None, None, [(core, out_parts[0][1]), (core, out_parts[1][1])])
    far0, far1 = far_sum(out_parts[0][0], core0), far_sum(out_parts[1][0], core1)
    done, [got0, got1, gate_last_a, gate_last_b] = side_by_side(
        load_first,
        [gate_a, gate_b, gate_xa, gate_xb, gate_za, gate_zb],
        [(chip, far0), (chip, far1), (by_x, gate_za), (by_z, gate_xb)],
    )
    windows.carried.append(done)
    attn_pre[0], resid[0], resid_low[0] = attention_rows(0, out_parts[0][0], core0, got0)
    attn_pre[1], resid[1], resid_low[1] = attention_rows(1, out_parts[1][0], core1, got1)
    _, [far0, near0, up_xb, up_zb] = side_by_side(
        None, None, [(chip, resid_low[0]), (core, resid_low[0]), (by_x, up_b), (by_z, up_b)]
    )
    done, [cross0, far1, near1, up_last_a, up_last_b] = side_by_side(
        load_more,
        [gate_last_a, gate_last_b, up_a, up_b, up_xa, up_xb, up_za, up_zb],
        [(core, far0), (chip, resid_low[1]), (core, resid_low[1]), (by_x, up_za), (by_z, up_xb)],
    )
    windows.carried.append(done)
    resid_parts[0] = [resid_low[0], far0, near0, cross0]
    done, [cross1] = side_by_side(load_last, [up_last_a, up_last_b], [(core, far1)])
    windows.carried.append(done)
    gate_up_held = held["gate_up"]
    resid_parts[1] = [resid_low[1], far1, near1, cross1]

    cot_cuts = cut_rows(cotangent)
    hidden[0], [cot0] = side_by_side(up_gate, resid_parts[0], [(send_row(0), cot_cuts[0])])
    feed_parts[0], _ = side_by_side(down, hidden[0][2], [])
    _, [core0] = side_by_side(None, None, [(core, feed_parts[0][1])])
    hidden[1], [got, cot1] = side_by_side(
        up_gate, resid_parts[1], [(chip, far_sum(feed_parts[0][0], core0)), (send_row(1), cot_cuts[1])]
    )
    cot = chunk_order([cot0, cot1])
    output[0], grad0 = feed_rows(0, feed_parts[0][0], core0, got)
    feed_parts[1], [far, near] = side_by_side(down, hidden[1][2], [(chip, grad0), (core, grad0)])
    _, [cross, core1] = side_by_side(None, None, [(core, far), (core, feed_parts[1][1])])
    hidden_grads[0], [got] = side_by_side(
        lambda x: back_down(0, x), [grad0, far, near, cross], [(chip, far_sum(feed_parts[1][0], core1))]
    )
    output[1], grad1 = feed_rows(1, feed_parts[1][0], core1, got)
    output = return_cuts(output)
    resid_grads[0], [far, near, output0] = side_by_side(
        lambda x: back_up_gate(0, *x),
        hidden_grads[0][:2],
        [(chip, grad1), (core, grad1), (return_row(0), output[0])],
    )
    _, [cross, core0] = side_by_side(None, None, [(core, far), (core, resid_grads[0][1])])
    hidden_grads[1], [got, output1] = side_by_side(
        lambda x: back_down(1, x),
        [grad1, far, near, cross],
        [(chip, far_sum(resid_grads[0][0], core0)), (return_row(1), output[1])],
    )
    output = return_order([output0, output1])
    grad_resid[0], grad0 = back_rows(0, resid_grads[0][0], core0, got)

    broad = jnp.concatenate(
        [sum(g[3] for g in hidden_grads), sum(g[5] for g in hidden_grads).reshape(2 * rank, -1)]
    ).astype(BF)
    broad = [x[None] for x in jnp.split(broad, 2, axis=1)]
    step0, step1, step2 = [ctx_step(at) for at in range(3)]

    def grown(value, got):
        return jnp.concatenate([value, got])

    resid_grads[1], [far, near, *got] = side_by_side(
        lambda x: back_up_gate(1, *x),
        hidden_grads[1][:2],
        [(chip, grad0), (core, grad0), (step0, broad[0]), (step0, broad[1])],
    )
    broad = [grown(*pair) for pair in zip(broad, got)]
    own_early, far_early, cuts = column_cuts(
        jnp.concatenate([sum(g[4] for g in hidden_grads), sum(g[2] for g in resid_grads)]), flags["columns"]
    )
    _, [cross, core1, got_early] = side_by_side(
        None, None, [(core, far), (core, resid_grads[1][1]), (core, cuts)]
    )
    own_early = own_early + got_early[0].astype(F32)
    far_early = (far_early + got_early[1].astype(F32)).astype(BF)
    out_grads[0], [got1, got_early, got] = side_by_side(
        lambda x: back_out(0, x),
        [grad0, far, near, cross],
        [(chip, far_sum(resid_grads[1][0], core1)), (chip, far_early), (step1, broad[0])],
    )
    broad[0] = grown(broad[0], got)
    early = (own_early + got_early.astype(F32)).astype(BF)[None]
    grad_resid[1], grad1 = back_rows(1, resid_grads[1][0], core1, got1)
    _, [far, near, got, got_early] = side_by_side(
        None, None, [(chip, grad1), (core, grad1), (step2, broad[0]), (step0, early)]
    )
    broad[0] = grown(broad[0], got)
    early = grown(early, got_early)
    _, [cross] = side_by_side(None, None, [(core, far)])
    out_grads[1] = back_out(1, [grad1, far, near, cross])
    grad_mixed = jnp.concatenate([g[0] for g in out_grads])

    attention_sends = [(step1, broad[1])]
    if simple:
        (query_turned, key_turned, grad_values, inner), [got] = side_by_side(
            lambda x: attention_back(
                queries, key_rows, pre, x, logs, cosine, sine, head_gains, chunks
            ),
            grad_mixed,
            attention_sends,
        )
    else:
        query_turned, key_turned, grad_values, inner = attention_grads(grad_mixed)
        [got] = [send(value) for send, value in attention_sends]
    broad[1] = grown(broad[1], got)
    inners, [got] = from_all(inner, [(step1, early)])
    early = grown(early, got)
    (grads, lows, down_late, up_late), [got] = side_by_side(
        lambda x: qkv_grads(x[:2], x[2], pre, squares, x[3:], token_parts, qkv_low, own_model, chunks),
        [query_turned, key_turned, grad_values, *inners],
        [(step2, early)],
    )
    early = grown(early, got)
    partial = jnp.concatenate([down_late, sum(g[2] for g in out_grads)])
    cuts = [lax.dynamic_slice(partial, (jnp.uint32(0), start), (partial.shape[0], wide)) for start in flags["columns"]]

    def rest_of(value):
        for at in range(3, len(ctx_flips())):
            value = grown(value, ctx_step(at)(value))
        if per_sequence > 1:
            value = jnp.sum(value.astype(F32)[gathered_place(ctx, table)], axis=1)
        return value

    def placed(sources, counts, plan, carried=()):
        width = sum(sources[piece[0]].shape[-1] for piece in plan[0][0])
        outs = [shape_of((count, adapters, rank, width), F32) for count in counts]
        return call(
            functools.partial(place_body, rank, len(sources), len(carried), plan),
            (1,),
            [*sources, *carried],
            [whole(x) for x in (*sources, *carried)],
            [(o, whole(o)) for o in outs],
            scalars=[where],
        )

    def back_qkv(x, p):
        return qkv_back(x, lows, qkv_held, qkv_downs, chunks, flags["turn"][p])

    def input_rows(p, keep, near, got):
        return by_rows(input_rows_body, [keep, near, got, *grad_resid], [BF], [flags["turn"][p]])[0]

    def place_broad(x):
        return placed([rest_of(value) for value in x], (1, 2), ((((0, 0), (1, 0)),), (((0, 1), (1, 1)), ((0, 2), (1, 2)))))

    parts0, got = side_by_side(
        lambda x: back_qkv(x, 0),
        grads,
        [(send, piece.astype(BF)) for send, piece in zip((chip, core, across), cuts[1:])],
    )
    late = jnp.concatenate(
        [
            cuts[0] + sum(piece.astype(F32) for piece in got),
            up_late.reshape(3 * rank, -1),
            sum(g[1] for g in out_grads),
        ]
    ).astype(BF)[None]
    parts1, [core0, got_late] = side_by_side(
        lambda x: back_qkv(x, 1), grads, [(core, parts0[1]), (step0, late)]
    )
    late = grown(late, got_late)
    _, [got0, core1, got_late, got] = side_by_side(
        None,
        None,
        [(chip, far_sum(parts0[0], core0)), (core, parts1[1]), (step1, late), (step2, broad[1])],
    )
    broad[1] = grown(broad[1], got)
    late = grown(late, got_late)
    (grad_down, grad_hidden), [got1, input0, got_late] = side_by_side(
        place_broad,
        broad,
        [
            (chip, far_sum(parts1[0], core1)),
            (return_row(0), input_rows(0, parts0[0], core0, got0)),
            (step2, late),
        ],
    )
    late = rest_of(grown(late, got_late))
    early = rest_of(early)
    def place_late(x):
        return placed(
            x,
            (6, 5),
            (
                (((1, 0),), ((1, 1),), ((1, 2),), ((1, 7),), ((0, 1),), ((0, 2),)),
                (((1, 4),), ((1, 5),), ((1, 6),), ((1, 3),), ((0, 0),)),
            ),
            windows.carried,
        )

    (grad_wide, grad_model), [input1] = side_by_side(
        place_late, [early, late], [(return_row(1), input_rows(1, parts1[0], core1, got1))]
    )
    input_grad = return_order([input0, input1]).astype(F32)
    return (output, input_grad, grad_wide, grad_down[0], grad_model, grad_hidden)


def solution(mesh):
    return jax.shard_map(
        on_device,
        mesh=mesh,
        in_specs=(
            P("shard", "ctx", None),
            P("shard", "ctx", None),
            P("shard", None),
            P(None, "shard", None),
            P(None, "shard", None),
            P("shard", None),
            P(None, "shard"),
            P(None, None, None, "shard"),
            P(None, None, "shard"),
            P(None, None, None, "shard"),
            P(None, None, None, "shard"),
        ),
        out_specs=(
            P("shard", "ctx", None),
            P("shard", "ctx", None),
            P(None, None, None, "shard"),
            P(None, None, "shard"),
            P(None, None, None, "shard"),
            P(None, None, None, "shard"),
        ),
        check_vma=False,
    )
```

```python
import functools
import math

import jax
import jax.numpy as jnp
from jax import lax
from jax.experimental import pallas as pl
from jax.experimental.pallas import tpu as pltpu
from jax.sharding import PartitionSpec as P

D = 2048
HEADS = 16
HD = 128
BLOCK = 256

epsilon = 1e-06
rope_base = 500000.0
far_below = -1e30
BF = jnp.bfloat16
F32 = jnp.float32
VMEM_BYTES = 16 * 2**20


def dot(left, right):
    return lax.dot_general(left, right, (((1,), (0,)), ((), ())), preferred_element_type=F32)


def dot_nt(left, right):
    return lax.dot_general(left, right, (((1,), (1,)), ((), ())), preferred_element_type=F32)


def dot_tn(left, right):
    return lax.dot_general(left, right, (((0,), (0,)), ((), ())), preferred_element_type=F32)


def over_shard(value, flip):
    size = lax.axis_size("shard")
    return lax.ppermute(value, "shard", [(i, i ^ flip) for i in range(size)])


class Windows:
    def __init__(self):
        self.carried = []

    def side_by_side(self, run, inputs, sends):
        values = [value for _, value in sends]
        inputs, values, self.carried = lax.optimization_barrier((inputs, values, self.carried))
        got = [send(value) for (send, _), value in zip(sends, values)]
        out = run(inputs) if run else None
        out, got, self.carried = lax.optimization_barrier((out, got, self.carried))
        return out, got


def over_ctx(value, flip):
    size = lax.axis_size("ctx")
    return lax.ppermute(value, "ctx", [(i, i ^ flip) for i in range(size)])


FLIPS = (0, 2, 1, 3)


def call(body, grid, args, in_specs, outs, scratch=(), scalars=(), flops=0, aliases={}):
    placed = []
    for arg, spec in zip(args, in_specs):
        if spec.memory_space == pltpu.VMEM:
            arg = pltpu.with_memory_space_constraint(arg, pltpu.VMEM)
        elif spec.memory_space == pltpu.HBM:
            arg = pltpu.with_memory_space_constraint(arg, pltpu.HBM)
        placed.append(arg)
    return pl.pallas_call(
        body,
        grid_spec=pltpu.PrefetchScalarGridSpec(
            num_scalar_prefetch=len(scalars),
            grid=grid,
            in_specs=in_specs,
            out_specs=[spec for _, spec in outs],
            scratch_shapes=scratch,
        ),
        out_shape=[shape for shape, _ in outs],
        input_output_aliases=aliases,
        compiler_params=pltpu.CompilerParams(vmem_limit_bytes=VMEM_BYTES),
        cost_estimate=pl.CostEstimate(flops=flops, bytes_accessed=0, transcendentals=0),
    )(*scalars, *placed)


def shape_of(shape, kind):
    return jax.ShapeDtypeStruct(shape, kind)


def whole(value):
    zeros = (0,) * value.ndim
    return pl.BlockSpec(value.shape, lambda *_: zeros)


def spec(block, index):
    return pl.BlockSpec(block, lambda i, *_: index(i))


def column_spec(value, tile):
    zeros = (0,) * (value.ndim - 1)
    return pl.BlockSpec(value.shape[:-1] + (tile,), lambda i, *_: (*zeros, i))


HBM = pl.BlockSpec(memory_space=pltpu.HBM)
ANY = pl.BlockSpec(memory_space=pl.ANY)
VMEM = pl.BlockSpec(memory_space=pltpu.VMEM)


def tile_of(width):
    return min(1024, width)


def run_copies(copies):
    for copy in copies:
        copy.start()
    for copy in copies:
        copy.wait()


def cut_body(first, apart, places, weight, near, *refs):
    fars, sems = refs[:-1], refs[-1]
    step = pl.program_id(0)
    width = near.shape[2]
    slim = fars[0].shape[1]
    rows = pl.ds(pl.multiple_of(places[1] * slim, slim), slim)

    def columns(flip):
        return pl.ds(pl.multiple_of((places[0] ^ flip) * width, width), width)

    def copies(far, cross):
        sources = [(slice(None), columns(1), near), (rows, columns(2), far), (rows, columns(3), cross)]
        return [
            pltpu.make_async_copy(weight.at[first + step, r, c], to.at[0], sems.at[i])
            for i, (r, c, to) in enumerate(sources)
        ]

    if apart:
        for matrix in range(len(fars) // 2):
            pair = fars[2 * matrix : 2 * matrix + 2]
            pl.when(step == matrix)(functools.partial(lambda pair: run_copies(copies(*pair)), pair))
    else:
        run_copies(copies(*fars))


def cut(weight, first, count, places, apart):
    depth, full = weight.shape[1:]
    width, slim = full // 4, depth // 4
    if apart:
        far = (shape_of((1, slim, width), BF), pl.BlockSpec((1, slim, width), lambda *_: (0, 0, 0)))
    else:
        far = (shape_of((count, slim, width), BF), pl.BlockSpec((1, slim, width), lambda m, _: (m, 0, 0)))
    return call(
        functools.partial(cut_body, first, apart),
        (count,),
        [weight],
        [HBM],
        [(shape_of((count, depth, width), BF), pl.BlockSpec((1, depth, width), lambda m, _: (m, 0, 0)))]
        + [far] * (2 * count if apart else 2),
        [pltpu.SemaphoreType.DMA((3,))],
        scalars=[places],
    )


COPIES = 10
PARTS = 8


def copies_of(weight, matrix, near, near_at, parts, at, places, held, sems):
    width = held.shape[1]
    depth = held.shape[0] // 4
    slim = depth // 4
    shard, quarter = places[0], places[1]

    def to(flip, rows, begin=0):
        start = pl.multiple_of((shard ^ flip) * depth + begin, slim)
        return held.at[pl.ds(start, rows), :]

    pairs = []
    if weight is not None:
        own_columns = pl.ds(pl.multiple_of(shard * width, width), width)
        pairs.append((weight.at[matrix, :, own_columns], to(0, depth)))
    if near is not None:
        pairs.append((near.at[near_at], to(1, depth)))
    for i, part in enumerate(parts):
        if part is not None:
            pairs.append((part.at[at], to(2 + i % 2, slim, (quarter ^ (i // 2)) * slim)))
    return [pltpu.make_async_copy(source, target, sems.at[i]) for i, (source, target) in enumerate(pairs)]


DONE = (shape_of((8, 128), F32), pl.BlockSpec((8, 128), lambda *_: (0, 0)))


def load_plain_body(attn, down, out_held, down_held, done, sems):
    run_copies(
        [
            pltpu.make_async_copy(attn.at[attn.shape[0] - 1], out_held, sems.at[0]),
            pltpu.make_async_copy(down, down_held, sems.at[1]),
        ]
    )
    done[...] = jnp.zeros_like(done)


def load_plain(w_attn, w_down):
    return call(
        load_plain_body,
        (1,),
        [w_attn, w_down],
        [HBM] * 2,
        [(pltpu.VMEM(w_attn.shape[1:], BF), VMEM), (pltpu.VMEM(w_down.shape, BF), VMEM), DONE],
        [pltpu.SemaphoreType.DMA((2,))],
    )


def load_body(first, there, places, *refs):
    refs = list(refs)
    weight, near = (refs.pop(0), refs.pop(0)) if first else (None, None)
    parts = [[refs.pop(0) if is_there else None for is_there in matrix] for matrix in there]
    held, done, sems = refs[-3:]
    copies = []
    for m, matrix_parts in enumerate(parts):
        copies += copies_of(weight, m, near, m, matrix_parts, 0, places, held.at[m], sems.at[m])
    run_copies(copies)
    done[...] = jnp.zeros_like(done)


def load(parts, places, weight=None, near=None, held=None):
    there = [[part is not None for part in matrix] for matrix in parts]
    arrays = [part for matrix in parts for part in matrix if part is not None]
    arrays = ([weight, near] if held is None else []) + arrays
    depth, full = (weight if held is None else held).shape[1:]
    shape = (2, 4 * depth, full // 4) if held is None else held.shape
    return call(
        functools.partial(load_body, held is None, there),
        (1,),
        arrays + ([] if held is None else [held]),
        ([HBM] + [ANY] * (len(arrays) - 1) if held is None else [ANY] * len(arrays) + [VMEM]),
        [(pltpu.VMEM(shape, BF), VMEM), DONE],
        [pltpu.SemaphoreType.DMA((2, COPIES))],
        [places],
        aliases={} if held is None else {1 + len(arrays): 0},
    )


def row_of(column):
    return jnp.transpose(jnp.broadcast_to(column, (column.shape[0], 128)))[:8]


def column_of(row):
    return jnp.transpose(jnp.broadcast_to(row[:1], (128, row.shape[1])))[:, :1]


def qkv_body(chunks, size, places, *refs):
    x_refs, refs = refs[:3], refs[3:]
    weight, near, weight_parts, refs = refs[0], refs[1], refs[2 : 2 + PARTS], refs[2 + PARTS :]
    down, up, pre, low, sums, kept, held, rows, sems, keep_sems = refs
    step = pl.program_id(0)

    def copies(p):
        return copies_of(weight, p, near, p, weight_parts, p, places, held.at[p], sems.at[p])

    @pl.when(step == 0)
    def _():
        for p in range(held.shape[0]):
            for copy in copies(p):
                copy.start()
        for h in range(chunks):
            rows[4 * h * size : 4 * (h + 1) * size] = load_parts(x_refs, h * size, size)

    lowrank = dot_nt(rows[...], down[...]).astype(BF)
    for copy in copies(step):
        copy.wait()
    keep = [pltpu.make_async_copy(held.at[p], kept.at[p], keep_sems.at[p]) for p in range(held.shape[0])]
    for p, copy in enumerate(keep):
        pl.when(step == p)(copy.start)
    value = dot(rows[...], held[step]) + dot(lowrank, up[0])
    pre[0] = value.astype(BF)
    low[0] = lowrank
    sums[...] = row_of(jnp.sum(value * value, axis=1, keepdims=True))

    @pl.when(step == held.shape[0] - 1)
    def _():
        for copy in keep:
            copy.wait()


def qkv_forward(x_parts, chunks, size, weight, weight_parts, places, downs, ups):
    count, depth, width = weight_parts[0].shape
    full = x_parts[0].shape[1]
    total, rank = 4 * chunks * size, ups.shape[1]
    return call(
        functools.partial(qkv_body, chunks, size),
        (count,),
        [*x_parts, weight, *weight_parts, downs, ups],
        [whole(x) for x in x_parts]
        + [HBM] * (2 + PARTS)
        + [
            spec((rank, full), lambda p: (p, 0)),
            spec((1, rank, width), lambda p: (p, 0, 0)),
        ],
        [
            (shape_of((count, total, width), BF), spec((1, total, width), lambda p: (p, 0, 0))),
            (shape_of((count, total, rank), BF), spec((1, total, rank), lambda p: (p, 0, 0))),
            (shape_of((8 * count, total), F32), spec((8, total), lambda p: (p, 0))),
            (pltpu.HBM((count, full, width), BF), HBM),
        ],
        [
            pltpu.VMEM((count, full, width), BF),
            pltpu.VMEM((total, full), BF),
            pltpu.SemaphoreType.DMA((count, COPIES)),
            pltpu.SemaphoreType.DMA((count,)),
        ],
        [places],
        flops=2 * total * full * width * count,
    )


def aligned_sums(refs, which, chunks):
    total = refs[0].shape[1]
    block = total // (4 * chunks)
    out = 0.0
    for flip, ref in zip(FLIPS, refs):
        column = column_of(ref[8 * which : 8 * which + 8])
        if flip:
            order = [FLIPS.index(f ^ flip) for f in FLIPS]
            column = jnp.concatenate(
                [
                    column[(4 * h + i) * block : (4 * h + i + 1) * block]
                    for h in range(chunks)
                    for i in order
                ]
            )
        out = out + column
    return out


def attention_body(chunks, factor, *refs):
    (
        query_pre, key_pre, value, own, far, near, cross, cosine, sine, gains,
        query_out, key_out, mixed_out, logs_out, scale_rows,
    ) = refs
    total = query_pre.shape[1]
    size = total // chunks

    @pl.when(pl.program_id(0) == 0)
    def _():
        for p in range(2):
            sums = aligned_sums((own, far, near, cross), p, chunks)
            scale_rows[p] = jnp.broadcast_to(lax.rsqrt(sums / D + epsilon), (total, HD))

    def prepared(pre, p):
        value = pre[0].astype(F32) * scale_rows[p] * gains[p : p + 1]
        return (value * cosine[...] + pltpu.roll(value, HD // 2, 1) * sine[...]).astype(BF)

    query, key = prepared(query_pre, 0), prepared(key_pre, 1)
    query_out[...] = query
    key_out[...] = key
    logs = []
    for h in range(chunks):
        seen = (h + 1) * size
        scores = dot_nt(query[h * size : (h + 1) * size], key[:seen]) * factor
        top = jnp.max(scores, axis=1, keepdims=True)
        weights = jnp.exp(scores - top)
        sums = jnp.sum(weights, axis=1, keepdims=True)
        probs = (weights * (1.0 / sums)).astype(BF)
        mixed_out[h * size : (h + 1) * size] = dot(probs, value[0, :seen]).astype(BF)
        logs.append(top + jnp.log(sums))
    logs_out[...] = row_of(jnp.concatenate(logs))


def attention_forward(pre, sums, cosine, sine, gains, chunks):
    _, total, width = pre.shape
    heads = width // HD
    factor = 1.0 / math.sqrt(HD)

    def head(p):
        return spec((1, total, HD), lambda i: (p, 0, i))

    by_head = spec((total, HD), lambda i: (0, i))
    return call(
        functools.partial(attention_body, chunks, factor),
        (heads,),
        [pre, pre, pre, *sums, cosine, sine, gains],
        [head(0), head(1), head(2)]
        + [whole(s) for s in sums]
        + [whole(cosine), whole(sine), spec((gains.shape[0], HD), lambda i: (0, i))],
        [
            (shape_of((total, width), BF), by_head),
            (shape_of((total, width), BF), by_head),
            (shape_of((total, width), BF), by_head),
            (shape_of((8 * heads, total), F32), spec((8, total), lambda i: (i, 0))),
        ],
        [pltpu.VMEM((2, total, HD), F32)],
        flops=4 * total * total * width,
    )


def attention_back_body(chunks, factor, *refs):
    (
        query_in, key_in, query_pre, key_pre, value, grad_in, logs, cosine, sine, gains,
        query_out, key_out, value_out, inner_out, inner_rows,
    ) = refs
    total = query_in.shape[0]
    size = total // chunks
    head = pl.program_id(0)
    query, key, values, grad = query_in[...], key_in[...], value[0], grad_in[...]
    log_column = column_of(logs[...])
    grad_key = [0.0] * chunks
    grad_value = [0.0] * chunks
    grad_query = []
    for h in range(chunks):
        rows = slice(h * size, (h + 1) * size)
        grad_row = 0.0
        delta = 0.0
        kept = []
        for k in range(h + 1):
            keys = slice(k * size, (k + 1) * size)
            scores = dot_nt(query[rows], key[keys]) * factor
            probs = jnp.exp(scores - log_column[rows])
            grad_probs = dot_nt(grad[rows], values[keys])
            delta = delta + jnp.sum(probs * grad_probs, axis=1, keepdims=True)
            kept.append((probs, grad_probs))
        for k, (probs, grad_probs) in enumerate(kept):
            keys = slice(k * size, (k + 1) * size)
            grad_scores = (probs * (grad_probs - delta)).astype(BF)
            grad_row = grad_row + dot(grad_scores, key[keys])
            grad_key[k] = grad_key[k] + dot_tn(grad_scores, query[rows])
            grad_value[k] = grad_value[k] + dot_tn(probs.astype(BF), grad[rows])
        grad_query.append(grad_row)

    value_out[...] = jnp.concatenate(grad_value).astype(BF)
    for p, (pre, grads, out) in enumerate(
        ((query_pre, grad_query, query_out), (key_pre, grad_key, key_out))
    ):
        turned = jnp.concatenate(grads) * factor
        turned = turned * cosine[...] - pltpu.roll(turned, HD // 2, 1) * sine[...]
        turned = turned * gains[p : p + 1]
        out[...] = turned.astype(BF)
        inner = jnp.sum(turned * pre[0].astype(F32), axis=1, keepdims=True)
        inner = jnp.broadcast_to(inner, (total, 128))

        @pl.when(head == 0)
        def _():
            inner_rows[p] = inner

        @pl.when(head > 0)
        def _():
            inner_rows[p] += inner

    @pl.when(head == pl.num_programs(0) - 1)
    def _():
        for p in range(2):
            inner_out[8 * p : 8 * p + 8] = jnp.transpose(inner_rows[p])[:8]


def attention_back(queries, key_rows, pre, grad_mixed, logs, cosine, sine, gains, chunks):
    _, total, width = pre.shape
    heads = width // HD
    factor = 1.0 / math.sqrt(HD)

    def head(p):
        return spec((1, total, HD), lambda i: (p, 0, i))

    by_head = spec((total, HD), lambda i: (0, i))
    return call(
        functools.partial(attention_back_body, chunks, factor),
        (heads,),
        [queries, key_rows, pre, pre, pre, grad_mixed, logs, cosine, sine, gains],
        [by_head, by_head, head(0), head(1), head(2), by_head]
        + [spec((8, total), lambda i: (i, 0)), whole(cosine), whole(sine)]
        + [spec((gains.shape[0], HD), lambda i: (0, i))],
        [
            (shape_of((total, width), BF), by_head),
            (shape_of((total, width), BF), by_head),
            (shape_of((total, width), BF), by_head),
            (shape_of((16, total), F32), pl.BlockSpec((16, total), lambda *_: (0, 0))),
        ],
        [pltpu.VMEM((2, total, 128), F32)],
        flops=10 * total * total * width,
    )


def split_out(value, keep, send):
    if keep.ndim == 2:
        half = value.shape[0] // 2
        keep[...] = value[:half].astype(BF)
        send[...] = value[half:].astype(BF)
        return
    half = keep.shape[1]
    for h in range(keep.shape[0]):
        keep[h] = value[2 * h * half : (2 * h + 1) * half].astype(BF)
        send[h] = value[(2 * h + 1) * half : (2 * h + 2) * half].astype(BF)


def qkv_grads_body(chunks, *refs):
    query_grad, key_grad, value_grad, query_pre, key_pre = refs[:5]
    squares, inners, x_refs = refs[5:9], refs[9:13], refs[13:16]
    low, ups, grads, lows, down_out, up_out = refs[16:]
    rank = ups.shape[1]
    total = query_grad.shape[0]
    for p, (grad, pre) in enumerate(((query_grad, query_pre), (key_grad, key_pre))):
        scale = lax.rsqrt(aligned_sums(squares, p, chunks) / D + epsilon)
        inner = aligned_sums(inners, p, chunks) * (scale * scale * scale / D)
        grads[p] = (grad[...].astype(F32) * scale - pre[0].astype(F32) * inner).astype(BF)
    grads[2] = value_grad[...]
    for p in range(3):
        lows[:, p * rank : (p + 1) * rank] = dot_nt(grads[p], ups[p]).astype(BF)
        up_out[p] = dot_tn(low[p], grads[p])
    size = total // chunks
    down = 0.0
    for h in range(chunks):
        x = load_parts(x_refs, h * size // 4, size // 4)
        down += dot_tn(lows[h * size : (h + 1) * size], x)
    down_out[...] = down


def qkv_grads(turned, grad_values, pre, squares, inners, x_parts, low, ups, chunks):
    count, total, width = pre.shape
    rank = ups.shape[1]
    full = x_parts[0].shape[1]

    def pre_rows(p):
        return pl.BlockSpec((1, total, width), lambda *_: (p, 0, 0))

    outs = [
        shape_of((count, total, width), BF),
        shape_of((total, count * rank), BF),
        shape_of((count * rank, full), F32),
        shape_of((count, rank, width), F32),
    ]
    return call(
        functools.partial(qkv_grads_body, chunks),
        (1,),
        [*turned, grad_values, pre, pre, *squares, *inners, *x_parts, low, ups],
        [whole(turned[0]), whole(turned[1]), whole(grad_values), pre_rows(0), pre_rows(1)]
        + [whole(v) for v in (*squares, *inners, *x_parts, low)]
        + [pl.BlockSpec((count, rank, width), lambda *_: (0, 0, 0))],
        [(o, whole(o)) for o in outs],
        flops=2 * total * width * 512,
    )


def qkv_back_body(grads, lows, weight, downs, keep, send):
    value = dot(lows[...], downs[...])
    for p in range(3):
        value += dot_nt(grads[p], weight[p])
    split_out(value, keep, send)


def qkv_back(grads, lows, weight, downs, chunks):
    count, full, width = weight.shape
    total = grads.shape[1]
    tile = tile_of(full)
    half = total // chunks // 2
    part = (shape_of((chunks, half, full), BF), spec((chunks, half, tile), lambda i: (0, 0, i)))
    return call(
        qkv_back_body,
        (full // tile,),
        [grads, lows, weight, downs],
        [
            whole(grads),
            whole(lows),
            spec((count, tile, width), lambda i: (0, i, 0)),
            spec((downs.shape[0], tile), lambda i: (0, i)),
        ],
        [part, part],
        flops=2 * total * full * width * count,
    )


def partial_body(streamed, beside, x, weight, down, up, *refs):
    keep, send, low, *scratch = refs[beside:]
    step = pl.program_id(0)
    tile = keep.shape[1]

    def columns(i):
        return pl.ds(pl.multiple_of(i * tile, tile), tile)

    def copy(i):
        held, sems = scratch
        return pltpu.make_async_copy(weight.at[:, columns(i)], held.at[:, columns(i)], sems.at[i])

    @pl.when(step == 0)
    def _():
        if streamed:
            for i in range(weight.shape[1] // tile):
                copy(i).start()
        low[...] = dot_nt(x[...], down[...]).astype(BF)

    if streamed:
        copy(step).wait()
        held = scratch[0]
    else:
        held = weight
    split_out(dot(x[...], held[:, columns(step)]) + dot(low[...], up[...]), keep, send)


def partial_forward(x, chunk, chunks, weight, down, up, streamed, beside=()):
    total, depth = x.shape
    size = total // chunks
    full = weight.shape[-1]
    tile = tile_of(full)
    half = size // 2
    rank = down.shape[0]
    scratch = [pltpu.VMEM(weight.shape, BF), pltpu.SemaphoreType.DMA((full // tile,))]
    return call(
        functools.partial(partial_body, streamed, len(beside)),
        (full // tile,),
        [x, weight, down, up, *beside],
        [
            pl.BlockSpec((size, depth), lambda *_: (chunk, 0)),
            HBM if streamed else VMEM,
            whole(down),
            spec((rank, tile), lambda i: (0, i)),
            *[VMEM] * len(beside),
        ],
        [
            (shape_of((half, full), BF), spec((half, tile), lambda i: (0, i))),
            (shape_of((half, full), BF), spec((half, tile), lambda i: (0, i))),
            (shape_of((size, rank), BF), pl.BlockSpec((size, rank), lambda *_: (0, 0))),
        ],
        scratch if streamed else (),
        flops=2 * size * depth * full,
    )


def gate_up_body(*refs):
    x_refs, (weight, downs, ups, gate, upper, act, low, rows) = refs[:4], refs[4:]
    rank = ups.shape[1]
    tile = gate.shape[1]
    step = pl.program_id(0)

    @pl.when(step == 0)
    def _():
        rows[...] = load_parts(x_refs)
        low[...] = dot_nt(rows[...], downs[...]).astype(BF)

    columns = pl.ds(pl.multiple_of(step * tile, tile), tile)
    gate_pre = dot(rows[...], weight[0, :, columns]) + dot(low[:, :rank], ups[0])
    upper_pre = dot(rows[...], weight[1, :, columns]) + dot(low[:, rank:], ups[1])
    gate[...] = gate_pre.astype(BF)
    upper[...] = upper_pre.astype(BF)
    act[...] = (gate_pre * jax.nn.sigmoid(gate_pre) * upper_pre).astype(BF)


def gate_up_forward(x_parts, weight, downs, ups):
    _, full, width = weight.shape
    size = 4 * x_parts[0].shape[0]
    rank = ups.shape[1]
    tile = tile_of(width)
    out = (shape_of((size, width), BF), spec((size, tile), lambda i: (0, i)))
    return call(
        gate_up_body,
        (width // tile,),
        [*x_parts, weight, downs, ups],
        [whole(x) for x in x_parts] + [VMEM, whole(downs), spec((2, rank, tile), lambda i: (0, 0, i))],
        [
            out,
            out,
            out,
            (shape_of((size, 2 * rank), BF), pl.BlockSpec((size, 2 * rank), lambda *_: (0, 0))),
        ],
        [pltpu.VMEM((size, full), BF)],
        flops=4 * size * full * width,
    )


def feed_back_body(*refs):
    g_refs = refs[:4]
    weight, down, gate, upper, gate_low, feed_low, feed_up, ups, _ = refs[4:13]
    gate_grad, upper_grad, low_out, down_a, feed_b, hidden_b, rows, low, lows = refs[13:]
    rank = down.shape[0]
    step = pl.program_id(0)
    @pl.when(step == 0)
    def _():
        rows[...] = load_parts(g_refs)
        low[...] = dot_nt(rows[...], feed_up[...]).astype(BF)
        feed_b[...] = dot_tn(feed_low[...], rows[...])
        lows[...] = jnp.zeros_like(lows)

    tile = gate.shape[1]
    held_rows = pl.ds(pl.multiple_of(step * tile, tile), tile)
    grad_act = dot_nt(rows[...], weight[held_rows]) + dot(low[...], down[...])
    gate_pre, upper_pre = gate[...].astype(F32), upper[...].astype(F32)
    sig = jax.nn.sigmoid(gate_pre)
    silu = gate_pre * sig
    down_a[...] = dot_tn(low[...], (silu * upper_pre).astype(BF))
    grad_upper = (grad_act * silu).astype(BF)
    grad_gate = (grad_act * upper_pre * (sig + silu * (1.0 - sig))).astype(BF)
    gate_grad[...] = grad_gate
    upper_grad[...] = grad_upper
    hidden_b[0] = dot_tn(gate_low[:, :rank], grad_gate)
    hidden_b[1] = dot_tn(gate_low[:, rank:], grad_upper)
    lows[:, :rank] += dot_nt(grad_gate, ups[0])
    lows[:, rank:] += dot_nt(grad_upper, ups[1])

    @pl.when(step == pl.num_programs(0) - 1)
    def _():
        low_out[...] = lows[...].astype(BF)


def feed_back(g_parts, weight, down, gate, upper, gate_low, feed_low, feed_up, ups, beside):
    width, depth = weight.shape
    size = 4 * g_parts[0].shape[0]
    rank = down.shape[0]
    tile = tile_of(width)
    by_tile = spec((size, tile), lambda i: (0, i))
    return call(
        feed_back_body,
        (width // tile,),
        [*g_parts, weight, down, gate, upper, gate_low, feed_low, feed_up, ups, beside],
        [whole(g) for g in g_parts]
        + [
            VMEM,
            spec((rank, tile), lambda i: (0, i)),
            by_tile,
            by_tile,
            whole(gate_low),
            whole(feed_low),
            whole(feed_up),
            spec((2, rank, tile), lambda i: (0, 0, i)),
            VMEM,
        ],
        [
            (shape_of((size, width), BF), by_tile),
            (shape_of((size, width), BF), by_tile),
            (shape_of((size, 2 * rank), BF), pl.BlockSpec((size, 2 * rank), lambda *_: (0, 0))),
            (shape_of((rank, width), F32), spec((rank, tile), lambda i: (0, i))),
            (shape_of((rank, depth), F32), pl.BlockSpec((rank, depth), lambda *_: (0, 0))),
            (shape_of((2, rank, width), F32), spec((2, rank, tile), lambda i: (0, 0, i))),
        ],
        [
            pltpu.VMEM((size, depth), BF),
            pltpu.VMEM((size, rank), BF),
            pltpu.VMEM((size, 2 * rank), F32),
        ],
        flops=2 * size * depth * width,
    )


def gate_up_back_body(gate_grad, upper_grad, weight, low, downs, *refs):
    x_refs, (keep, send, down_out) = refs[:4], refs[4:]
    tile = keep.shape[1]
    held_rows = pl.ds(pl.multiple_of(pl.program_id(0) * tile, tile), tile)
    value = dot_nt(gate_grad[...], weight[0, held_rows]) + dot_nt(upper_grad[...], weight[1, held_rows])
    split_out(value + dot(low[...], downs[...]), keep, send)
    down_out[...] = dot_tn(low[...], load_parts(x_refs))


def gate_up_back(gate_grad, upper_grad, weight, low, downs, x_parts):
    _, full, width = weight.shape
    size = gate_grad.shape[0]
    half = size // 2
    ranks = downs.shape[0]
    tile = tile_of(full)
    return call(
        gate_up_back_body,
        (full // tile,),
        [gate_grad, upper_grad, weight, low, downs, *x_parts],
        [whole(gate_grad), whole(upper_grad), VMEM, whole(low), spec((ranks, tile), lambda i: (0, i))]
        + [column_spec(x, tile) for x in x_parts],
        [
            (shape_of((half, full), BF), spec((half, tile), lambda i: (0, i))),
            (shape_of((half, full), BF), spec((half, tile), lambda i: (0, i))),
            (shape_of((ranks, full), F32), spec((ranks, tile), lambda i: (0, i))),
        ],
        flops=4 * size * full * width,
    )


def out_back_body(*refs):
    g_refs = refs[:4]
    weight, down, up, mixed, low, grad_mixed, down_out, up_out, rows, grad_low = refs[4:]

    @pl.when(pl.program_id(0) == 0)
    def _():
        rows[...] = load_parts(g_refs)
        grad_low[...] = dot_nt(rows[...], up[...]).astype(BF)
        up_out[...] = dot_tn(low[...], rows[...])

    tile = grad_mixed.shape[1]
    held_rows = pl.ds(pl.multiple_of(pl.program_id(0) * tile, tile), tile)
    grad_mixed[...] = (dot_nt(rows[...], weight[held_rows]) + dot(grad_low[...], down[...])).astype(BF)
    down_out[...] = dot_tn(grad_low[...], mixed[...])


def out_back(g_parts, weight, down, up, mixed, low, chunk):
    width, depth = weight.shape
    size = 4 * g_parts[0].shape[0]
    rank = down.shape[0]
    tile = min(256, width)
    return call(
        out_back_body,
        (width // tile,),
        [*g_parts, weight, down, up, mixed, low],
        [whole(g) for g in g_parts]
        + [
            VMEM,
            spec((rank, tile), lambda i: (0, i)),
            whole(up),
            spec((size, tile), lambda i: (chunk, i)),
            whole(low),
        ],
        [
            (shape_of((size, width), BF), spec((size, tile), lambda i: (0, i))),
            (shape_of((rank, width), F32), spec((rank, tile), lambda i: (0, i))),
            (shape_of((rank, depth), F32), pl.BlockSpec((rank, depth), lambda *_: (0, 0))),
        ],
        [pltpu.VMEM((size, depth), BF), pltpu.VMEM((size, rank), BF)],
        flops=2 * size * depth * width,
    )


def load_parts(refs, first=0, count=None, columns=slice(None)):
    own, far, *near = refs
    if len(near) == 1:
        near = near[0].at[0], near[0].at[1]
    rows = slice(first, own.shape[0] if count is None else first + count)
    return jnp.concatenate([ref[rows, columns] for ref in (own, far, *near)])


def ctx_flips():
    size = lax.axis_size("ctx")
    return [flip for flip in (2, 4, 8, 16, 1) if flip < size]


def ctx_step(at):
    return lambda value: over_ctx(value, ctx_flips()[at])


def gathered_place(ctx, other):
    place = 0
    for at, flip in enumerate(ctx_flips()):
        place = place + (((ctx ^ other) // flip) % 2) * 2**at
    return place


def column_cuts(partial, starts):
    width = partial.shape[-1] // 4
    zero = jnp.uint32(0)
    blocks = [lax.dynamic_slice(partial, (zero, start), (partial.shape[0], width)) for start in starts]
    return blocks[0], blocks[1], jnp.stack(blocks[2:]).astype(BF)


def natural(parts, shard):
    out = []
    for index in range(4):
        value = parts[0]
        for flip, part in zip(FLIPS[1:], parts[1:]):
            value = jnp.where((shard ^ flip) == index, part, value)
        out.append(value)
    return out


def row_sum(keep, near, got):
    rows = got.shape[-2]
    own = (slice(None),) * (len(keep.shape) - 2) + (slice(0, rows),)
    return keep[own].astype(F32) + near[own].astype(F32) + got[...].astype(F32)


def rms_scale(value):
    return lax.rsqrt(jnp.mean(value * value, axis=-1, keepdims=True) + epsilon)


def rms_back(value, scale, gain, grad):
    weighted = grad * gain
    return scale * weighted - value * (
        scale * scale * scale * jnp.mean(value * weighted, axis=-1, keepdims=True)
    )


def far_body(keep, near, far):
    rows = far.shape[-2]
    below = (slice(None),) * (len(keep.shape) - 2) + (slice(rows, 2 * rows),)
    far[...] = (keep[below].astype(F32) + near[below].astype(F32)).astype(BF)


def attention_rows_body(keep, near, got, token, gain, value_out, resid_out, low_out):
    value = row_sum(keep, near, got)
    resid = token[...].astype(F32) + value * rms_scale(value) * gain[...]
    value_out[...] = value
    resid_out[...] = resid
    low_out[...] = resid.astype(BF)


def feed_rows_body(keep, near, got, resid, cot, gain, output, grad):
    value = row_sum(keep, near, got)
    scale = rms_scale(value)
    output[...] = (resid[...] + value * scale * gain[...]).astype(BF)
    grad[...] = rms_back(value, scale, gain[...], cot[...].astype(F32)).astype(BF)


def back_rows_body(keep, near, got, value, cot, gain, grad_out, low_out):
    grad = cot[...].astype(F32) + row_sum(keep, near, got)
    grad_out[...] = grad
    value = value[...]
    low_out[...] = rms_back(value, rms_scale(value), gain[...], grad).astype(BF)


def far_two_body(keep, near, *fars):
    for h, far in enumerate(fars):
        far_body(keep.at[h], near.at[h], far)


def input_rows_body(order, keep, near, *refs):
    chunks = keep.shape[0]
    gots, resids, outs = refs[:chunks], refs[chunks : 2 * chunks], refs[2 * chunks :]
    rows = [
        (row_sum(keep.at[h], near.at[h], gots[h]) + resids[h][...]).astype(BF) for h in range(chunks)
    ]

    @pl.when(order[0] == 0)
    def _():
        for out, row in zip(outs, rows):
            out[...] = row

    @pl.when(order[0] != 0)
    def _():
        for out, row in zip(outs, rows[::-1]):
            out[...] = row


def input_rows(keep, near, gots, resids, order):
    args = [keep, near, *gots, *resids]
    outs = [shape_of(resid.shape, BF) for resid in resids]
    return call(
        input_rows_body, (1,), args, [whole(x) for x in args], [(o, whole(o)) for o in outs], scalars=[order]
    )


def by_rows(body, args, kinds):
    *lead, rows, width = args[0].shape
    outs = [shape_of((*lead, rows // 2, width), kind) for kind in kinds]
    return call(body, (1,), args, [whole(x) for x in args], [(o, whole(o)) for o in outs])


def rotate(value, cosine, sine):
    half = value.shape[-1] // 2
    turned = jnp.concatenate([value[..., half:], value[..., :half]], axis=-1)
    return value * cosine[:, None, :] + turned * sine[:, None, :]


def realign(value, flip, chunks):
    shape = value.shape
    value = value.reshape(shape[0], chunks, 2, 2, -1)
    if flip & 1:
        value = value[:, :, ::-1]
    if flip & 2:
        value = value[:, :, :, ::-1]
    return value.reshape(shape)


def group_of(sequence, part, per_sequence, ctx_size):
    if per_sequence > 1:
        return sequence * per_sequence + part
    depth = sequence % (ctx_size // 2)
    return 2 * depth + (depth + sequence // (ctx_size // 2)) % 2


def sequence_of(ctx, per_sequence, ctx_size):
    if per_sequence > 1:
        return ctx // per_sequence, ctx % per_sequence
    depth = ctx // 2
    return depth + ctx_size // 2 * ((ctx + depth) % 2), 0 * ctx


def wide_attention(pre, sums, cosine, sine, gains, chunks, positions, groups):
    _, total, width = pre.shape
    heads = width // HD
    pre = pre.astype(F32)
    squares = sum(realign(s[::8], flip, chunks) for flip, s in zip(FLIPS, sums))
    scales = lax.rsqrt(squares[:2] / D + epsilon)[:, :, None]

    def as_heads(value):
        return value.reshape(total, heads, HD)

    queries, key_rows = [
        rotate(as_heads(pre[p] * scales[p] * gains[p]), cosine, sine).astype(BF) for p in range(2)
    ]

    def over_sequence(value):
        return lax.all_gather(value, "ctx", axis=0, tiled=True, axis_index_groups=groups)

    key_all, value_all = over_sequence(key_rows), over_sequence(as_heads(pre[2].astype(BF)))
    visible = over_sequence(positions // BLOCK)[None, :] <= (positions // BLOCK)[:, None]
    factor = 1.0 / math.sqrt(HD)
    scores = jnp.einsum("qhd,khd->hqk", queries, key_all, preferred_element_type=F32) * factor
    scores = jnp.where(visible, scores, far_below)
    weights = jnp.exp(scores - jnp.max(scores, axis=-1, keepdims=True))
    probs = weights / jnp.sum(weights, axis=-1, keepdims=True)
    mixed = jnp.einsum("hqk,khd->qhd", probs.astype(BF), value_all, preferred_element_type=F32)
    mixed = mixed.astype(BF).reshape(total, width)

    def back(grad_mixed):
        grad = as_heads(grad_mixed)
        grad_probs = jnp.einsum("qhd,khd->hqk", grad, value_all, preferred_element_type=F32)
        delta = jnp.sum(probs * grad_probs, axis=-1, keepdims=True)
        grad_scores = (probs * (grad_probs - delta)).astype(BF)
        grad_queries = jnp.einsum("hqk,khd->qhd", grad_scores, key_all, preferred_element_type=F32)
        grad_keys = jnp.einsum("hqk,qhd->khd", grad_scores, queries, preferred_element_type=F32)
        grad_values = jnp.einsum("hqk,qhd->khd", probs.astype(BF), grad, preferred_element_type=F32)
        grad_keys, grad_values = [
            lax.psum_scatter(
                g.astype(BF), "ctx", scatter_dimension=0, tiled=True, axis_index_groups=groups
            ).astype(F32)
            for g in (grad_keys * factor, grad_values)
        ]
        turned = [
            rotate(g, cosine, -sine).reshape(total, width) * gains[p]
            for p, g in enumerate((grad_queries * factor, grad_keys))
        ]
        inner = jnp.stack([jnp.sum(turned[p] * pre[p], axis=-1) for p in range(2)])
        inner = jnp.repeat(inner, 8, axis=0)
        values = grad_values.reshape(total, width).astype(BF)
        return turned[0].astype(BF), turned[1].astype(BF), values, inner

    return mixed, back


def choose_body(place, wide, down, model, hidden, gains, wide_out, down_out, model_out, hidden_out, small, sems):
    at = place[0]
    sources = [(wide.at[:, at], wide_out), (down.at[at], down_out)]
    sources += [(model.at[:, at], model_out), (hidden.at[:, at], hidden_out)]
    run_copies([pltpu.make_async_copy(source, to, sems.at[i]) for i, (source, to) in enumerate(sources)])
    rank, width = wide_out.shape[1:]
    shared = [wide_out[p] for p in (0, 1, 2, 4, 5)] + [model_out[p] for p in (3, 4)]
    last = jnp.concatenate([gains[2:], jnp.zeros((rank - 2, width), BF)])
    for at, value in enumerate([*shared, last]):
        column = at // 2 * width
        small[at % 2 * rank : (at % 2 + 1) * rank, column : column + width] = value


def choose(place, a_wide, a_down, b_model, b_hidden, gains):
    rank, width = a_wide.shape[2:]
    shapes = [a_wide.shape[:1] + a_wide.shape[2:], a_down.shape[1:]]
    shapes += [b_model.shape[:1] + b_model.shape[2:], b_hidden.shape[:1] + b_hidden.shape[2:]]
    shapes.append((2 * rank, 4 * width))
    outs = [shape_of(s, BF) for s in shapes]
    return call(
        choose_body,
        (1,),
        [a_wide, a_down, b_model, b_hidden, gains],
        [HBM] * 4 + [whole(gains)],
        [(o, whole(o)) for o in outs],
        [pltpu.SemaphoreType.DMA((4,))],
        scalars=[place],
    )


def place_body(rank, count, unused, plan, at, *refs):
    sources, outs = refs[:count], refs[count + unused :]
    for out, maps in zip(outs, plan):
        for n in range(out.shape[1]):
            for p, pieces in enumerate(maps):
                begin = 0
                for source, place in pieces:
                    value = sources[source][at[n], place * rank : (place + 1) * rank].astype(F32)
                    out[p, n, :, begin : begin + value.shape[-1]] = value
                    begin += value.shape[-1]


def on_device(
    tokens,
    cotangent,
    adapter_index,
    w_attn,
    w_gate_up,
    w_down,
    gains,
    a_wide,
    a_down,
    b_model,
    b_hidden,
):
    seqs, rows = tokens.shape[0], tokens.shape[1]
    shards, ctxs = lax.axis_size("shard"), lax.axis_size("ctx")
    shard, ctx = lax.axis_index("shard"), lax.axis_index("ctx")
    batch = seqs * shards
    per_sequence = ctxs // batch
    group_rows = batch * rows
    chunks = seqs
    chunk_rows = shards * rows
    wide = HEADS // shards * HD
    adapters, rank = a_down.shape[:2]

    groups = [[group_of(q, k, per_sequence, ctxs) for k in range(per_sequence)] for q in range(batch)]
    my_sequence, my_part = sequence_of(ctx, per_sequence, ctxs)
    my_slot = my_sequence % seqs
    my_spot = (ctx % batch) // shards

    pairs = []
    for p in range(seqs):
        pairs.append([])
        for c in range(ctxs):
            for s in range(shards):
                k, local = c // batch, c % batch
                spot, owner = local // shards, local % shards
                to = groups[seqs * s + (p + spot) % seqs][k]
                pairs[p].append((c * shards + s, to * shards + owner))

    windows = Windows()
    side_by_side = windows.side_by_side

    def is_place(index):
        return [index % seqs == at for at in range(1, seqs)]

    flags = {
        "cut": [((p + my_spot) % seqs).astype(jnp.uint32) for p in range(seqs)],
        "chunk": [is_place(my_slot - h) for h in range(seqs)],
        "return": [is_place(my_slot - p) for p in range(seqs)],
        "order": [is_place(j - my_spot) for j in range(seqs)],
        "columns": [((shard ^ flip) * wide).astype(jnp.uint32) for flip in FLIPS],
        "places": jnp.stack([shard, ctx % 4]).astype(jnp.int32),
        "turn": [((my_slot - p) % seqs)[None].astype(jnp.int32) for p in range(seqs)],
    }

    def pick(parts, is_it):
        value = parts[0]
        for part, flag in zip(parts[1:], is_it):
            value = jnp.where(flag, part, value)
        return value

    def cut_rows(*values):
        return [
            jnp.concatenate(
                [
                    lax.dynamic_index_in_dim(value, flags["cut"][p], 0, keepdims=False)
                    for value in values
                ]
            )
            for p in range(seqs)
        ]

    def send_row(p):
        return lambda cut: lax.ppermute(cut, ("ctx", "shard"), pairs[p])

    def chunk_order(got):
        return [pick(got, flags["chunk"][h]) for h in range(seqs)]

    def return_cuts(parts):
        return [pick(parts, flags["return"][p]) for p in range(seqs)]

    def return_row(p):
        return lambda cut: lax.ppermute(cut, ("ctx", "shard"), [(b, a) for a, b in pairs[p]])

    def return_order(got):
        return jnp.stack([pick(got, flags["order"][j]) for j in range(seqs)])

    def core(value):
        return over_shard(value, 1)

    def chip(value):
        return over_shard(value, 2)

    def across(value):
        return over_shard(value, 3)

    def by_x(value):
        return over_ctx(value, 1)

    def by_z(value):
        return over_ctx(value, 2)

    def to_all(value):
        return [(functools.partial(over_shard, flip=flip), value) for flip in FLIPS[1:]]

    index_own = adapter_index[:, 0]
    (qkv_near, qkv_far, qkv_cross, flags), index_got = side_by_side(
        lambda x: (*cut(x[0], 0, 3, x[1]["places"], False), x[1]), [w_attn, flags], to_all(index_own)
    )
    places = flags["places"]
    index_all = jnp.concatenate(natural([index_own, *index_got], shard))
    sequence_with = jnp.sum(
        jnp.where(
            index_all[None, :] == jnp.arange(adapters, dtype=jnp.int32)[:, None],
            jnp.arange(batch, dtype=jnp.int32)[None, :],
            0,
        ),
        axis=1,
    )
    table = jnp.array(groups, jnp.int32)
    if per_sequence > 1:
        where = sequence_with
    else:
        group_with = jnp.sum(
            jnp.where(
                sequence_with[:, None] == jnp.arange(batch, dtype=jnp.int32)[None, :], table[:, 0][None, :], 0
            ),
            axis=1,
        )
        where = gathered_place(ctx, group_with)

    row_cuts = cut_rows(tokens)

    def rope_tables(place):
        shape = (chunks, shards, rows, HD)
        spot, turn, row, lane = [lax.broadcasted_iota(jnp.int32, shape, axis) for axis in range(4)]
        owner = place ^ (turn // 2 + turn % 2 * 2)
        position = my_part * group_rows + (spot * shards + owner) * rows + row
        freqs = jnp.exp((lane % (HD // 2)).astype(F32) * (-2.0 * math.log(rope_base) / HD))
        angles = position.astype(F32) * freqs
        sine = jnp.sin(angles) * jnp.where(lane < HD // 2, -1.0, 1.0)
        return position[..., 0].reshape(-1), jnp.cos(angles).reshape(-1, HD), sine.reshape(-1, HD)

    def prepare(x):
        chosen = choose(x[0], a_wide, a_down, b_model, b_hidden, gains)
        return chosen, cut(x[1], 0, 2, x[2], True), x[3], rope_tables(x[2][0])

    (chosen, gate_up_cuts, where, (positions, cosine, sine)), [qkv_a, qkv_b, *row_got, qkv_near] = side_by_side(
        prepare,
        [index_all[my_sequence][None], w_gate_up, places, where],
        [
            (chip, qkv_far),
            (across, qkv_cross),
            (send_row(0), row_cuts[0]),
            (send_row(1), row_cuts[1]),
            (core, qkv_near),
        ],
    )
    own_wide, own_down, own_model, own_hidden, small = chosen
    near, gate_far, gate_cross, up_far, up_cross = gate_up_cuts

    token_rows = chunk_order(row_got)
    token_own = jnp.concatenate([*token_rows, small])
    held = {}

    def load_out(weights):
        held["out"], held["down"], done = load_plain(*weights)
        return done

    done, [qkv_xa, qkv_xb, qkv_za, qkv_zb, token_far] = side_by_side(
        load_out,
        [w_attn, w_down],
        [(by_x, qkv_a), (by_x, qkv_b), (by_z, qkv_a), (by_z, qkv_b), (chip, token_own)],
    )
    windows.carried.append(done)
    _, [last_a, last_b, token_near, gate_a] = side_by_side(
        None,
        None,
        [
            (by_x, qkv_za),
            (by_z, qkv_xb),
            (core, jnp.stack([token_own, token_far])),
            (chip, gate_far),
        ],
    )
    w_qkv = [qkv_near, qkv_a, qkv_b, qkv_xa, qkv_xb, qkv_za, qkv_zb, last_a, last_b]
    token_parts = [token_own, token_far, token_near]
    small_parts = [part[..., seqs * rows :, :] for part in token_parts]
    small_parts = [small_parts[0], small_parts[1], small_parts[2][0], small_parts[2][1]]
    small_all = jnp.concatenate(
        natural(
            [
                jnp.concatenate([part[:, at * wide : (at + 1) * wide] for at in range(4)])
                for part in small_parts
            ],
            shard,
        ),
        axis=1,
    )
    qkv_downs = small_all[: 3 * rank]
    gate_downs = small_all[3 * rank : 5 * rank]
    out_up = small_all[5 * rank : 6 * rank]
    feed_up = small_all[6 * rank : 7 * rank]
    attn_gain = small_all[7 * rank : 7 * rank + 1].astype(F32)
    feed_gain = small_all[7 * rank + 1 : 7 * rank + 2].astype(F32)
    head_gains = gains[:2].astype(F32)

    (pre, qkv_low, squares, qkv_held), [gate_b, gate_xa, gate_za, near] = side_by_side(
        lambda x: qkv_forward(x, chunks, rows, w_attn, w_qkv, places, qkv_downs, own_model),
        token_parts,
        [(across, gate_cross), (by_x, gate_a), (by_z, gate_a), (core, near)],
    )

    def from_all(sums, others):
        _, got = side_by_side(None, None, to_all(sums) + others)
        return [sums, *got[:3]], got[3:]

    squares, _ = from_all(squares[:16], [])
    simple = per_sequence == 1 and chunk_rows == BLOCK
    attention_sends = [(chip, up_far), (by_x, gate_b), (by_z, gate_b)]
    if simple:
        (queries, key_rows, mixed, logs), got = side_by_side(
            lambda x: attention_forward(x[0], x[1], x[2], x[3], head_gains, chunks),
            [pre, squares, cosine, sine],
            attention_sends,
        )
    else:
        mixed, attention_grads = wide_attention(
            pre, squares, cosine, sine, head_gains, chunks, positions, groups
        )
        got = [send(value) for send, value in attention_sends]
    up_a, gate_xb, gate_zb = got

    every = range(chunks)
    assert chunks == 2
    def far_sum(keep, near):
        return by_rows(far_body, [keep, near], [BF])[0]

    def project_out(x, h):
        return partial_forward(x, h, chunks, held["out"], own_wide[3], out_up, False)

    def attention_rows(h, keep, near, got):
        return by_rows(attention_rows_body, [keep, near, got, token_rows[h], attn_gain], [F32, F32, BF])

    def feed_rows(h, keep, near, got):
        return by_rows(feed_rows_body, [keep, near, got, resid[h], cot[h], feed_gain], [BF, BF])

    def back_rows(h, keep, near, got):
        return by_rows(back_rows_body, [keep, near, got, attn_pre[h], cot[h], attn_gain], [F32, BF])

    def up_gate(parts):
        return gate_up_forward(parts, gate_up_held, gate_downs, own_hidden)

    def down(act):
        return partial_forward(act, 0, 1, held["down"], own_down, feed_up, False, [gate_up_held])

    def back_down(h, parts):
        return feed_back(
            parts, held["down"], own_down, hidden[h][0], hidden[h][1], hidden[h][3], feed_parts[h][2], feed_up, own_hidden, gate_up_held
        )

    def back_up_gate(h, gate_grad, upper_grad):
        return gate_up_back(
            gate_grad, upper_grad, gate_up_held, hidden_grads[h][2], gate_downs, resid_parts[h]
        )

    def back_out(h, parts):
        return out_back(parts, held["out"], own_wide[3], out_up, mixed, out_parts[h][2], h)

    none = [None] * PARTS

    def load_first(x):
        gate = [*x, None, None]
        held["gate_up"], done = load([gate, none], places, w_gate_up, near)
        return done

    def load_more(x):
        gate = none[:6] + x[:2]
        up = [*x[2:], None, None]
        held["gate_up"], done = load([gate, up], places, held=held["gate_up"])
        return done

    def load_last(x):
        held["gate_up"], done = load([none, none[:6] + x], places, held=held["gate_up"])
        return done

    attn_pre, resid, resid_low = [None] * 2, [None] * 2, [None] * 2
    resid_parts, hidden, feed_parts, output = [None] * 2, [None] * 2, [None] * 2, [None] * 2
    hidden_grads, resid_grads, grad_resid, out_grads = [None] * 2, [None] * 2, [None] * 2, [None] * 2
    out_parts, [up_b, up_xa, up_za] = side_by_side(
        lambda x: [project_out(x, h) for h in every], mixed, [(across, up_cross), (by_x, up_a), (by_z, up_a)]
    )
    _, [core0, core1] = side_by_side(None, None, [(core, out_parts[0][1]), (core, out_parts[1][1])])
    far0, far1 = far_sum(out_parts[0][0], core0), far_sum(out_parts[1][0], core1)
    done, [got0, got1, gate_last_a, gate_last_b] = side_by_side(
        load_first,
        [gate_a, gate_b, gate_xa, gate_xb, gate_za, gate_zb],
        [(chip, far0), (chip, far1), (by_x, gate_za), (by_z, gate_xb)],
    )
    windows.carried.append(done)
    attn_pre[0], resid[0], resid_low[0] = attention_rows(0, out_parts[0][0], core0, got0)
    attn_pre[1], resid[1], resid_low[1] = attention_rows(1, out_parts[1][0], core1, got1)
    _, [far0, near0, up_xb, up_zb] = side_by_side(
        None, None, [(chip, resid_low[0]), (core, resid_low[0]), (by_x, up_b), (by_z, up_b)]
    )
    done, [cross0, far1, near1, up_last_a, up_last_b] = side_by_side(
        load_more,
        [gate_last_a, gate_last_b, up_a, up_b, up_xa, up_xb, up_za, up_zb],
        [(core, far0), (chip, resid_low[1]), (core, resid_low[1]), (by_x, up_za), (by_z, up_xb)],
    )
    windows.carried.append(done)
    resid_parts[0] = [resid_low[0], far0, near0, cross0]
    done, [cross1] = side_by_side(load_last, [up_last_a, up_last_b], [(core, far1)])
    windows.carried.append(done)
    gate_up_held = held["gate_up"]
    resid_parts[1] = [resid_low[1], far1, near1, cross1]

    cot_cuts = cut_rows(cotangent)
    hidden[0], [cot0] = side_by_side(up_gate, resid_parts[0], [(send_row(0), cot_cuts[0])])
    feed_parts[0], _ = side_by_side(down, hidden[0][2], [])
    _, [core0] = side_by_side(None, None, [(core, feed_parts[0][1])])
    hidden[1], [got, cot1] = side_by_side(
        up_gate, resid_parts[1], [(chip, far_sum(feed_parts[0][0], core0)), (send_row(1), cot_cuts[1])]
    )
    cot = chunk_order([cot0, cot1])
    output[0], grad0 = feed_rows(0, feed_parts[0][0], core0, got)
    feed_parts[1], [far, near] = side_by_side(down, hidden[1][2], [(chip, grad0), (core, grad0)])
    _, [cross, core1] = side_by_side(None, None, [(core, far), (core, feed_parts[1][1])])
    hidden_grads[0], [got] = side_by_side(
        lambda x: back_down(0, x), [grad0, far, near, cross], [(chip, far_sum(feed_parts[1][0], core1))]
    )
    output[1], grad1 = feed_rows(1, feed_parts[1][0], core1, got)
    output = return_cuts(output)
    resid_grads[0], [far, near, output0] = side_by_side(
        lambda x: back_up_gate(0, *x),
        hidden_grads[0][:2],
        [(chip, grad1), (core, grad1), (return_row(0), output[0])],
    )
    _, [cross, core0] = side_by_side(None, None, [(core, far), (core, resid_grads[0][1])])
    hidden_grads[1], [got, output1] = side_by_side(
        lambda x: back_down(1, x),
        [grad1, far, near, cross],
        [(chip, far_sum(resid_grads[0][0], core0)), (return_row(1), output[1])],
    )
    output = return_order([output0, output1])
    grad_resid[0], grad0 = back_rows(0, resid_grads[0][0], core0, got)

    broad = jnp.concatenate(
        [sum(g[3] for g in hidden_grads), sum(g[5] for g in hidden_grads).reshape(2 * rank, -1)]
    ).astype(BF)
    broad = [x[None] for x in jnp.split(broad, 2, axis=1)]
    step0, step1, step2 = [ctx_step(at) for at in range(3)]

    def grown(value, got):
        return jnp.concatenate([value, got])

    resid_grads[1], [far, near, *got] = side_by_side(
        lambda x: back_up_gate(1, *x),
        hidden_grads[1][:2],
        [(chip, grad0), (core, grad0), (step0, broad[0]), (step0, broad[1])],
    )
    broad = [grown(*pair) for pair in zip(broad, got)]
    own_early, far_early, cuts = column_cuts(
        jnp.concatenate([sum(g[4] for g in hidden_grads), sum(g[2] for g in resid_grads)]), flags["columns"]
    )
    _, [cross, core1, got_early] = side_by_side(
        None, None, [(core, far), (core, resid_grads[1][1]), (core, cuts)]
    )
    own_early = own_early + got_early[0].astype(F32)
    far_early = (far_early + got_early[1].astype(F32)).astype(BF)
    out_grads[0], [got1, got_early, got] = side_by_side(
        lambda x: back_out(0, x),
        [grad0, far, near, cross],
        [(chip, far_sum(resid_grads[1][0], core1)), (chip, far_early), (step1, broad[0])],
    )
    broad[0] = grown(broad[0], got)
    early = (own_early + got_early.astype(F32)).astype(BF)[None]
    grad_resid[1], grad1 = back_rows(1, resid_grads[1][0], core1, got1)
    _, [far, near, got, got_early] = side_by_side(
        None, None, [(chip, grad1), (core, grad1), (step2, broad[0]), (step0, early)]
    )
    broad[0] = grown(broad[0], got)
    early = grown(early, got_early)
    _, [cross] = side_by_side(None, None, [(core, far)])
    out_grads[1] = back_out(1, [grad1, far, near, cross])
    grad_mixed = jnp.concatenate([g[0] for g in out_grads])

    attention_sends = [(step1, broad[1])]
    if simple:
        (query_turned, key_turned, grad_values, inner), [got] = side_by_side(
            lambda x: attention_back(
                queries, key_rows, pre, x, logs, cosine, sine, head_gains, chunks
            ),
            grad_mixed,
            attention_sends,
        )
    else:
        query_turned, key_turned, grad_values, inner = attention_grads(grad_mixed)
        [got] = [send(value) for send, value in attention_sends]
    broad[1] = grown(broad[1], got)
    inners, _ = from_all(inner, [])
    grads, lows, down_late, up_late = qkv_grads(
        [query_turned, key_turned], grad_values, pre, squares, inners, token_parts, qkv_low, own_model, chunks
    )
    partial = jnp.concatenate([down_late, sum(g[2] for g in out_grads)])
    cuts = [lax.dynamic_slice(partial, (jnp.uint32(0), start), (partial.shape[0], wide)) for start in flags["columns"]]

    def rest_of(value):
        for at in range(3, len(ctx_flips())):
            value = grown(value, ctx_step(at)(value))
        if per_sequence > 1:
            value = jnp.sum(value.astype(F32)[gathered_place(ctx, table)], axis=1)
        return value

    def placed(sources, counts, plan, carried=()):
        width = sum(sources[piece[0]].shape[-1] for piece in plan[0][0])
        outs = [shape_of((count, adapters, rank, width), F32) for count in counts]
        return call(
            functools.partial(place_body, rank, len(sources), len(carried), plan),
            (1,),
            [*sources, *carried],
            [whole(x) for x in (*sources, *carried)],
            [(o, whole(o)) for o in outs],
            scalars=[where],
        )

    def place_broad(x):
        return placed([rest_of(value) for value in x], (1, 2), ((((0, 0), (1, 0)),), (((0, 1), (1, 1)), ((0, 2), (1, 2)))))

    sends = [(send, piece.astype(BF)) for send, piece in zip((chip, core, across), cuts[1:])]
    (keep, send), [*got, got_early] = side_by_side(
        lambda x: qkv_back(x, lows, qkv_held, qkv_downs, chunks), grads, sends + [(step1, early)]
    )
    early = grown(early, got_early)
    late = jnp.concatenate(
        [
            cuts[0] + sum(piece.astype(F32) for piece in got),
            up_late.reshape(3 * rank, -1),
            sum(g[1] for g in out_grads),
        ]
    ).astype(BF)[None]
    _, [near_sum, got, got_early] = side_by_side(None, None, [(core, send), (step0, late), (step2, early)])
    early = grown(early, got_early)
    late = jnp.split(grown(late, got), 2, axis=2)
    far = shape_of(grad_resid[0].shape, BF)
    fars = call(
        far_two_body, (1,), [keep, near_sum], [whole(keep), whole(near_sum)], [(far, whole(far))] * chunks
    )
    _, [got0, got_a, got] = side_by_side(
        None, None, [(chip, fars[0]), (step1, late[0]), (step2, broad[1])]
    )
    broad[1] = grown(broad[1], got)
    late[0] = grown(late[0], got_a)
    (grad_down, grad_hidden), [got1, got_a, got_b] = side_by_side(
        place_broad, broad, [(chip, fars[1]), (step2, late[0]), (step1, late[1])]
    )
    late = [grown(late[0], got_a), grown(late[1], got_b)]
    def place_late(x):
        return placed(
            x,
            (6, 5),
            (
                (*[((1, at), (2, at)) for at in (0, 1, 2, 7)], ((0, 1),), ((0, 2),)),
                (*[((1, at), (2, at)) for at in (4, 5, 6, 3)], ((0, 0),)),
            ),
            windows.carried,
        )

    sends, [got_late] = side_by_side(
        lambda x: input_rows(keep, near_sum, x, grad_resid, flags["turn"][0]), [got0, got1], [(step2, late[1])]
    )
    sources = [rest_of(early), rest_of(late[0]), rest_of(grown(late[1], got_late))]
    (grad_wide, grad_model), got = side_by_side(
        place_late, sources, [(return_row(p), rows_back) for p, rows_back in enumerate(sends)]
    )
    input_grad = return_order(got).astype(F32)
    return (output, input_grad, grad_wide, grad_down[0], grad_model, grad_hidden)


def solution(mesh):
    return jax.shard_map(
        on_device,
        mesh=mesh,
        in_specs=(
            P("shard", "ctx", None),
            P("shard", "ctx", None),
            P("shard", None),
            P(None, "shard", None),
            P(None, "shard", None),
            P("shard", None),
            P(None, "shard"),
            P(None, None, None, "shard"),
            P(None, None, "shard"),
            P(None, None, None, "shard"),
            P(None, None, None, "shard"),
        ),
        out_specs=(
            P("shard", "ctx", None),
            P("shard", "ctx", None),
            P(None, None, None, "shard"),
            P(None, None, "shard"),
            P(None, None, None, "shard"),
            P(None, None, None, "shard"),
        ),
        check_vma=False,
    )
```

```python
import functools
import math

import jax
import jax.numpy as jnp
import numpy as np
from jax import lax
from jax.experimental import pallas as pl
from jax.experimental.pallas import tpu as pltpu
from jax.sharding import PartitionSpec as P

D = 2048
HEADS = 16
HD = 128
BLOCK = 256

epsilon = 1e-06
rope_base = 500000.0
far_below = -1e30
BF = jnp.bfloat16
F32 = jnp.float32
VMEM_BYTES = 16 * 2**20


def dot(left, right):
    return lax.dot_general(left, right, (((1,), (0,)), ((), ())), preferred_element_type=F32)


def dot_nt(left, right):
    return lax.dot_general(left, right, (((1,), (1,)), ((), ())), preferred_element_type=F32)


def dot_tn(left, right):
    return lax.dot_general(left, right, (((0,), (0,)), ((), ())), preferred_element_type=F32)


def over_shard(value, flip):
    size = lax.axis_size("shard")
    return lax.ppermute(value, "shard", [(i, i ^ flip) for i in range(size)])


class Windows:
    def __init__(self):
        self.carried = []

    def side_by_side(self, run, inputs, sends):
        values = [value for _, value in sends]
        inputs, values, self.carried = lax.optimization_barrier((inputs, values, self.carried))
        got = [send(value) for (send, _), value in zip(sends, values)]
        out = run(inputs) if run else None
        out, got, self.carried = lax.optimization_barrier((out, got, self.carried))
        return out, got


def over_ctx(value, flip):
    size = lax.axis_size("ctx")
    return lax.ppermute(value, "ctx", [(i, i ^ flip) for i in range(size)])


FLIPS = (0, 2, 1, 3)


def call(body, grid, args, in_specs, outs, scratch=(), scalars=(), flops=0, aliases={}):
    placed = []
    for arg, spec in zip(args, in_specs):
        if spec.memory_space == pltpu.VMEM:
            arg = pltpu.with_memory_space_constraint(arg, pltpu.VMEM)
        elif spec.memory_space == pltpu.HBM:
            arg = pltpu.with_memory_space_constraint(arg, pltpu.HBM)
        placed.append(arg)
    return pl.pallas_call(
        body,
        grid_spec=pltpu.PrefetchScalarGridSpec(
            num_scalar_prefetch=len(scalars),
            grid=grid,
            in_specs=in_specs,
            out_specs=[spec for _, spec in outs],
            scratch_shapes=scratch,
        ),
        out_shape=[shape for shape, _ in outs],
        input_output_aliases=aliases,
        compiler_params=pltpu.CompilerParams(vmem_limit_bytes=VMEM_BYTES),
        cost_estimate=pl.CostEstimate(flops=flops, bytes_accessed=0, transcendentals=0),
    )(*scalars, *placed)


def shape_of(shape, kind):
    return jax.ShapeDtypeStruct(shape, kind)


def whole(value):
    zeros = (0,) * value.ndim
    return pl.BlockSpec(value.shape, lambda *_: zeros)


def spec(block, index):
    return pl.BlockSpec(block, lambda i, *_: index(i))


def column_spec(value, tile):
    zeros = (0,) * (value.ndim - 1)
    return pl.BlockSpec(value.shape[:-1] + (tile,), lambda i, *_: (*zeros, i))


HBM = pl.BlockSpec(memory_space=pltpu.HBM)
ANY = pl.BlockSpec(memory_space=pl.ANY)
VMEM = pl.BlockSpec(memory_space=pltpu.VMEM)


def tile_of(width):
    return min(1024, width)


def run_copies(copies):
    for copy in copies:
        copy.start()
    for copy in copies:
        copy.wait()


def cut_body(first, apart, places, weight, near, *refs):
    fars, sems = refs[:-1], refs[-1]
    step = pl.program_id(0)
    width = near.shape[2]
    slim = fars[0].shape[1]
    rows = pl.ds(pl.multiple_of(places[1] * slim, slim), slim)

    def columns(flip):
        return pl.ds(pl.multiple_of((places[0] ^ flip) * width, width), width)

    def copies(far, cross):
        sources = [(slice(None), columns(1), near), (rows, columns(2), far), (rows, columns(3), cross)]
        return [
            pltpu.make_async_copy(weight.at[first + step, r, c], to.at[0], sems.at[i])
            for i, (r, c, to) in enumerate(sources)
        ]

    if apart:
        for matrix in range(len(fars) // 2):
            pair = fars[2 * matrix : 2 * matrix + 2]
            pl.when(step == matrix)(functools.partial(lambda pair: run_copies(copies(*pair)), pair))
    else:
        run_copies(copies(*fars))


def cut(weight, first, count, places, apart):
    depth, full = weight.shape[1:]
    width, slim = full // 4, depth // 4
    if apart:
        far = (shape_of((1, slim, width), BF), pl.BlockSpec((1, slim, width), lambda *_: (0, 0, 0)))
    else:
        far = (shape_of((count, slim, width), BF), pl.BlockSpec((1, slim, width), lambda m, _: (m, 0, 0)))
    return call(
        functools.partial(cut_body, first, apart),
        (count,),
        [weight],
        [HBM],
        [(shape_of((count, depth, width), BF), pl.BlockSpec((1, depth, width), lambda m, _: (m, 0, 0)))]
        + [far] * (2 * count if apart else 2),
        [pltpu.SemaphoreType.DMA((3,))],
        scalars=[places],
    )


COPIES = 10
PARTS = 8


def copies_of(weight, matrix, near, near_at, parts, at, places, held, sems):
    width = held.shape[1]
    depth = held.shape[0] // 4
    slim = depth // 4
    shard, quarter = places[0], places[1]

    def to(flip, rows, begin=0):
        start = pl.multiple_of((shard ^ flip) * depth + begin, slim)
        return held.at[pl.ds(start, rows), :]

    pairs = []
    if weight is not None:
        own_columns = pl.ds(pl.multiple_of(shard * width, width), width)
        pairs.append((weight.at[matrix, :, own_columns], to(0, depth)))
    if near is not None:
        pairs.append((near.at[near_at], to(1, depth)))
    for i, part in enumerate(parts):
        if part is not None:
            pairs.append((part.at[at], to(2 + i % 2, slim, (quarter ^ (i // 2)) * slim)))
    return [pltpu.make_async_copy(source, target, sems.at[i]) for i, (source, target) in enumerate(pairs)]


DONE = (shape_of((8, 128), F32), pl.BlockSpec((8, 128), lambda *_: (0, 0)))


def load_plain_body(attn, down, out_held, down_held, done, sems):
    run_copies(
        [
            pltpu.make_async_copy(attn.at[attn.shape[0] - 1], out_held, sems.at[0]),
            pltpu.make_async_copy(down, down_held, sems.at[1]),
        ]
    )
    done[...] = jnp.zeros_like(done)


def load_plain(w_attn, w_down):
    return call(
        load_plain_body,
        (1,),
        [w_attn, w_down],
        [HBM] * 2,
        [(pltpu.VMEM(w_attn.shape[1:], BF), VMEM), (pltpu.VMEM(w_down.shape, BF), VMEM), DONE],
        [pltpu.SemaphoreType.DMA((2,))],
    )


def load_body(first, there, places, *refs):
    refs = list(refs)
    weight, near = (refs.pop(0), refs.pop(0)) if first else (None, None)
    parts = [[refs.pop(0) if is_there else None for is_there in matrix] for matrix in there]
    held, done, sems = refs[-3:]
    copies = []
    for m, matrix_parts in enumerate(parts):
        copies += copies_of(weight, m, near, m, matrix_parts, 0, places, held.at[m], sems.at[m])
    run_copies(copies)
    done[...] = jnp.zeros_like(done)


def load(parts, places, weight=None, near=None, held=None):
    there = [[part is not None for part in matrix] for matrix in parts]
    arrays = [part for matrix in parts for part in matrix if part is not None]
    arrays = ([weight, near] if held is None else []) + arrays
    depth, full = (weight if held is None else held).shape[1:]
    shape = (2, 4 * depth, full // 4) if held is None else held.shape
    return call(
        functools.partial(load_body, held is None, there),
        (1,),
        arrays + ([] if held is None else [held]),
        ([HBM] + [ANY] * (len(arrays) - 1) if held is None else [ANY] * len(arrays) + [VMEM]),
        [(pltpu.VMEM(shape, BF), VMEM), DONE],
        [pltpu.SemaphoreType.DMA((2, COPIES))],
        [places],
        aliases={} if held is None else {1 + len(arrays): 0},
    )


def row_of(column):
    return jnp.transpose(jnp.broadcast_to(column, (column.shape[0], 128)))[:8]


def column_of(row):
    return jnp.transpose(jnp.broadcast_to(row[:1], (128, row.shape[1])))[:, :1]


def qkv_body(chunks, size, places, *refs):
    x_refs, refs = refs[:3], refs[3:]
    weight, near, weight_parts, refs = refs[0], refs[1], refs[2 : 2 + PARTS], refs[2 + PARTS :]
    down, up, pre, low, sums, kept, held, rows, sems, keep_sems = refs
    step = pl.program_id(0)

    def copies(p):
        return copies_of(weight, p, near, p, weight_parts, p, places, held.at[p], sems.at[p])

    @pl.when(step == 0)
    def _():
        for p in range(held.shape[0]):
            for copy in copies(p):
                copy.start()
        for h in range(chunks):
            rows[4 * h * size : 4 * (h + 1) * size] = load_parts(x_refs, h * size, size)

    lowrank = dot_nt(rows[...], down[...]).astype(BF)
    for copy in copies(step):
        copy.wait()
    keep = [pltpu.make_async_copy(held.at[p], kept.at[p], keep_sems.at[p]) for p in range(held.shape[0])]
    for p, copy in enumerate(keep):
        pl.when(step == p)(copy.start)
    value = dot(rows[...], held[step]) + dot(lowrank, up[0])
    pre[0] = value.astype(BF)
    low[0] = lowrank
    sums[...] = row_of(jnp.sum(value * value, axis=1, keepdims=True))

    @pl.when(step == held.shape[0] - 1)
    def _():
        for copy in keep:
            copy.wait()


def qkv_forward(x_parts, chunks, size, weight, weight_parts, places, downs, ups):
    count, depth, width = weight_parts[0].shape
    full = x_parts[0].shape[1]
    total, rank = 4 * chunks * size, ups.shape[1]
    return call(
        functools.partial(qkv_body, chunks, size),
        (count,),
        [*x_parts, weight, *weight_parts, downs, ups],
        [whole(x) for x in x_parts]
        + [HBM] * (2 + PARTS)
        + [
            spec((rank, full), lambda p: (p, 0)),
            spec((1, rank, width), lambda p: (p, 0, 0)),
        ],
        [
            (shape_of((count, total, width), BF), spec((1, total, width), lambda p: (p, 0, 0))),
            (shape_of((count, total, rank), BF), spec((1, total, rank), lambda p: (p, 0, 0))),
            (shape_of((8 * count, total), F32), spec((8, total), lambda p: (p, 0))),
            (pltpu.HBM((count, full, width), BF), HBM),
        ],
        [
            pltpu.VMEM((count, full, width), BF),
            pltpu.VMEM((total, full), BF),
            pltpu.SemaphoreType.DMA((count, COPIES)),
            pltpu.SemaphoreType.DMA((count,)),
        ],
        [places],
        flops=2 * total * full * width * count,
    )


def aligned_sums(refs, which, chunks):
    total = refs[0].shape[1]
    block = total // (4 * chunks)
    out = 0.0
    for flip, ref in zip(FLIPS, refs):
        column = column_of(ref[8 * which : 8 * which + 8])
        if flip:
            order = [FLIPS.index(f ^ flip) for f in FLIPS]
            column = jnp.concatenate(
                [
                    column[(4 * h + i) * block : (4 * h + i + 1) * block]
                    for h in range(chunks)
                    for i in order
                ]
            )
        out = out + column
    return out


def attention_body(chunks, factor, *refs):
    (
        query_pre, key_pre, value, own, far, near, cross, cosine, sine, gains,
        query_out, key_out, mixed_out, logs_out, scale_rows,
    ) = refs
    total = query_pre.shape[1]
    size = total // chunks

    @pl.when(pl.program_id(0) == 0)
    def _():
        for p in range(2):
            sums = aligned_sums((own, far, near, cross), p, chunks)
            scale_rows[p] = jnp.broadcast_to(lax.rsqrt(sums / D + epsilon), (total, HD))

    def prepared(pre, p):
        value = pre[0].astype(F32) * scale_rows[p] * gains[p : p + 1]
        return (value * cosine[...] + pltpu.roll(value, HD // 2, 1) * sine[...]).astype(BF)

    query, key = prepared(query_pre, 0), prepared(key_pre, 1)
    query_out[...] = query
    key_out[...] = key
    logs = []
    for h in range(chunks):
        seen = (h + 1) * size
        scores = dot_nt(query[h * size : (h + 1) * size], key[:seen]) * factor
        top = jnp.max(scores, axis=1, keepdims=True)
        weights = jnp.exp(scores - top)
        sums = jnp.sum(weights, axis=1, keepdims=True)
        probs = (weights * (1.0 / sums)).astype(BF)
        mixed_out[h * size : (h + 1) * size] = dot(probs, value[0, :seen]).astype(BF)
        logs.append(top + jnp.log(sums))
    logs_out[...] = row_of(jnp.concatenate(logs))


def attention_forward(pre, sums, cosine, sine, gains, chunks):
    _, total, width = pre.shape
    heads = width // HD
    factor = 1.0 / math.sqrt(HD)

    def head(p):
        return spec((1, total, HD), lambda i: (p, 0, i))

    by_head = spec((total, HD), lambda i: (0, i))
    return call(
        functools.partial(attention_body, chunks, factor),
        (heads,),
        [pre, pre, pre, *sums, cosine, sine, gains],
        [head(0), head(1), head(2)]
        + [whole(s) for s in sums]
        + [whole(cosine), whole(sine), spec((gains.shape[0], HD), lambda i: (0, i))],
        [
            (shape_of((total, width), BF), by_head),
            (shape_of((total, width), BF), by_head),
            (shape_of((total, width), BF), by_head),
            (shape_of((8 * heads, total), F32), spec((8, total), lambda i: (i, 0))),
        ],
        [pltpu.VMEM((2, total, HD), F32)],
        flops=4 * total * total * width,
    )


def attention_back_body(chunks, factor, *refs):
    (
        query_in, key_in, query_pre, key_pre, value, grad_in, logs, cosine, sine, gains,
        query_out, key_out, value_out, inner_out, inner_rows,
    ) = refs
    total = query_in.shape[0]
    size = total // chunks
    head = pl.program_id(0)
    query, key, values, grad = query_in[...], key_in[...], value[0], grad_in[...]
    log_column = column_of(logs[...])
    grad_key = [0.0] * chunks
    grad_value = [0.0] * chunks
    grad_query = []
    for h in range(chunks):
        rows = slice(h * size, (h + 1) * size)
        grad_row = 0.0
        delta = 0.0
        kept = []
        for k in range(h + 1):
            keys = slice(k * size, (k + 1) * size)
            scores = dot_nt(query[rows], key[keys]) * factor
            probs = jnp.exp(scores - log_column[rows])
            grad_probs = dot_nt(grad[rows], values[keys])
            delta = delta + jnp.sum(probs * grad_probs, axis=1, keepdims=True)
            kept.append((probs, grad_probs))
        for k, (probs, grad_probs) in enumerate(kept):
            keys = slice(k * size, (k + 1) * size)
            grad_scores = (probs * (grad_probs - delta)).astype(BF)
            grad_row = grad_row + dot(grad_scores, key[keys])
            grad_key[k] = grad_key[k] + dot_tn(grad_scores, query[rows])
            grad_value[k] = grad_value[k] + dot_tn(probs.astype(BF), grad[rows])
        grad_query.append(grad_row)

    value_out[...] = jnp.concatenate(grad_value).astype(BF)
    for p, (pre, grads, out) in enumerate(
        ((query_pre, grad_query, query_out), (key_pre, grad_key, key_out))
    ):
        turned = jnp.concatenate(grads) * factor
        turned = turned * cosine[...] - pltpu.roll(turned, HD // 2, 1) * sine[...]
        turned = turned * gains[p : p + 1]
        out[...] = turned.astype(BF)
        inner = jnp.sum(turned * pre[0].astype(F32), axis=1, keepdims=True)
        inner = jnp.broadcast_to(inner, (total, 128))

        @pl.when(head == 0)
        def _():
            inner_rows[p] = inner

        @pl.when(head > 0)
        def _():
            inner_rows[p] += inner

    @pl.when(head == pl.num_programs(0) - 1)
    def _():
        for p in range(2):
            inner_out[8 * p : 8 * p + 8] = jnp.transpose(inner_rows[p])[:8]


def attention_back(queries, key_rows, pre, grad_mixed, logs, cosine, sine, gains, chunks):
    _, total, width = pre.shape
    heads = width // HD
    factor = 1.0 / math.sqrt(HD)

    def head(p):
        return spec((1, total, HD), lambda i: (p, 0, i))

    by_head = spec((total, HD), lambda i: (0, i))
    return call(
        functools.partial(attention_back_body, chunks, factor),
        (heads,),
        [queries, key_rows, pre, pre, pre, grad_mixed, logs, cosine, sine, gains],
        [by_head, by_head, head(0), head(1), head(2), by_head]
        + [spec((8, total), lambda i: (i, 0)), whole(cosine), whole(sine)]
        + [spec((gains.shape[0], HD), lambda i: (0, i))],
        [
            (shape_of((total, width), BF), by_head),
            (shape_of((total, width), BF), by_head),
            (shape_of((total, width), BF), by_head),
            (shape_of((16, total), F32), pl.BlockSpec((16, total), lambda *_: (0, 0))),
        ],
        [pltpu.VMEM((2, total, 128), F32)],
        flops=10 * total * total * width,
    )


def split_out(value, keep, send):
    if keep.ndim == 2:
        half = value.shape[0] // 2
        keep[...] = value[:half].astype(BF)
        send[...] = value[half:].astype(BF)
        return
    half = keep.shape[1]
    for h in range(keep.shape[0]):
        keep[h] = value[2 * h * half : (2 * h + 1) * half].astype(BF)
        send[h] = value[(2 * h + 1) * half : (2 * h + 2) * half].astype(BF)


def qkv_grads_body(chunks, *refs):
    query_grad, key_grad, value_grad, query_pre, key_pre = refs[:5]
    squares, inners, x_refs = refs[5:9], refs[9:13], refs[13:16]
    low, ups, grads, lows, down_out, up_out = refs[16:]
    rank = ups.shape[1]
    total = query_grad.shape[0]
    for p, (grad, pre) in enumerate(((query_grad, query_pre), (key_grad, key_pre))):
        scale = lax.rsqrt(aligned_sums(squares, p, chunks) / D + epsilon)
        inner = aligned_sums(inners, p, chunks) * (scale * scale * scale / D)
        grads[p] = (grad[...].astype(F32) * scale - pre[0].astype(F32) * inner).astype(BF)
    grads[2] = value_grad[...]
    for p in range(3):
        lows[:, p * rank : (p + 1) * rank] = dot_nt(grads[p], ups[p]).astype(BF)
        up_out[p] = dot_tn(low[p], grads[p])
    size = total // chunks
    down = 0.0
    for h in range(chunks):
        x = load_parts(x_refs, h * size // 4, size // 4)
        down += dot_tn(lows[h * size : (h + 1) * size], x)
    down_out[...] = down


def qkv_grads(turned, grad_values, pre, squares, inners, x_parts, low, ups, chunks):
    count, total, width = pre.shape
    rank = ups.shape[1]
    full = x_parts[0].shape[1]

    def pre_rows(p):
        return pl.BlockSpec((1, total, width), lambda *_: (p, 0, 0))

    outs = [
        shape_of((count, total, width), BF),
        shape_of((total, count * rank), BF),
        shape_of((count * rank, full), F32),
        shape_of((count, rank, width), F32),
    ]
    return call(
        functools.partial(qkv_grads_body, chunks),
        (1,),
        [*turned, grad_values, pre, pre, *squares, *inners, *x_parts, low, ups],
        [whole(turned[0]), whole(turned[1]), whole(grad_values), pre_rows(0), pre_rows(1)]
        + [whole(v) for v in (*squares, *inners, *x_parts, low)]
        + [pl.BlockSpec((count, rank, width), lambda *_: (0, 0, 0))],
        [(o, whole(o)) for o in outs],
        flops=2 * total * width * 512,
    )


def qkv_back_body(grads, lows, weight, downs, keep, send):
    value = dot(lows[...], downs[...])
    for p in range(3):
        value += dot_nt(grads[p], weight[p])
    split_out(value, keep, send)


def qkv_back(grads, lows, weight, downs, chunks):
    count, full, width = weight.shape
    total = grads.shape[1]
    tile = tile_of(full)
    half = total // chunks // 2
    part = (shape_of((chunks, half, full), BF), spec((chunks, half, tile), lambda i: (0, 0, i)))
    return call(
        qkv_back_body,
        (full // tile,),
        [grads, lows, weight, downs],
        [
            whole(grads),
            whole(lows),
            spec((count, tile, width), lambda i: (0, i, 0)),
            spec((downs.shape[0], tile), lambda i: (0, i)),
        ],
        [part, part],
        flops=2 * total * full * width * count,
    )


def partial_body(streamed, beside, x, weight, down, up, *refs):
    keep, send, low, *scratch = refs[beside:]
    step = pl.program_id(0)
    tile = keep.shape[1]

    def columns(i):
        return pl.ds(pl.multiple_of(i * tile, tile), tile)

    def copy(i):
        held, sems = scratch
        return pltpu.make_async_copy(weight.at[:, columns(i)], held.at[:, columns(i)], sems.at[i])

    @pl.when(step == 0)
    def _():
        if streamed:
            for i in range(weight.shape[1] // tile):
                copy(i).start()
        low[...] = dot_nt(x[...], down[...]).astype(BF)

    if streamed:
        copy(step).wait()
        held = scratch[0]
    else:
        held = weight
    split_out(dot(x[...], held[:, columns(step)]) + dot(low[...], up[...]), keep, send)


def partial_forward(x, chunk, chunks, weight, down, up, streamed, beside=()):
    total, depth = x.shape
    size = total // chunks
    full = weight.shape[-1]
    tile = tile_of(full)
    half = size // 2
    rank = down.shape[0]
    scratch = [pltpu.VMEM(weight.shape, BF), pltpu.SemaphoreType.DMA((full // tile,))]
    return call(
        functools.partial(partial_body, streamed, len(beside)),
        (full // tile,),
        [x, weight, down, up, *beside],
        [
            pl.BlockSpec((size, depth), lambda *_: (chunk, 0)),
            HBM if streamed else VMEM,
            whole(down),
            spec((rank, tile), lambda i: (0, i)),
            *[VMEM] * len(beside),
        ],
        [
            (shape_of((half, full), BF), spec((half, tile), lambda i: (0, i))),
            (shape_of((half, full), BF), spec((half, tile), lambda i: (0, i))),
            (shape_of((size, rank), BF), pl.BlockSpec((size, rank), lambda *_: (0, 0))),
        ],
        scratch if streamed else (),
        flops=2 * size * depth * full,
    )


def gate_up_body(*refs):
    x_refs, (weight, downs, ups, gate, upper, act, low, rows) = refs[:4], refs[4:]
    rank = ups.shape[1]
    tile = gate.shape[1]
    step = pl.program_id(0)

    @pl.when(step == 0)
    def _():
        rows[...] = load_parts(x_refs)
        low[...] = dot_nt(rows[...], downs[...]).astype(BF)

    columns = pl.ds(pl.multiple_of(step * tile, tile), tile)
    gate_pre = dot(rows[...], weight[0, :, columns]) + dot(low[:, :rank], ups[0])
    upper_pre = dot(rows[...], weight[1, :, columns]) + dot(low[:, rank:], ups[1])
    gate[...] = gate_pre.astype(BF)
    upper[...] = upper_pre.astype(BF)
    act[...] = (gate_pre * jax.nn.sigmoid(gate_pre) * upper_pre).astype(BF)


def gate_up_forward(x_parts, weight, downs, ups):
    _, full, width = weight.shape
    size = 4 * x_parts[0].shape[0]
    rank = ups.shape[1]
    tile = tile_of(width)
    out = (shape_of((size, width), BF), spec((size, tile), lambda i: (0, i)))
    return call(
        gate_up_body,
        (width // tile,),
        [*x_parts, weight, downs, ups],
        [whole(x) for x in x_parts] + [VMEM, whole(downs), spec((2, rank, tile), lambda i: (0, 0, i))],
        [
            out,
            out,
            out,
            (shape_of((size, 2 * rank), BF), pl.BlockSpec((size, 2 * rank), lambda *_: (0, 0))),
        ],
        [pltpu.VMEM((size, full), BF)],
        flops=4 * size * full * width,
    )


def feed_back_body(*refs):
    g_refs = refs[:4]
    weight, down, gate, upper, gate_low, feed_low, feed_up, ups, _ = refs[4:13]
    gate_grad, upper_grad, low_out, down_a, feed_b, hidden_b, rows, low, lows = refs[13:]
    rank = down.shape[0]
    step = pl.program_id(0)
    @pl.when(step == 0)
    def _():
        rows[...] = load_parts(g_refs)
        low[...] = dot_nt(rows[...], feed_up[...]).astype(BF)
        feed_b[...] = dot_tn(feed_low[...], rows[...])
        lows[...] = jnp.zeros_like(lows)

    tile = gate.shape[1]
    held_rows = pl.ds(pl.multiple_of(step * tile, tile), tile)
    grad_act = dot_nt(rows[...], weight[held_rows]) + dot(low[...], down[...])
    gate_pre, upper_pre = gate[...].astype(F32), upper[...].astype(F32)
    sig = jax.nn.sigmoid(gate_pre)
    silu = gate_pre * sig
    down_a[...] = dot_tn(low[...], (silu * upper_pre).astype(BF))
    grad_upper = (grad_act * silu).astype(BF)
    grad_gate = (grad_act * upper_pre * (sig + silu * (1.0 - sig))).astype(BF)
    gate_grad[...] = grad_gate
    upper_grad[...] = grad_upper
    hidden_b[0] = dot_tn(gate_low[:, :rank], grad_gate)
    hidden_b[1] = dot_tn(gate_low[:, rank:], grad_upper)
    lows[:, :rank] += dot_nt(grad_gate, ups[0])
    lows[:, rank:] += dot_nt(grad_upper, ups[1])

    @pl.when(step == pl.num_programs(0) - 1)
    def _():
        low_out[...] = lows[...].astype(BF)


def feed_back(g_parts, weight, down, gate, upper, gate_low, feed_low, feed_up, ups, beside):
    width, depth = weight.shape
    size = 4 * g_parts[0].shape[0]
    rank = down.shape[0]
    tile = tile_of(width)
    by_tile = spec((size, tile), lambda i: (0, i))
    return call(
        feed_back_body,
        (width // tile,),
        [*g_parts, weight, down, gate, upper, gate_low, feed_low, feed_up, ups, beside],
        [whole(g) for g in g_parts]
        + [
            VMEM,
            spec((rank, tile), lambda i: (0, i)),
            by_tile,
            by_tile,
            whole(gate_low),
            whole(feed_low),
            whole(feed_up),
            spec((2, rank, tile), lambda i: (0, 0, i)),
            VMEM,
        ],
        [
            (shape_of((size, width), BF), by_tile),
            (shape_of((size, width), BF), by_tile),
            (shape_of((size, 2 * rank), BF), pl.BlockSpec((size, 2 * rank), lambda *_: (0, 0))),
            (shape_of((rank, width), F32), spec((rank, tile), lambda i: (0, i))),
            (shape_of((rank, depth), F32), pl.BlockSpec((rank, depth), lambda *_: (0, 0))),
            (shape_of((2, rank, width), F32), spec((2, rank, tile), lambda i: (0, 0, i))),
        ],
        [
            pltpu.VMEM((size, depth), BF),
            pltpu.VMEM((size, rank), BF),
            pltpu.VMEM((size, 2 * rank), F32),
        ],
        flops=2 * size * depth * width,
    )


def gate_up_back_body(gate_grad, upper_grad, weight, low, downs, *refs):
    x_refs, (keep, send, down_out) = refs[:4], refs[4:]
    tile = keep.shape[1]
    held_rows = pl.ds(pl.multiple_of(pl.program_id(0) * tile, tile), tile)
    value = dot_nt(gate_grad[...], weight[0, held_rows]) + dot_nt(upper_grad[...], weight[1, held_rows])
    split_out(value + dot(low[...], downs[...]), keep, send)
    down_out[...] = dot_tn(low[...], load_parts(x_refs))


def gate_up_back(gate_grad, upper_grad, weight, low, downs, x_parts):
    _, full, width = weight.shape
    size = gate_grad.shape[0]
    half = size // 2
    ranks = downs.shape[0]
    tile = tile_of(full)
    return call(
        gate_up_back_body,
        (full // tile,),
        [gate_grad, upper_grad, weight, low, downs, *x_parts],
        [whole(gate_grad), whole(upper_grad), VMEM, whole(low), spec((ranks, tile), lambda i: (0, i))]
        + [column_spec(x, tile) for x in x_parts],
        [
            (shape_of((half, full), BF), spec((half, tile), lambda i: (0, i))),
            (shape_of((half, full), BF), spec((half, tile), lambda i: (0, i))),
            (shape_of((ranks, full), F32), spec((ranks, tile), lambda i: (0, i))),
        ],
        flops=4 * size * full * width,
    )


def out_back_body(*refs):
    g_refs = refs[:4]
    weight, down, up, mixed, low, grad_mixed, down_out, up_out, rows, grad_low = refs[4:]

    @pl.when(pl.program_id(0) == 0)
    def _():
        rows[...] = load_parts(g_refs)
        grad_low[...] = dot_nt(rows[...], up[...]).astype(BF)
        up_out[...] = dot_tn(low[...], rows[...])

    tile = grad_mixed.shape[1]
    held_rows = pl.ds(pl.multiple_of(pl.program_id(0) * tile, tile), tile)
    grad_mixed[...] = (dot_nt(rows[...], weight[held_rows]) + dot(grad_low[...], down[...])).astype(BF)
    down_out[...] = dot_tn(grad_low[...], mixed[...])


def out_back(g_parts, weight, down, up, mixed, low, chunk):
    width, depth = weight.shape
    size = 4 * g_parts[0].shape[0]
    rank = down.shape[0]
    tile = min(256, width)
    return call(
        out_back_body,
        (width // tile,),
        [*g_parts, weight, down, up, mixed, low],
        [whole(g) for g in g_parts]
        + [
            VMEM,
            spec((rank, tile), lambda i: (0, i)),
            whole(up),
            spec((size, tile), lambda i: (chunk, i)),
            whole(low),
        ],
        [
            (shape_of((size, width), BF), spec((size, tile), lambda i: (0, i))),
            (shape_of((rank, width), F32), spec((rank, tile), lambda i: (0, i))),
            (shape_of((rank, depth), F32), pl.BlockSpec((rank, depth), lambda *_: (0, 0))),
        ],
        [pltpu.VMEM((size, depth), BF), pltpu.VMEM((size, rank), BF)],
        flops=2 * size * depth * width,
    )


def load_parts(refs, first=0, count=None, columns=slice(None)):
    own, far, *near = refs
    if len(near) == 1:
        near = near[0].at[0], near[0].at[1]
    rows = slice(first, own.shape[0] if count is None else first + count)
    return jnp.concatenate([ref[rows, columns] for ref in (own, far, *near)])


def ctx_flips():
    size = lax.axis_size("ctx")
    return [flip for flip in (2, 4, 8, 16, 1) if flip < size]


def ctx_step(at):
    return lambda value: over_ctx(value, ctx_flips()[at])


def gathered_place(ctx, other):
    place = 0
    for at, flip in enumerate(ctx_flips()):
        place = place + (((ctx ^ other) // flip) % 2) * 2**at
    return place


def column_cuts(partial, starts):
    width = partial.shape[-1] // 4
    zero = jnp.uint32(0)
    blocks = [lax.dynamic_slice(partial, (zero, start), (partial.shape[0], width)) for start in starts]
    return blocks[0], blocks[1], jnp.stack(blocks[2:]).astype(BF)


def natural(parts, shard):
    out = []
    for index in range(4):
        value = parts[0]
        for flip, part in zip(FLIPS[1:], parts[1:]):
            value = jnp.where((shard ^ flip) == index, part, value)
        out.append(value)
    return out


def row_sum(keep, near, got):
    rows = got.shape[-2]
    own = (slice(None),) * (len(keep.shape) - 2) + (slice(0, rows),)
    return keep[own].astype(F32) + near[own].astype(F32) + got[...].astype(F32)


def rms_scale(value):
    return lax.rsqrt(jnp.mean(value * value, axis=-1, keepdims=True) + epsilon)


def rms_back(value, scale, gain, grad):
    weighted = grad * gain
    return scale * weighted - value * (
        scale * scale * scale * jnp.mean(value * weighted, axis=-1, keepdims=True)
    )


def far_body(keep, near, far):
    rows = far.shape[-2]
    below = (slice(None),) * (len(keep.shape) - 2) + (slice(rows, 2 * rows),)
    far[...] = (keep[below].astype(F32) + near[below].astype(F32)).astype(BF)


def attention_rows_body(keep, near, got, token, gain, value_out, resid_out, low_out):
    value = row_sum(keep, near, got)
    resid = token[...].astype(F32) + value * rms_scale(value) * gain[...]
    value_out[...] = value
    resid_out[...] = resid
    low_out[...] = resid.astype(BF)


def feed_rows_body(keep, near, got, resid, cot, gain, output, grad):
    value = row_sum(keep, near, got)
    scale = rms_scale(value)
    output[...] = (resid[...] + value * scale * gain[...]).astype(BF)
    grad[...] = rms_back(value, scale, gain[...], cot[...].astype(F32)).astype(BF)


def back_rows_body(keep, near, got, value, cot, gain, grad_out, low_out):
    grad = cot[...].astype(F32) + row_sum(keep, near, got)
    grad_out[...] = grad
    value = value[...]
    low_out[...] = rms_back(value, rms_scale(value), gain[...], grad).astype(BF)


def far_two_body(keep, near, *fars):
    for h, far in enumerate(fars):
        far_body(keep.at[h], near.at[h], far)


def input_rows_body(order, keep, near, *refs):
    chunks = keep.shape[0]
    gots, resids, outs = refs[:chunks], refs[chunks : 2 * chunks], refs[2 * chunks :]
    rows = [
        (row_sum(keep.at[h], near.at[h], gots[h]) + resids[h][...]).astype(BF) for h in range(chunks)
    ]

    @pl.when(order[0] == 0)
    def _():
        for out, row in zip(outs, rows):
            out[...] = row

    @pl.when(order[0] != 0)
    def _():
        for out, row in zip(outs, rows[::-1]):
            out[...] = row


def input_rows(keep, near, gots, resids, order):
    args = [keep, near, *gots, *resids]
    outs = [shape_of(resid.shape, BF) for resid in resids]
    return call(
        input_rows_body, (1,), args, [whole(x) for x in args], [(o, whole(o)) for o in outs], scalars=[order]
    )


def order_body(spot, *refs):
    gots, out = refs[:-1], refs[-1]
    for turn in range(len(gots)):

        @pl.when(spot[0] == turn)
        def _():
            for j in range(len(gots)):
                out[j] = gots[(j - turn) % len(gots)][...].astype(F32)


def order_rows(gots, spot):
    out = shape_of((len(gots), *gots[0].shape), F32)
    return call(order_body, (1,), gots, [whole(x) for x in gots], [(out, whole(out))], scalars=[spot])[0]


def by_rows(body, args, kinds):
    *lead, rows, width = args[0].shape
    outs = [shape_of((*lead, rows // 2, width), kind) for kind in kinds]
    return call(body, (1,), args, [whole(x) for x in args], [(o, whole(o)) for o in outs])


def rotate(value, cosine, sine):
    half = value.shape[-1] // 2
    turned = jnp.concatenate([value[..., half:], value[..., :half]], axis=-1)
    return value * cosine[:, None, :] + turned * sine[:, None, :]


def realign(value, flip, chunks):
    shape = value.shape
    value = value.reshape(shape[0], chunks, 2, 2, -1)
    if flip & 1:
        value = value[:, :, ::-1]
    if flip & 2:
        value = value[:, :, :, ::-1]
    return value.reshape(shape)


def group_of(sequence, part, per_sequence, ctx_size):
    if per_sequence > 1:
        return sequence * per_sequence + part
    depth = sequence % (ctx_size // 2)
    return 2 * depth + (depth + sequence // (ctx_size // 2)) % 2


def sequence_of(ctx, per_sequence, ctx_size):
    if per_sequence > 1:
        return ctx // per_sequence, ctx % per_sequence
    depth = ctx // 2
    return depth + ctx_size // 2 * ((ctx + depth) % 2), 0 * ctx


def wide_attention(pre, sums, cosine, sine, gains, chunks, positions, groups):
    _, total, width = pre.shape
    heads = width // HD
    pre = pre.astype(F32)
    squares = sum(realign(s[::8], flip, chunks) for flip, s in zip(FLIPS, sums))
    scales = lax.rsqrt(squares[:2] / D + epsilon)[:, :, None]

    def as_heads(value):
        return value.reshape(total, heads, HD)

    queries, key_rows = [
        rotate(as_heads(pre[p] * scales[p] * gains[p]), cosine, sine).astype(BF) for p in range(2)
    ]

    def over_sequence(value):
        return lax.all_gather(value, "ctx", axis=0, tiled=True, axis_index_groups=groups)

    key_all, value_all = over_sequence(key_rows), over_sequence(as_heads(pre[2].astype(BF)))
    visible = over_sequence(positions // BLOCK)[None, :] <= (positions // BLOCK)[:, None]
    factor = 1.0 / math.sqrt(HD)
    scores = jnp.einsum("qhd,khd->hqk", queries, key_all, preferred_element_type=F32) * factor
    scores = jnp.where(visible, scores, far_below)
    weights = jnp.exp(scores - jnp.max(scores, axis=-1, keepdims=True))
    probs = weights / jnp.sum(weights, axis=-1, keepdims=True)
    mixed = jnp.einsum("hqk,khd->qhd", probs.astype(BF), value_all, preferred_element_type=F32)
    mixed = mixed.astype(BF).reshape(total, width)

    def back(grad_mixed):
        grad = as_heads(grad_mixed)
        grad_probs = jnp.einsum("qhd,khd->hqk", grad, value_all, preferred_element_type=F32)
        delta = jnp.sum(probs * grad_probs, axis=-1, keepdims=True)
        grad_scores = (probs * (grad_probs - delta)).astype(BF)
        grad_queries = jnp.einsum("hqk,khd->qhd", grad_scores, key_all, preferred_element_type=F32)
        grad_keys = jnp.einsum("hqk,qhd->khd", grad_scores, queries, preferred_element_type=F32)
        grad_values = jnp.einsum("hqk,qhd->khd", probs.astype(BF), grad, preferred_element_type=F32)
        grad_keys, grad_values = [
            lax.psum_scatter(
                g.astype(BF), "ctx", scatter_dimension=0, tiled=True, axis_index_groups=groups
            ).astype(F32)
            for g in (grad_keys * factor, grad_values)
        ]
        turned = [
            rotate(g, cosine, -sine).reshape(total, width) * gains[p]
            for p, g in enumerate((grad_queries * factor, grad_keys))
        ]
        inner = jnp.stack([jnp.sum(turned[p] * pre[p], axis=-1) for p in range(2)])
        inner = jnp.repeat(inner, 8, axis=0)
        values = grad_values.reshape(total, width).astype(BF)
        return turned[0].astype(BF), turned[1].astype(BF), values, inner

    return mixed, back


def choose_body(place, wide, down, model, hidden, gains, wide_out, down_out, model_out, hidden_out, small, sems):
    at = place[0]
    sources = [(wide.at[:, at], wide_out), (down.at[at], down_out)]
    sources += [(model.at[:, at], model_out), (hidden.at[:, at], hidden_out)]
    run_copies([pltpu.make_async_copy(source, to, sems.at[i]) for i, (source, to) in enumerate(sources)])
    rank, width = wide_out.shape[1:]
    shared = [wide_out[p] for p in (0, 1, 2, 4, 5)] + [model_out[p] for p in (3, 4)]
    last = jnp.concatenate([gains[2:], jnp.zeros((rank - 2, width), BF)])
    for at, value in enumerate([*shared, last]):
        column = at // 2 * width
        small[at % 2 * rank : (at % 2 + 1) * rank, column : column + width] = value


def choose(place, a_wide, a_down, b_model, b_hidden, gains):
    rank, width = a_wide.shape[2:]
    shapes = [a_wide.shape[:1] + a_wide.shape[2:], a_down.shape[1:]]
    shapes += [b_model.shape[:1] + b_model.shape[2:], b_hidden.shape[:1] + b_hidden.shape[2:]]
    shapes.append((2 * rank, 4 * width))
    outs = [shape_of(s, BF) for s in shapes]
    return call(
        choose_body,
        (1,),
        [a_wide, a_down, b_model, b_hidden, gains],
        [HBM] * 4 + [whole(gains)],
        [(o, whole(o)) for o in outs],
        [pltpu.SemaphoreType.DMA((4,))],
        scalars=[place],
    )


def place_body(rank, count, unused, plan, at, *refs):
    sources, outs = refs[:count], refs[count + unused :]
    for out, maps in zip(outs, plan):
        for n in range(out.shape[1]):
            for p, pieces in enumerate(maps):
                begin = 0
                for source, place in pieces:
                    value = sources[source][at[n], place * rank : (place + 1) * rank].astype(F32)
                    out[p, n, :, begin : begin + value.shape[-1]] = value
                    begin += value.shape[-1]


def on_device(
    tokens,
    cotangent,
    adapter_index,
    w_attn,
    w_gate_up,
    w_down,
    gains,
    a_wide,
    a_down,
    b_model,
    b_hidden,
):
    seqs, rows = tokens.shape[0], tokens.shape[1]
    shards, ctxs = lax.axis_size("shard"), lax.axis_size("ctx")
    shard, ctx = lax.axis_index("shard"), lax.axis_index("ctx")
    batch = seqs * shards
    per_sequence = ctxs // batch
    group_rows = batch * rows
    chunks = seqs
    chunk_rows = shards * rows
    wide = HEADS // shards * HD
    adapters, rank = a_down.shape[:2]

    groups = [[group_of(q, k, per_sequence, ctxs) for k in range(per_sequence)] for q in range(batch)]
    my_sequence, my_part = sequence_of(ctx, per_sequence, ctxs)
    my_slot = my_sequence % seqs
    my_spot = (ctx % batch) // shards

    pairs = []
    for p in range(seqs):
        pairs.append([])
        for c in range(ctxs):
            for s in range(shards):
                k, local = c // batch, c % batch
                spot, owner = local // shards, local % shards
                to = groups[seqs * s + (p + spot) % seqs][k]
                pairs[p].append((c * shards + s, to * shards + owner))

    windows = Windows()
    side_by_side = windows.side_by_side

    def is_place(index):
        return [index % seqs == at for at in range(1, seqs)]

    flags = {
        "cut": [((p + my_spot) % seqs).astype(jnp.uint32) for p in range(seqs)],
        "chunk": [is_place(my_slot - h) for h in range(seqs)],
        "return": [is_place(my_slot - p) for p in range(seqs)],
        "order": [is_place(j - my_spot) for j in range(seqs)],
        "columns": [((shard ^ flip) * wide).astype(jnp.uint32) for flip in FLIPS],
        "places": jnp.stack([shard, ctx % 4]).astype(jnp.int32),
        "turn": [((my_slot - p) % seqs)[None].astype(jnp.int32) for p in range(seqs)],
        "spot": my_spot[None].astype(jnp.int32),
    }

    def pick(parts, is_it):
        value = parts[0]
        for part, flag in zip(parts[1:], is_it):
            value = jnp.where(flag, part, value)
        return value

    def cut_rows(*values):
        return [
            jnp.concatenate(
                [
                    lax.dynamic_index_in_dim(value, flags["cut"][p], 0, keepdims=False)
                    for value in values
                ]
            )
            for p in range(seqs)
        ]

    def send_row(p):
        return lambda cut: lax.ppermute(cut, ("ctx", "shard"), pairs[p])

    def chunk_order(got):
        return [pick(got, flags["chunk"][h]) for h in range(seqs)]

    def return_cuts(parts):
        return [pick(parts, flags["return"][p]) for p in range(seqs)]

    def return_row(p):
        return lambda cut: lax.ppermute(cut, ("ctx", "shard"), [(b, a) for a, b in pairs[p]])

    def return_order(got):
        return jnp.stack([pick(got, flags["order"][j]) for j in range(seqs)])

    def core(value):
        return over_shard(value, 1)

    def chip(value):
        return over_shard(value, 2)

    def across(value):
        return over_shard(value, 3)

    def by_x(value):
        return over_ctx(value, 1)

    def by_z(value):
        return over_ctx(value, 2)

    def to_all(value):
        return [(functools.partial(over_shard, flip=flip), value) for flip in FLIPS[1:]]

    index_own = adapter_index[:, 0]
    (qkv_near, qkv_far, qkv_cross, flags), index_got = side_by_side(
        lambda x: (*cut(x[0], 0, 3, x[1]["places"], False), x[1]), [w_attn, flags], to_all(index_own)
    )
    places = flags["places"]
    index_all = jnp.concatenate(natural([index_own, *index_got], shard))
    sequence_with = jnp.sum(
        jnp.where(
            index_all[None, :] == jnp.arange(adapters, dtype=jnp.int32)[:, None],
            jnp.arange(batch, dtype=jnp.int32)[None, :],
            0,
        ),
        axis=1,
    )
    table = jnp.array(groups, jnp.int32)
    if per_sequence > 1:
        where = sequence_with
    else:
        group_with = jnp.sum(
            jnp.where(
                sequence_with[:, None] == jnp.arange(batch, dtype=jnp.int32)[None, :], table[:, 0][None, :], 0
            ),
            axis=1,
        )
        where = gathered_place(ctx, group_with)

    row_cuts = cut_rows(tokens)

    def rope_tables(place):
        spot, turn, row = np.indices((chunks, shards, rows)).reshape(3, -1).astype(np.int32)
        owner = place ^ np.array(FLIPS, np.int32)[turn]
        position = my_part * group_rows + (spot * shards + owner) * rows + row
        lane = np.arange(HD)
        freqs = np.exp((lane % (HD // 2)) * (-2.0 * math.log(rope_base) / HD)).astype(np.float32)
        angles = position.astype(F32)[:, None] * freqs[None, :]
        sign = np.where(lane < HD // 2, -1.0, 1.0).astype(np.float32)
        return position, jnp.cos(angles), jnp.sin(angles) * sign

    def prepare(x):
        chosen = choose(x[0], a_wide, a_down, b_model, b_hidden, gains)
        return chosen, cut(x[1], 0, 2, x[2], True), x[3], rope_tables(x[2][0])

    (chosen, gate_up_cuts, where, (positions, cosine, sine)), [qkv_a, *row_got, qkv_near] = side_by_side(
        prepare,
        [index_all[my_sequence][None], w_gate_up, places, where],
        [(chip, qkv_far), (send_row(0), row_cuts[0]), (send_row(1), row_cuts[1]), (core, qkv_near)],
    )
    own_wide, own_down, own_model, own_hidden, small = chosen
    near, gate_far, gate_cross, up_far, up_cross = gate_up_cuts

    token_rows = chunk_order(row_got)
    held = {}

    def load_out(x):
        held["out"], held["down"], done = load_plain(*x[:2])
        return done, jnp.concatenate(x[2:])

    (done, token_own), [qkv_b, qkv_xa, qkv_za] = side_by_side(
        load_out,
        [w_attn, w_down, *token_rows, small],
        [(across, qkv_cross), (by_x, qkv_a), (by_z, qkv_a)],
    )
    windows.carried.append(done)
    _, [token_far, qkv_xb, qkv_zb] = side_by_side(
        None, None, [(chip, token_own), (by_x, qkv_b), (by_z, qkv_b)]
    )
    _, [last_a, last_b, token_near, gate_a] = side_by_side(
        None,
        None,
        [
            (by_x, qkv_za),
            (by_z, qkv_xb),
            (core, jnp.stack([token_own, token_far])),
            (chip, gate_far),
        ],
    )
    w_qkv = [qkv_near, qkv_a, qkv_b, qkv_xa, qkv_xb, qkv_za, qkv_zb, last_a, last_b]
    token_parts = [token_own, token_far, token_near]
    small_parts = [part[..., seqs * rows :, :] for part in token_parts]
    small_parts = [small_parts[0], small_parts[1], small_parts[2][0], small_parts[2][1]]
    small_all = jnp.concatenate(
        natural(
            [
                jnp.concatenate([part[:, at * wide : (at + 1) * wide] for at in range(4)])
                for part in small_parts
            ],
            shard,
        ),
        axis=1,
    )
    qkv_downs = small_all[: 3 * rank]
    gate_downs = small_all[3 * rank : 5 * rank]
    out_up = small_all[5 * rank : 6 * rank]
    feed_up = small_all[6 * rank : 7 * rank]
    attn_gain = small_all[7 * rank : 7 * rank + 1].astype(F32)
    feed_gain = small_all[7 * rank + 1 : 7 * rank + 2].astype(F32)
    head_gains = gains[:2].astype(F32)

    (pre, qkv_low, squares, qkv_held), [gate_b, gate_xa, gate_za, near] = side_by_side(
        lambda x: qkv_forward(x, chunks, rows, w_attn, w_qkv, places, qkv_downs, own_model),
        token_parts,
        [(across, gate_cross), (by_x, gate_a), (by_z, gate_a), (core, near)],
    )

    def from_all(sums, others):
        _, got = side_by_side(None, None, to_all(sums) + others)
        return [sums, *got[:3]], got[3:]

    squares, _ = from_all(squares[:16], [])
    simple = per_sequence == 1 and chunk_rows == BLOCK
    attention_sends = [(chip, up_far), (by_x, gate_b), (by_z, gate_b)]
    if simple:
        (queries, key_rows, mixed, logs), got = side_by_side(
            lambda x: attention_forward(x[0], x[1], x[2], x[3], head_gains, chunks),
            [pre, squares, cosine, sine],
            attention_sends,
        )
    else:
        mixed, attention_grads = wide_attention(
            pre, squares, cosine, sine, head_gains, chunks, positions, groups
        )
        got = [send(value) for send, value in attention_sends]
    up_a, gate_xb, gate_zb = got

    every = range(chunks)
    assert chunks == 2
    def far_sum(keep, near):
        return by_rows(far_body, [keep, near], [BF])[0]

    def project_out(x, h):
        return partial_forward(x, h, chunks, held["out"], own_wide[3], out_up, False)

    def attention_rows(h, keep, near, got):
        return by_rows(attention_rows_body, [keep, near, got, token_rows[h], attn_gain], [F32, F32, BF])

    def feed_rows(h, keep, near, got):
        return by_rows(feed_rows_body, [keep, near, got, resid[h], cot[h], feed_gain], [BF, BF])

    def back_rows(h, keep, near, got):
        return by_rows(back_rows_body, [keep, near, got, attn_pre[h], cot[h], attn_gain], [F32, BF])

    def up_gate(parts):
        return gate_up_forward(parts, gate_up_held, gate_downs, own_hidden)

    def down(act):
        return partial_forward(act, 0, 1, held["down"], own_down, feed_up, False, [gate_up_held])

    def back_down(h, parts):
        return feed_back(
            parts, held["down"], own_down, hidden[h][0], hidden[h][1], hidden[h][3], feed_parts[h][2], feed_up, own_hidden, gate_up_held
        )

    def back_up_gate(h, gate_grad, upper_grad):
        return gate_up_back(
            gate_grad, upper_grad, gate_up_held, hidden_grads[h][2], gate_downs, resid_parts[h]
        )

    def back_out(h, parts):
        return out_back(parts, held["out"], own_wide[3], out_up, mixed, out_parts[h][2], h)

    none = [None] * PARTS

    def load_first(x):
        gate = [*x, None, None]
        held["gate_up"], done = load([gate, none], places, w_gate_up, near)
        return done

    def load_more(x):
        gate = none[:6] + x[:2]
        up = [*x[2:], None, None]
        held["gate_up"], done = load([gate, up], places, held=held["gate_up"])
        return done

    def load_last(x):
        held["gate_up"], done = load([none, none[:6] + x], places, held=held["gate_up"])
        return done

    attn_pre, resid, resid_low = [None] * 2, [None] * 2, [None] * 2
    resid_parts, hidden, feed_parts, output = [None] * 2, [None] * 2, [None] * 2, [None] * 2
    hidden_grads, resid_grads, grad_resid, out_grads = [None] * 2, [None] * 2, [None] * 2, [None] * 2
    out_parts, [up_b, up_xa, up_za] = side_by_side(
        lambda x: [project_out(x, h) for h in every], mixed, [(across, up_cross), (by_x, up_a), (by_z, up_a)]
    )
    _, [core0, core1] = side_by_side(None, None, [(core, out_parts[0][1]), (core, out_parts[1][1])])
    far0, far1 = far_sum(out_parts[0][0], core0), far_sum(out_parts[1][0], core1)
    done, [got0, got1, gate_last_a, gate_last_b] = side_by_side(
        load_first,
        [gate_a, gate_b, gate_xa, gate_xb, gate_za, gate_zb],
        [(chip, far0), (chip, far1), (by_x, gate_za), (by_z, gate_xb)],
    )
    windows.carried.append(done)
    attn_pre[0], resid[0], resid_low[0] = attention_rows(0, out_parts[0][0], core0, got0)
    attn_pre[1], resid[1], resid_low[1] = attention_rows(1, out_parts[1][0], core1, got1)
    _, [far0, near0, up_xb, up_zb] = side_by_side(
        None, None, [(chip, resid_low[0]), (core, resid_low[0]), (by_x, up_b), (by_z, up_b)]
    )
    done, [cross0, far1, near1, up_last_a, up_last_b] = side_by_side(
        load_more,
        [gate_last_a, gate_last_b, up_a, up_b, up_xa, up_xb, up_za, up_zb],
        [(core, far0), (chip, resid_low[1]), (core, resid_low[1]), (by_x, up_za), (by_z, up_xb)],
    )
    windows.carried.append(done)
    resid_parts[0] = [resid_low[0], far0, near0, cross0]
    done, [cross1] = side_by_side(load_last, [up_last_a, up_last_b], [(core, far1)])
    windows.carried.append(done)
    gate_up_held = held["gate_up"]
    resid_parts[1] = [resid_low[1], far1, near1, cross1]

    cot_cuts = cut_rows(cotangent)
    hidden[0], [cot0] = side_by_side(up_gate, resid_parts[0], [(send_row(0), cot_cuts[0])])
    feed_parts[0], _ = side_by_side(down, hidden[0][2], [])
    _, [core0] = side_by_side(None, None, [(core, feed_parts[0][1])])
    hidden[1], [got, cot1] = side_by_side(
        up_gate, resid_parts[1], [(chip, far_sum(feed_parts[0][0], core0)), (send_row(1), cot_cuts[1])]
    )
    cot = chunk_order([cot0, cot1])
    output[0], grad0 = feed_rows(0, feed_parts[0][0], core0, got)
    feed_parts[1], [far, near] = side_by_side(down, hidden[1][2], [(chip, grad0), (core, grad0)])
    _, [cross, core1] = side_by_side(None, None, [(core, far), (core, feed_parts[1][1])])
    hidden_grads[0], [got] = side_by_side(
        lambda x: back_down(0, x), [grad0, far, near, cross], [(chip, far_sum(feed_parts[1][0], core1))]
    )
    output[1], grad1 = feed_rows(1, feed_parts[1][0], core1, got)
    output = return_cuts(output)
    resid_grads[0], [far, near, output0] = side_by_side(
        lambda x: back_up_gate(0, *x),
        hidden_grads[0][:2],
        [(chip, grad1), (core, grad1), (return_row(0), output[0])],
    )
    _, [cross, core0] = side_by_side(None, None, [(core, far), (core, resid_grads[0][1])])
    hidden_grads[1], [got, output1] = side_by_side(
        lambda x: back_down(1, x),
        [grad1, far, near, cross],
        [(chip, far_sum(resid_grads[0][0], core0)), (return_row(1), output[1])],
    )
    output = return_order([output0, output1])
    grad_resid[0], grad0 = back_rows(0, resid_grads[0][0], core0, got)

    broad = jnp.concatenate(
        [sum(g[3] for g in hidden_grads), sum(g[5] for g in hidden_grads).reshape(2 * rank, -1)]
    ).astype(BF)
    broad = [x[None] for x in jnp.split(broad, 2, axis=1)]
    step0, step1, step2 = [ctx_step(at) for at in range(3)]

    def grown(value, got):
        return jnp.concatenate([value, got])

    resid_grads[1], [far, near, *got] = side_by_side(
        lambda x: back_up_gate(1, *x),
        hidden_grads[1][:2],
        [(chip, grad0), (core, grad0), (step0, broad[0]), (step0, broad[1])],
    )
    broad = [grown(*pair) for pair in zip(broad, got)]
    own_early, far_early, cuts = column_cuts(
        jnp.concatenate([sum(g[4] for g in hidden_grads), sum(g[2] for g in resid_grads)]), flags["columns"]
    )
    _, [cross, core1, got_early] = side_by_side(
        None, None, [(core, far), (core, resid_grads[1][1]), (core, cuts)]
    )
    own_early = own_early + got_early[0].astype(F32)
    far_early = (far_early + got_early[1].astype(F32)).astype(BF)
    out_grads[0], [got1, got_early, got] = side_by_side(
        lambda x: back_out(0, x),
        [grad0, far, near, cross],
        [(chip, far_sum(resid_grads[1][0], core1)), (chip, far_early), (step1, broad[0])],
    )
    broad[0] = grown(broad[0], got)
    early = (own_early + got_early.astype(F32)).astype(BF)[None]
    grad_resid[1], grad1 = back_rows(1, resid_grads[1][0], core1, got1)
    _, [far, near, got, got_early] = side_by_side(
        None, None, [(chip, grad1), (core, grad1), (step2, broad[0]), (step0, early)]
    )
    broad[0] = grown(broad[0], got)
    early = grown(early, got_early)
    _, [cross] = side_by_side(None, None, [(core, far)])
    out_grads[1] = back_out(1, [grad1, far, near, cross])
    grad_mixed = jnp.concatenate([g[0] for g in out_grads])

    attention_sends = [(step1, broad[1])]
    if simple:
        (query_turned, key_turned, grad_values, inner), [got] = side_by_side(
            lambda x: attention_back(
                queries, key_rows, pre, x, logs, cosine, sine, head_gains, chunks
            ),
            grad_mixed,
            attention_sends,
        )
    else:
        query_turned, key_turned, grad_values, inner = attention_grads(grad_mixed)
        [got] = [send(value) for send, value in attention_sends]
    broad[1] = grown(broad[1], got)
    inners, _ = from_all(inner, [])
    grads, lows, down_late, up_late = qkv_grads(
        [query_turned, key_turned], grad_values, pre, squares, inners, token_parts, qkv_low, own_model, chunks
    )
    partial = jnp.concatenate([down_late, sum(g[2] for g in out_grads)])
    cuts = [lax.dynamic_slice(partial, (jnp.uint32(0), start), (partial.shape[0], wide)) for start in flags["columns"]]

    def rest_of(value):
        for at in range(3, len(ctx_flips())):
            value = grown(value, ctx_step(at)(value))
        if per_sequence > 1:
            value = jnp.sum(value.astype(F32)[gathered_place(ctx, table)], axis=1)
        return value

    def placed(sources, counts, plan, carried=()):
        width = sum(sources[piece[0]].shape[-1] for piece in plan[0][0])
        outs = [shape_of((count, adapters, rank, width), F32) for count in counts]
        return call(
            functools.partial(place_body, rank, len(sources), len(carried), plan),
            (1,),
            [*sources, *carried],
            [whole(x) for x in (*sources, *carried)],
            [(o, whole(o)) for o in outs],
            scalars=[where],
        )

    def place_broad(x):
        return placed([rest_of(value) for value in x], (1, 2), ((((0, 0), (1, 0)),), (((0, 1), (1, 1)), ((0, 2), (1, 2)))))

    sends = [(send, piece.astype(BF)) for send, piece in zip((chip, core, across), cuts[1:])]
    (keep, send), [*got, got_early] = side_by_side(
        lambda x: qkv_back(x, lows, qkv_held, qkv_downs, chunks), grads, sends + [(step1, early)]
    )
    early = grown(early, got_early)
    late = jnp.concatenate(
        [
            cuts[0] + sum(piece.astype(F32) for piece in got),
            up_late.reshape(3 * rank, -1),
            sum(g[1] for g in out_grads),
        ]
    ).astype(BF)[None]
    _, [near_sum, got, got_early] = side_by_side(None, None, [(core, send), (step0, late), (step2, early)])
    early = grown(early, got_early)
    late = jnp.split(grown(late, got), 2, axis=2)
    far = shape_of(grad_resid[0].shape, BF)
    fars = call(
        far_two_body, (1,), [keep, near_sum], [whole(keep), whole(near_sum)], [(far, whole(far))] * chunks
    )
    _, [got0, got_a, got] = side_by_side(
        None, None, [(chip, fars[0]), (step1, late[0]), (step2, broad[1])]
    )
    broad[1] = grown(broad[1], got)
    late[0] = grown(late[0], got_a)
    (grad_down, grad_hidden), [got1, got_a, got_b] = side_by_side(
        place_broad, broad, [(chip, fars[1]), (step2, late[0]), (step1, late[1])]
    )
    late = [grown(late[0], got_a), grown(late[1], got_b)]
    def place_late(x):
        return placed(
            x,
            (6, 5),
            (
                (*[((1, at), (2, at)) for at in (0, 1, 2, 7)], ((0, 1),), ((0, 2),)),
                (*[((1, at), (2, at)) for at in (4, 5, 6, 3)], ((0, 0),)),
            ),
            windows.carried,
        )

    sends, [got_late] = side_by_side(
        lambda x: input_rows(keep, near_sum, x, grad_resid, flags["turn"][0]), [got0, got1], [(step2, late[1])]
    )
    sources = [rest_of(early), rest_of(late[0]), rest_of(grown(late[1], got_late))]
    (grad_wide, grad_model), got = side_by_side(
        place_late, sources, [(return_row(p), rows_back) for p, rows_back in enumerate(sends)]
    )
    input_grad = order_rows(got, flags["spot"])
    return (output, input_grad, grad_wide, grad_down[0], grad_model, grad_hidden)


def solution(mesh):
    return jax.shard_map(
        on_device,
        mesh=mesh,
        in_specs=(
            P("shard", "ctx", None),
            P("shard", "ctx", None),
            P("shard", None),
            P(None, "shard", None),
            P(None, "shard", None),
            P("shard", None),
            P(None, "shard"),
            P(None, None, None, "shard"),
            P(None, None, "shard"),
            P(None, None, None, "shard"),
            P(None, None, None, "shard"),
        ),
        out_specs=(
            P("shard", "ctx", None),
            P("shard", "ctx", None),
            P(None, None, None, "shard"),
            P(None, None, "shard"),
            P(None, None, None, "shard"),
            P(None, None, None, "shard"),
        ),
        check_vma=False,
    )
```

```python
import functools
import math

import jax
import jax.numpy as jnp
import numpy as np
from jax import lax
from jax.experimental import pallas as pl
from jax.experimental.pallas import tpu as pltpu
from jax.sharding import PartitionSpec as P

D = 2048
HEADS = 16
HD = 128
BLOCK = 256

epsilon = 1e-06
rope_base = 500000.0
far_below = -1e30
BF = jnp.bfloat16
F32 = jnp.float32
VMEM_BYTES = 16 * 2**20


def dot(left, right):
    return lax.dot_general(left, right, (((1,), (0,)), ((), ())), preferred_element_type=F32)


def dot_nt(left, right):
    return lax.dot_general(left, right, (((1,), (1,)), ((), ())), preferred_element_type=F32)


def dot_tn(left, right):
    return lax.dot_general(left, right, (((0,), (0,)), ((), ())), preferred_element_type=F32)


def over_shard(value, flip):
    size = lax.axis_size("shard")
    return lax.ppermute(value, "shard", [(i, i ^ flip) for i in range(size)])


class Windows:
    def __init__(self):
        self.carried = []

    def side_by_side(self, run, inputs, sends):
        values = [value for _, value in sends]
        inputs, values, self.carried = lax.optimization_barrier((inputs, values, self.carried))
        got = [send(value) for (send, _), value in zip(sends, values)]
        out = run(inputs) if run else None
        out, got, self.carried = lax.optimization_barrier((out, got, self.carried))
        return out, got


def over_ctx(value, flip):
    size = lax.axis_size("ctx")
    return lax.ppermute(value, "ctx", [(i, i ^ flip) for i in range(size)])


FLIPS = (0, 2, 1, 3)


def call(body, grid, args, in_specs, outs, scratch=(), scalars=(), flops=0, aliases={}):
    placed = []
    for arg, spec in zip(args, in_specs):
        if spec.memory_space == pltpu.VMEM:
            arg = pltpu.with_memory_space_constraint(arg, pltpu.VMEM)
        elif spec.memory_space == pltpu.HBM:
            arg = pltpu.with_memory_space_constraint(arg, pltpu.HBM)
        placed.append(arg)
    return pl.pallas_call(
        body,
        grid_spec=pltpu.PrefetchScalarGridSpec(
            num_scalar_prefetch=len(scalars),
            grid=grid,
            in_specs=in_specs,
            out_specs=[spec for _, spec in outs],
            scratch_shapes=scratch,
        ),
        out_shape=[shape for shape, _ in outs],
        input_output_aliases=aliases,
        compiler_params=pltpu.CompilerParams(vmem_limit_bytes=VMEM_BYTES),
        cost_estimate=pl.CostEstimate(flops=flops, bytes_accessed=0, transcendentals=0),
    )(*scalars, *placed)


def shape_of(shape, kind):
    return jax.ShapeDtypeStruct(shape, kind)


def whole(value):
    zeros = (0,) * value.ndim
    return pl.BlockSpec(value.shape, lambda *_: zeros)


def spec(block, index):
    return pl.BlockSpec(block, lambda i, *_: index(i))


def column_spec(value, tile):
    zeros = (0,) * (value.ndim - 1)
    return pl.BlockSpec(value.shape[:-1] + (tile,), lambda i, *_: (*zeros, i))


HBM = pl.BlockSpec(memory_space=pltpu.HBM)
ANY = pl.BlockSpec(memory_space=pl.ANY)
VMEM = pl.BlockSpec(memory_space=pltpu.VMEM)


def tile_of(width):
    return min(1024, width)


def run_copies(copies):
    for copy in copies:
        copy.start()
    for copy in copies:
        copy.wait()


def cut_body(first, apart, places, weight, near, *refs):
    fars, sems = refs[:-1], refs[-1]
    step = pl.program_id(0)
    width = near.shape[2]
    slim = fars[0].shape[1]
    rows = pl.ds(pl.multiple_of(places[1] * slim, slim), slim)

    def columns(flip):
        return pl.ds(pl.multiple_of((places[0] ^ flip) * width, width), width)

    def copies(far, cross):
        sources = [(slice(None), columns(1), near), (rows, columns(2), far), (rows, columns(3), cross)]
        return [
            pltpu.make_async_copy(weight.at[first + step, r, c], to.at[0], sems.at[i])
            for i, (r, c, to) in enumerate(sources)
        ]

    if apart:
        for matrix in range(len(fars) // 2):
            pair = fars[2 * matrix : 2 * matrix + 2]
            pl.when(step == matrix)(functools.partial(lambda pair: run_copies(copies(*pair)), pair))
    else:
        run_copies(copies(*fars))


def cut(weight, first, count, places, apart):
    depth, full = weight.shape[1:]
    width, slim = full // 4, depth // 4
    if apart:
        far = (shape_of((1, slim, width), BF), pl.BlockSpec((1, slim, width), lambda *_: (0, 0, 0)))
    else:
        far = (shape_of((count, slim, width), BF), pl.BlockSpec((1, slim, width), lambda m, _: (m, 0, 0)))
    return call(
        functools.partial(cut_body, first, apart),
        (count,),
        [weight],
        [HBM],
        [(shape_of((count, depth, width), BF), pl.BlockSpec((1, depth, width), lambda m, _: (m, 0, 0)))]
        + [far] * (2 * count if apart else 2),
        [pltpu.SemaphoreType.DMA((3,))],
        scalars=[places],
    )


COPIES = 10
PARTS = 8


def copies_of(weight, matrix, near, near_at, parts, at, places, held, sems):
    width = held.shape[1]
    depth = held.shape[0] // 4
    slim = depth // 4
    shard, quarter = places[0], places[1]

    def to(flip, rows, begin=0):
        start = pl.multiple_of((shard ^ flip) * depth + begin, slim)
        return held.at[pl.ds(start, rows), :]

    pairs = []
    if weight is not None:
        own_columns = pl.ds(pl.multiple_of(shard * width, width), width)
        pairs.append((weight.at[matrix, :, own_columns], to(0, depth)))
    if near is not None:
        pairs.append((near.at[near_at], to(1, depth)))
    for i, part in enumerate(parts):
        if part is not None:
            pairs.append((part.at[at], to(2 + i % 2, slim, (quarter ^ (i // 2)) * slim)))
    return [pltpu.make_async_copy(source, target, sems.at[i]) for i, (source, target) in enumerate(pairs)]


DONE = (shape_of((8, 128), F32), pl.BlockSpec((8, 128), lambda *_: (0, 0)))


def load_plain_body(attn, down, out_held, down_held, done, sems):
    run_copies(
        [
            pltpu.make_async_copy(attn.at[attn.shape[0] - 1], out_held, sems.at[0]),
            pltpu.make_async_copy(down, down_held, sems.at[1]),
        ]
    )
    done[...] = jnp.zeros_like(done)


def load_plain(w_attn, w_down):
    return call(
        load_plain_body,
        (1,),
        [w_attn, w_down],
        [HBM] * 2,
        [(pltpu.VMEM(w_attn.shape[1:], BF), VMEM), (pltpu.VMEM(w_down.shape, BF), VMEM), DONE],
        [pltpu.SemaphoreType.DMA((2,))],
    )


def load_body(first, there, places, *refs):
    refs = list(refs)
    weight, near = (refs.pop(0), refs.pop(0)) if first else (None, None)
    parts = [[refs.pop(0) if is_there else None for is_there in matrix] for matrix in there]
    held, done, sems = refs[-3:]
    copies = []
    for m, matrix_parts in enumerate(parts):
        copies += copies_of(weight, m, near, m, matrix_parts, 0, places, held.at[m], sems.at[m])
    run_copies(copies)
    done[...] = jnp.zeros_like(done)


def load(parts, places, weight=None, near=None, held=None):
    there = [[part is not None for part in matrix] for matrix in parts]
    arrays = [part for matrix in parts for part in matrix if part is not None]
    arrays = ([weight, near] if held is None else []) + arrays
    depth, full = (weight if held is None else held).shape[1:]
    shape = (2, 4 * depth, full // 4) if held is None else held.shape
    return call(
        functools.partial(load_body, held is None, there),
        (1,),
        arrays + ([] if held is None else [held]),
        ([HBM] + [ANY] * (len(arrays) - 1) if held is None else [ANY] * len(arrays) + [VMEM]),
        [(pltpu.VMEM(shape, BF), VMEM), DONE],
        [pltpu.SemaphoreType.DMA((2, COPIES))],
        [places],
        aliases={} if held is None else {1 + len(arrays): 0},
    )


def row_of(column):
    return jnp.transpose(jnp.broadcast_to(column, (column.shape[0], 128)))[:8]


def column_of(row):
    return jnp.transpose(jnp.broadcast_to(row[:1], (128, row.shape[1])))[:, :1]


def qkv_body(chunks, size, places, *refs):
    x_refs, refs = refs[:3], refs[3:]
    weight, near, weight_parts, refs = refs[0], refs[1], refs[2 : 2 + PARTS], refs[2 + PARTS :]
    down, up, pre, low, sums, kept, held, rows, sems, keep_sems = refs
    step = pl.program_id(0)

    def copies(p):
        return copies_of(weight, p, near, p, weight_parts, p, places, held.at[p], sems.at[p])

    @pl.when(step == 0)
    def _():
        for p in range(held.shape[0]):
            for copy in copies(p):
                copy.start()
        for h in range(chunks):
            rows[4 * h * size : 4 * (h + 1) * size] = load_parts(x_refs, h * size, size)

    lowrank = dot_nt(rows[...], down[...]).astype(BF)
    for copy in copies(step):
        copy.wait()
    keep = [pltpu.make_async_copy(held.at[p], kept.at[p], keep_sems.at[p]) for p in range(held.shape[0])]
    for p, copy in enumerate(keep):
        pl.when(step == p)(copy.start)
    value = dot(rows[...], held[step]) + dot(lowrank, up[0])
    pre[0] = value.astype(BF)
    low[0] = lowrank
    sums[...] = row_of(jnp.sum(value * value, axis=1, keepdims=True))

    @pl.when(step == held.shape[0] - 1)
    def _():
        for copy in keep:
            copy.wait()


def qkv_forward(x_parts, chunks, size, weight, weight_parts, places, downs, ups):
    count, depth, width = weight_parts[0].shape
    full = x_parts[0].shape[1]
    total, rank = 4 * chunks * size, ups.shape[1]
    return call(
        functools.partial(qkv_body, chunks, size),
        (count,),
        [*x_parts, weight, *weight_parts, downs, ups],
        [whole(x) for x in x_parts]
        + [HBM] * (2 + PARTS)
        + [
            spec((rank, full), lambda p: (p, 0)),
            spec((1, rank, width), lambda p: (p, 0, 0)),
        ],
        [
            (shape_of((count, total, width), BF), spec((1, total, width), lambda p: (p, 0, 0))),
            (shape_of((count, total, rank), BF), spec((1, total, rank), lambda p: (p, 0, 0))),
            (shape_of((8 * count, total), F32), spec((8, total), lambda p: (p, 0))),
            (pltpu.HBM((count, full, width), BF), HBM),
        ],
        [
            pltpu.VMEM((count, full, width), BF),
            pltpu.VMEM((total, full), BF),
            pltpu.SemaphoreType.DMA((count, COPIES)),
            pltpu.SemaphoreType.DMA((count,)),
        ],
        [places],
        flops=2 * total * full * width * count,
    )


def aligned_sums(refs, which, chunks):
    total = refs[0].shape[1]
    block = total // (4 * chunks)
    out = 0.0
    for flip, ref in zip(FLIPS, refs):
        column = column_of(ref[8 * which : 8 * which + 8])
        if flip:
            order = [FLIPS.index(f ^ flip) for f in FLIPS]
            column = jnp.concatenate(
                [
                    column[(4 * h + i) * block : (4 * h + i + 1) * block]
                    for h in range(chunks)
                    for i in order
                ]
            )
        out = out + column
    return out


def attention_body(chunks, factor, *refs):
    (
        query_pre, key_pre, value, own, far, near, cross, cosine, sine, gains,
        query_out, key_out, mixed_out, logs_out, scale_rows,
    ) = refs
    total = query_pre.shape[1]
    size = total // chunks

    @pl.when(pl.program_id(0) == 0)
    def _():
        for p in range(2):
            sums = aligned_sums((own, far, near, cross), p, chunks)
            scale_rows[p] = jnp.broadcast_to(lax.rsqrt(sums / D + epsilon), (total, HD))

    def prepared(pre, p):
        value = pre[0].astype(F32) * scale_rows[p] * gains[p : p + 1]
        return (value * cosine[...] + pltpu.roll(value, HD // 2, 1) * sine[...]).astype(BF)

    query, key = prepared(query_pre, 0), prepared(key_pre, 1)
    query_out[...] = query
    key_out[...] = key
    logs = []
    for h in range(chunks):
        seen = (h + 1) * size
        scores = dot_nt(query[h * size : (h + 1) * size], key[:seen]) * factor
        top = jnp.max(scores, axis=1, keepdims=True)
        weights = jnp.exp(scores - top)
        sums = jnp.sum(weights, axis=1, keepdims=True)
        probs = (weights * (1.0 / sums)).astype(BF)
        mixed_out[h * size : (h + 1) * size] = dot(probs, value[0, :seen]).astype(BF)
        logs.append(top + jnp.log(sums))
    logs_out[...] = row_of(jnp.concatenate(logs))


def attention_forward(pre, sums, cosine, sine, gains, chunks):
    _, total, width = pre.shape
    heads = width // HD
    factor = 1.0 / math.sqrt(HD)

    def head(p):
        return spec((1, total, HD), lambda i: (p, 0, i))

    by_head = spec((total, HD), lambda i: (0, i))
    return call(
        functools.partial(attention_body, chunks, factor),
        (heads,),
        [pre, pre, pre, *sums, cosine, sine, gains],
        [head(0), head(1), head(2)]
        + [whole(s) for s in sums]
        + [whole(cosine), whole(sine), spec((gains.shape[0], HD), lambda i: (0, i))],
        [
            (shape_of((total, width), BF), by_head),
            (shape_of((total, width), BF), by_head),
            (shape_of((total, width), BF), by_head),
            (shape_of((8 * heads, total), F32), spec((8, total), lambda i: (i, 0))),
        ],
        [pltpu.VMEM((2, total, HD), F32)],
        flops=4 * total * total * width,
    )


def attention_back_body(chunks, factor, *refs):
    (
        query_in, key_in, query_pre, key_pre, value, grad_in, logs, cosine, sine, gains,
        query_out, key_out, value_out, inner_out, inner_rows,
    ) = refs
    total = query_in.shape[0]
    size = total // chunks
    head = pl.program_id(0)
    query, key, values, grad = query_in[...], key_in[...], value[0], grad_in[...]
    log_column = column_of(logs[...])
    grad_key = [0.0] * chunks
    grad_value = [0.0] * chunks
    grad_query = []
    for h in range(chunks):
        rows = slice(h * size, (h + 1) * size)
        grad_row = 0.0
        delta = 0.0
        kept = []
        for k in range(h + 1):
            keys = slice(k * size, (k + 1) * size)
            scores = dot_nt(query[rows], key[keys]) * factor
            probs = jnp.exp(scores - log_column[rows])
            grad_probs = dot_nt(grad[rows], values[keys])
            delta = delta + jnp.sum(probs * grad_probs, axis=1, keepdims=True)
            kept.append((probs, grad_probs))
        for k, (probs, grad_probs) in enumerate(kept):
            keys = slice(k * size, (k + 1) * size)
            grad_scores = (probs * (grad_probs - delta)).astype(BF)
            grad_row = grad_row + dot(grad_scores, key[keys])
            grad_key[k] = grad_key[k] + dot_tn(grad_scores, query[rows])
            grad_value[k] = grad_value[k] + dot_tn(probs.astype(BF), grad[rows])
        grad_query.append(grad_row)

    value_out[...] = jnp.concatenate(grad_value).astype(BF)
    for p, (pre, grads, out) in enumerate(
        ((query_pre, grad_query, query_out), (key_pre, grad_key, key_out))
    ):
        turned = jnp.concatenate(grads) * factor
        turned = turned * cosine[...] - pltpu.roll(turned, HD // 2, 1) * sine[...]
        turned = turned * gains[p : p + 1]
        out[...] = turned.astype(BF)
        inner = jnp.sum(turned * pre[0].astype(F32), axis=1, keepdims=True)
        inner = jnp.broadcast_to(inner, (total, 128))

        @pl.when(head == 0)
        def _():
            inner_rows[p] = inner

        @pl.when(head > 0)
        def _():
            inner_rows[p] += inner

    @pl.when(head == pl.num_programs(0) - 1)
    def _():
        for p in range(2):
            inner_out[8 * p : 8 * p + 8] = jnp.transpose(inner_rows[p])[:8]


def attention_back(queries, key_rows, pre, grad_mixed, logs, cosine, sine, gains, chunks):
    _, total, width = pre.shape
    heads = width // HD
    factor = 1.0 / math.sqrt(HD)

    def head(p):
        return spec((1, total, HD), lambda i: (p, 0, i))

    by_head = spec((total, HD), lambda i: (0, i))
    return call(
        functools.partial(attention_back_body, chunks, factor),
        (heads,),
        [queries, key_rows, pre, pre, pre, grad_mixed, logs, cosine, sine, gains],
        [by_head, by_head, head(0), head(1), head(2), by_head]
        + [spec((8, total), lambda i: (i, 0)), whole(cosine), whole(sine)]
        + [spec((gains.shape[0], HD), lambda i: (0, i))],
        [
            (shape_of((total, width), BF), by_head),
            (shape_of((total, width), BF), by_head),
            (shape_of((total, width), BF), by_head),
            (shape_of((16, total), F32), pl.BlockSpec((16, total), lambda *_: (0, 0))),
        ],
        [pltpu.VMEM((2, total, 128), F32)],
        flops=10 * total * total * width,
    )


def split_out(value, keep, send):
    if keep.ndim == 2:
        half = value.shape[0] // 2
        keep[...] = value[:half].astype(BF)
        send[...] = value[half:].astype(BF)
        return
    half = keep.shape[1]
    for h in range(keep.shape[0]):
        keep[h] = value[2 * h * half : (2 * h + 1) * half].astype(BF)
        send[h] = value[(2 * h + 1) * half : (2 * h + 2) * half].astype(BF)


def qkv_grads_body(chunks, *refs):
    query_grad, key_grad, value_grad, query_pre, key_pre = refs[:5]
    squares, inners, x_refs = refs[5:9], refs[9:13], refs[13:16]
    low, ups, grads, lows, down_out, up_out = refs[16:]
    rank = ups.shape[1]
    total = query_grad.shape[0]
    for p, (grad, pre) in enumerate(((query_grad, query_pre), (key_grad, key_pre))):
        scale = lax.rsqrt(aligned_sums(squares, p, chunks) / D + epsilon)
        inner = aligned_sums(inners, p, chunks) * (scale * scale * scale / D)
        grads[p] = (grad[...].astype(F32) * scale - pre[0].astype(F32) * inner).astype(BF)
    grads[2] = value_grad[...]
    for p in range(3):
        lows[:, p * rank : (p + 1) * rank] = dot_nt(grads[p], ups[p]).astype(BF)
        up_out[p] = dot_tn(low[p], grads[p])
    size = total // chunks
    down = 0.0
    for h in range(chunks):
        x = load_parts(x_refs, h * size // 4, size // 4)
        down += dot_tn(lows[h * size : (h + 1) * size], x)
    down_out[...] = down


def qkv_grads(turned, grad_values, pre, squares, inners, x_parts, low, ups, chunks):
    count, total, width = pre.shape
    rank = ups.shape[1]
    full = x_parts[0].shape[1]

    def pre_rows(p):
        return pl.BlockSpec((1, total, width), lambda *_: (p, 0, 0))

    outs = [
        shape_of((count, total, width), BF),
        shape_of((total, count * rank), BF),
        shape_of((count * rank, full), F32),
        shape_of((count, rank, width), F32),
    ]
    return call(
        functools.partial(qkv_grads_body, chunks),
        (1,),
        [*turned, grad_values, pre, pre, *squares, *inners, *x_parts, low, ups],
        [whole(turned[0]), whole(turned[1]), whole(grad_values), pre_rows(0), pre_rows(1)]
        + [whole(v) for v in (*squares, *inners, *x_parts, low)]
        + [pl.BlockSpec((count, rank, width), lambda *_: (0, 0, 0))],
        [(o, whole(o)) for o in outs],
        flops=2 * total * width * 512,
    )


def qkv_back_body(grads, lows, weight, downs, keep, send):
    value = dot(lows[...], downs[...])
    for p in range(3):
        value += dot_nt(grads[p], weight[p])
    split_out(value, keep, send)


def qkv_back(grads, lows, weight, downs, chunks):
    count, full, width = weight.shape
    total = grads.shape[1]
    tile = tile_of(full)
    half = total // chunks // 2
    part = (shape_of((chunks, half, full), BF), spec((chunks, half, tile), lambda i: (0, 0, i)))
    return call(
        qkv_back_body,
        (full // tile,),
        [grads, lows, weight, downs],
        [
            whole(grads),
            whole(lows),
            spec((count, tile, width), lambda i: (0, i, 0)),
            spec((downs.shape[0], tile), lambda i: (0, i)),
        ],
        [part, part],
        flops=2 * total * full * width * count,
    )


def partial_body(streamed, beside, x, weight, down, up, *refs):
    keep, send, low, *scratch = refs[beside:]
    step = pl.program_id(0)
    tile = keep.shape[1]

    def columns(i):
        return pl.ds(pl.multiple_of(i * tile, tile), tile)

    def copy(i):
        held, sems = scratch
        return pltpu.make_async_copy(weight.at[:, columns(i)], held.at[:, columns(i)], sems.at[i])

    @pl.when(step == 0)
    def _():
        if streamed:
            for i in range(weight.shape[1] // tile):
                copy(i).start()
        low[...] = dot_nt(x[...], down[...]).astype(BF)

    if streamed:
        copy(step).wait()
        held = scratch[0]
    else:
        held = weight
    split_out(dot(x[...], held[:, columns(step)]) + dot(low[...], up[...]), keep, send)


def partial_forward(x, chunk, chunks, weight, down, up, streamed, beside=()):
    total, depth = x.shape
    size = total // chunks
    full = weight.shape[-1]
    tile = tile_of(full)
    half = size // 2
    rank = down.shape[0]
    scratch = [pltpu.VMEM(weight.shape, BF), pltpu.SemaphoreType.DMA((full // tile,))]
    return call(
        functools.partial(partial_body, streamed, len(beside)),
        (full // tile,),
        [x, weight, down, up, *beside],
        [
            pl.BlockSpec((size, depth), lambda *_: (chunk, 0)),
            HBM if streamed else VMEM,
            whole(down),
            spec((rank, tile), lambda i: (0, i)),
            *[VMEM] * len(beside),
        ],
        [
            (shape_of((half, full), BF), spec((half, tile), lambda i: (0, i))),
            (shape_of((half, full), BF), spec((half, tile), lambda i: (0, i))),
            (shape_of((size, rank), BF), pl.BlockSpec((size, rank), lambda *_: (0, 0))),
        ],
        scratch if streamed else (),
        flops=2 * size * depth * full,
    )


def gate_up_body(*refs):
    x_refs, (weight, downs, ups, gate, upper, act, low, rows) = refs[:4], refs[4:]
    rank = ups.shape[1]
    tile = gate.shape[1]
    step = pl.program_id(0)

    @pl.when(step == 0)
    def _():
        rows[...] = load_parts(x_refs)
        low[...] = dot_nt(rows[...], downs[...]).astype(BF)

    columns = pl.ds(pl.multiple_of(step * tile, tile), tile)
    gate_pre = dot(rows[...], weight[0, :, columns]) + dot(low[:, :rank], ups[0])
    upper_pre = dot(rows[...], weight[1, :, columns]) + dot(low[:, rank:], ups[1])
    gate[...] = gate_pre.astype(BF)
    upper[...] = upper_pre.astype(BF)
    act[...] = (gate_pre * jax.nn.sigmoid(gate_pre) * upper_pre).astype(BF)


def gate_up_forward(x_parts, weight, downs, ups):
    _, full, width = weight.shape
    size = 4 * x_parts[0].shape[0]
    rank = ups.shape[1]
    tile = tile_of(width)
    out = (shape_of((size, width), BF), spec((size, tile), lambda i: (0, i)))
    return call(
        gate_up_body,
        (width // tile,),
        [*x_parts, weight, downs, ups],
        [whole(x) for x in x_parts] + [VMEM, whole(downs), spec((2, rank, tile), lambda i: (0, 0, i))],
        [
            out,
            out,
            out,
            (shape_of((size, 2 * rank), BF), pl.BlockSpec((size, 2 * rank), lambda *_: (0, 0))),
        ],
        [pltpu.VMEM((size, full), BF)],
        flops=4 * size * full * width,
    )


def feed_back_body(*refs):
    g_refs = refs[:4]
    weight, down, gate, upper, gate_low, feed_low, feed_up, ups, _ = refs[4:13]
    gate_grad, upper_grad, low_out, down_a, feed_b, hidden_b, rows, low, lows = refs[13:]
    rank = down.shape[0]
    step = pl.program_id(0)
    @pl.when(step == 0)
    def _():
        rows[...] = load_parts(g_refs)
        low[...] = dot_nt(rows[...], feed_up[...]).astype(BF)
        feed_b[...] = dot_tn(feed_low[...], rows[...])
        lows[...] = jnp.zeros_like(lows)

    tile = gate.shape[1]
    held_rows = pl.ds(pl.multiple_of(step * tile, tile), tile)
    grad_act = dot_nt(rows[...], weight[held_rows]) + dot(low[...], down[...])
    gate_pre, upper_pre = gate[...].astype(F32), upper[...].astype(F32)
    sig = jax.nn.sigmoid(gate_pre)
    silu = gate_pre * sig
    down_a[...] = dot_tn(low[...], (silu * upper_pre).astype(BF))
    grad_upper = (grad_act * silu).astype(BF)
    grad_gate = (grad_act * upper_pre * (sig + silu * (1.0 - sig))).astype(BF)
    gate_grad[...] = grad_gate
    upper_grad[...] = grad_upper
    hidden_b[0] = dot_tn(gate_low[:, :rank], grad_gate)
    hidden_b[1] = dot_tn(gate_low[:, rank:], grad_upper)
    lows[:, :rank] += dot_nt(grad_gate, ups[0])
    lows[:, rank:] += dot_nt(grad_upper, ups[1])

    @pl.when(step == pl.num_programs(0) - 1)
    def _():
        low_out[...] = lows[...].astype(BF)


def feed_back(g_parts, weight, down, gate, upper, gate_low, feed_low, feed_up, ups, beside):
    width, depth = weight.shape
    size = 4 * g_parts[0].shape[0]
    rank = down.shape[0]
    tile = tile_of(width)
    by_tile = spec((size, tile), lambda i: (0, i))
    return call(
        feed_back_body,
        (width // tile,),
        [*g_parts, weight, down, gate, upper, gate_low, feed_low, feed_up, ups, beside],
        [whole(g) for g in g_parts]
        + [
            VMEM,
            spec((rank, tile), lambda i: (0, i)),
            by_tile,
            by_tile,
            whole(gate_low),
            whole(feed_low),
            whole(feed_up),
            spec((2, rank, tile), lambda i: (0, 0, i)),
            VMEM,
        ],
        [
            (shape_of((size, width), BF), by_tile),
            (shape_of((size, width), BF), by_tile),
            (shape_of((size, 2 * rank), BF), pl.BlockSpec((size, 2 * rank), lambda *_: (0, 0))),
            (shape_of((rank, width), F32), spec((rank, tile), lambda i: (0, i))),
            (shape_of((rank, depth), F32), pl.BlockSpec((rank, depth), lambda *_: (0, 0))),
            (shape_of((2, rank, width), F32), spec((2, rank, tile), lambda i: (0, 0, i))),
        ],
        [
            pltpu.VMEM((size, depth), BF),
            pltpu.VMEM((size, rank), BF),
            pltpu.VMEM((size, 2 * rank), F32),
        ],
        flops=2 * size * depth * width,
    )


def gate_up_back_body(gate_grad, upper_grad, weight, low, downs, *refs):
    x_refs, (keep, send, down_out) = refs[:4], refs[4:]
    tile = keep.shape[1]
    held_rows = pl.ds(pl.multiple_of(pl.program_id(0) * tile, tile), tile)
    value = dot_nt(gate_grad[...], weight[0, held_rows]) + dot_nt(upper_grad[...], weight[1, held_rows])
    split_out(value + dot(low[...], downs[...]), keep, send)
    down_out[...] = dot_tn(low[...], load_parts(x_refs))


def gate_up_back(gate_grad, upper_grad, weight, low, downs, x_parts):
    _, full, width = weight.shape
    size = gate_grad.shape[0]
    half = size // 2
    ranks = downs.shape[0]
    tile = tile_of(full)
    return call(
        gate_up_back_body,
        (full // tile,),
        [gate_grad, upper_grad, weight, low, downs, *x_parts],
        [whole(gate_grad), whole(upper_grad), VMEM, whole(low), spec((ranks, tile), lambda i: (0, i))]
        + [column_spec(x, tile) for x in x_parts],
        [
            (shape_of((half, full), BF), spec((half, tile), lambda i: (0, i))),
            (shape_of((half, full), BF), spec((half, tile), lambda i: (0, i))),
            (shape_of((ranks, full), F32), spec((ranks, tile), lambda i: (0, i))),
        ],
        flops=4 * size * full * width,
    )


def out_back_body(*refs):
    g_refs = refs[:4]
    weight, down, up, mixed, low, grad_mixed, down_out, up_out, rows, grad_low = refs[4:]

    @pl.when(pl.program_id(0) == 0)
    def _():
        rows[...] = load_parts(g_refs)
        grad_low[...] = dot_nt(rows[...], up[...]).astype(BF)
        up_out[...] = dot_tn(low[...], rows[...])

    tile = grad_mixed.shape[1]
    held_rows = pl.ds(pl.multiple_of(pl.program_id(0) * tile, tile), tile)
    grad_mixed[...] = (dot_nt(rows[...], weight[held_rows]) + dot(grad_low[...], down[...])).astype(BF)
    down_out[...] = dot_tn(grad_low[...], mixed[...])


def out_back(g_parts, weight, down, up, mixed, low, chunk):
    width, depth = weight.shape
    size = 4 * g_parts[0].shape[0]
    rank = down.shape[0]
    tile = min(256, width)
    return call(
        out_back_body,
        (width // tile,),
        [*g_parts, weight, down, up, mixed, low],
        [whole(g) for g in g_parts]
        + [
            VMEM,
            spec((rank, tile), lambda i: (0, i)),
            whole(up),
            spec((size, tile), lambda i: (chunk, i)),
            whole(low),
        ],
        [
            (shape_of((size, width), BF), spec((size, tile), lambda i: (0, i))),
            (shape_of((rank, width), F32), spec((rank, tile), lambda i: (0, i))),
            (shape_of((rank, depth), F32), pl.BlockSpec((rank, depth), lambda *_: (0, 0))),
        ],
        [pltpu.VMEM((size, depth), BF), pltpu.VMEM((size, rank), BF)],
        flops=2 * size * depth * width,
    )


def load_parts(refs, first=0, count=None, columns=slice(None)):
    own, far, *near = refs
    if len(near) == 1:
        near = near[0].at[0], near[0].at[1]
    rows = slice(first, own.shape[0] if count is None else first + count)
    return jnp.concatenate([ref[rows, columns] for ref in (own, far, *near)])


def ctx_flips():
    size = lax.axis_size("ctx")
    return [flip for flip in (2, 4, 8, 16, 1) if flip < size]


def ctx_step(at):
    return lambda value: over_ctx(value, ctx_flips()[at])


def gathered_place(ctx, other):
    place = 0
    for at, flip in enumerate(ctx_flips()):
        place = place + (((ctx ^ other) // flip) % 2) * 2**at
    return place


def column_cuts(partial, starts):
    width = partial.shape[-1] // 4
    zero = jnp.uint32(0)
    blocks = [lax.dynamic_slice(partial, (zero, start), (partial.shape[0], width)) for start in starts]
    return blocks[0], blocks[1], jnp.stack(blocks[2:]).astype(BF)


def natural(parts, shard):
    out = []
    for index in range(4):
        value = parts[0]
        for flip, part in zip(FLIPS[1:], parts[1:]):
            value = jnp.where((shard ^ flip) == index, part, value)
        out.append(value)
    return out


def row_sum(keep, near, got):
    rows = got.shape[-2]
    own = (slice(None),) * (len(keep.shape) - 2) + (slice(0, rows),)
    return keep[own].astype(F32) + near[own].astype(F32) + got[...].astype(F32)


def rms_scale(value):
    return lax.rsqrt(jnp.mean(value * value, axis=-1, keepdims=True) + epsilon)


def rms_back(value, scale, gain, grad):
    weighted = grad * gain
    return scale * weighted - value * (
        scale * scale * scale * jnp.mean(value * weighted, axis=-1, keepdims=True)
    )


def far_body(keep, near, far):
    rows = far.shape[-2]
    below = (slice(None),) * (len(keep.shape) - 2) + (slice(rows, 2 * rows),)
    far[...] = (keep[below].astype(F32) + near[below].astype(F32)).astype(BF)


def attention_rows_body(keep, near, got, token, gain, value_out, resid_out, low_out):
    value = row_sum(keep, near, got)
    resid = token[...].astype(F32) + value * rms_scale(value) * gain[...]
    value_out[...] = value
    resid_out[...] = resid
    low_out[...] = resid.astype(BF)


def feed_rows_body(keep, near, got, resid, cot, gain, output, grad):
    value = row_sum(keep, near, got)
    scale = rms_scale(value)
    output[...] = (resid[...] + value * scale * gain[...]).astype(BF)
    grad[...] = rms_back(value, scale, gain[...], cot[...].astype(F32)).astype(BF)


def back_rows_body(keep, near, got, value, cot, gain, grad_out, low_out):
    grad = cot[...].astype(F32) + row_sum(keep, near, got)
    grad_out[...] = grad
    value = value[...]
    low_out[...] = rms_back(value, rms_scale(value), gain[...], grad).astype(BF)


def far_two_body(keep, near, *fars):
    for h, far in enumerate(fars):
        far_body(keep.at[h], near.at[h], far)


def input_rows_body(order, keep, near, *refs):
    chunks = keep.shape[0]
    gots, resids, outs = refs[:chunks], refs[chunks : 2 * chunks], refs[2 * chunks :]
    rows = [
        (row_sum(keep.at[h], near.at[h], gots[h]) + resids[h][...]).astype(BF) for h in range(chunks)
    ]

    @pl.when(order[0] == 0)
    def _():
        for out, row in zip(outs, rows):
            out[...] = row

    @pl.when(order[0] != 0)
    def _():
        for out, row in zip(outs, rows[::-1]):
            out[...] = row


def input_rows(keep, near, gots, resids, order):
    args = [keep, near, *gots, *resids]
    outs = [shape_of(resid.shape, BF) for resid in resids]
    return call(
        input_rows_body, (1,), args, [whole(x) for x in args], [(o, whole(o)) for o in outs], scalars=[order]
    )


def order_body(spot, *refs):
    gots, out = refs[:-1], refs[-1]
    for turn in range(len(gots)):

        @pl.when(spot[0] == turn)
        def _():
            for j in range(len(gots)):
                out[j] = gots[(j - turn) % len(gots)][...].astype(F32)


def order_rows(gots, spot):
    out = shape_of((len(gots), *gots[0].shape), F32)
    return call(order_body, (1,), gots, [whole(x) for x in gots], [(out, whole(out))], scalars=[spot])[0]


def by_rows(body, args, kinds):
    *lead, rows, width = args[0].shape
    outs = [shape_of((*lead, rows // 2, width), kind) for kind in kinds]
    return call(body, (1,), args, [whole(x) for x in args], [(o, whole(o)) for o in outs])


def rotate(value, cosine, sine):
    half = value.shape[-1] // 2
    turned = jnp.concatenate([value[..., half:], value[..., :half]], axis=-1)
    return value * cosine[:, None, :] + turned * sine[:, None, :]


def realign(value, flip, chunks):
    shape = value.shape
    value = value.reshape(shape[0], chunks, 2, 2, -1)
    if flip & 1:
        value = value[:, :, ::-1]
    if flip & 2:
        value = value[:, :, :, ::-1]
    return value.reshape(shape)


def group_of(sequence, part, per_sequence, ctx_size):
    if per_sequence > 1:
        return sequence * per_sequence + part
    depth = sequence % (ctx_size // 2)
    return 2 * depth + (depth + sequence // (ctx_size // 2)) % 2


def sequence_of(ctx, per_sequence, ctx_size):
    if per_sequence > 1:
        return ctx // per_sequence, ctx % per_sequence
    depth = ctx // 2
    return depth + ctx_size // 2 * ((ctx + depth) % 2), 0 * ctx


def wide_attention(pre, sums, cosine, sine, gains, chunks, positions, groups):
    _, total, width = pre.shape
    heads = width // HD
    pre = pre.astype(F32)
    squares = sum(realign(s[::8], flip, chunks) for flip, s in zip(FLIPS, sums))
    scales = lax.rsqrt(squares[:2] / D + epsilon)[:, :, None]

    def as_heads(value):
        return value.reshape(total, heads, HD)

    queries, key_rows = [
        rotate(as_heads(pre[p] * scales[p] * gains[p]), cosine, sine).astype(BF) for p in range(2)
    ]

    def over_sequence(value):
        return lax.all_gather(value, "ctx", axis=0, tiled=True, axis_index_groups=groups)

    key_all, value_all = over_sequence(key_rows), over_sequence(as_heads(pre[2].astype(BF)))
    visible = over_sequence(positions // BLOCK)[None, :] <= (positions // BLOCK)[:, None]
    factor = 1.0 / math.sqrt(HD)
    scores = jnp.einsum("qhd,khd->hqk", queries, key_all, preferred_element_type=F32) * factor
    scores = jnp.where(visible, scores, far_below)
    weights = jnp.exp(scores - jnp.max(scores, axis=-1, keepdims=True))
    probs = weights / jnp.sum(weights, axis=-1, keepdims=True)
    mixed = jnp.einsum("hqk,khd->qhd", probs.astype(BF), value_all, preferred_element_type=F32)
    mixed = mixed.astype(BF).reshape(total, width)

    def back(grad_mixed):
        grad = as_heads(grad_mixed)
        grad_probs = jnp.einsum("qhd,khd->hqk", grad, value_all, preferred_element_type=F32)
        delta = jnp.sum(probs * grad_probs, axis=-1, keepdims=True)
        grad_scores = (probs * (grad_probs - delta)).astype(BF)
        grad_queries = jnp.einsum("hqk,khd->qhd", grad_scores, key_all, preferred_element_type=F32)
        grad_keys = jnp.einsum("hqk,qhd->khd", grad_scores, queries, preferred_element_type=F32)
        grad_values = jnp.einsum("hqk,qhd->khd", probs.astype(BF), grad, preferred_element_type=F32)
        grad_keys, grad_values = [
            lax.psum_scatter(
                g.astype(BF), "ctx", scatter_dimension=0, tiled=True, axis_index_groups=groups
            ).astype(F32)
            for g in (grad_keys * factor, grad_values)
        ]
        turned = [
            rotate(g, cosine, -sine).reshape(total, width) * gains[p]
            for p, g in enumerate((grad_queries * factor, grad_keys))
        ]
        inner = jnp.stack([jnp.sum(turned[p] * pre[p], axis=-1) for p in range(2)])
        inner = jnp.repeat(inner, 8, axis=0)
        values = grad_values.reshape(total, width).astype(BF)
        return turned[0].astype(BF), turned[1].astype(BF), values, inner

    return mixed, back


def choose_body(place, wide, down, model, hidden, gains, wide_out, down_out, model_out, hidden_out, small, sems):
    at = place[0]
    sources = [(wide.at[:, at], wide_out), (down.at[at], down_out)]
    sources += [(model.at[:, at], model_out), (hidden.at[:, at], hidden_out)]
    run_copies([pltpu.make_async_copy(source, to, sems.at[i]) for i, (source, to) in enumerate(sources)])
    rank, width = wide_out.shape[1:]
    shared = [wide_out[p] for p in (0, 1, 2, 4, 5)] + [model_out[p] for p in (3, 4)]
    last = jnp.concatenate([gains[2:], jnp.zeros((rank - 2, width), BF)])
    for at, value in enumerate([*shared, last]):
        column = at // 2 * width
        small[at % 2 * rank : (at % 2 + 1) * rank, column : column + width] = value


def choose(place, a_wide, a_down, b_model, b_hidden, gains):
    rank, width = a_wide.shape[2:]
    shapes = [a_wide.shape[:1] + a_wide.shape[2:], a_down.shape[1:]]
    shapes += [b_model.shape[:1] + b_model.shape[2:], b_hidden.shape[:1] + b_hidden.shape[2:]]
    shapes.append((2 * rank, 4 * width))
    outs = [shape_of(s, BF) for s in shapes]
    return call(
        choose_body,
        (1,),
        [a_wide, a_down, b_model, b_hidden, gains],
        [HBM] * 4 + [whole(gains)],
        [(o, whole(o)) for o in outs],
        [pltpu.SemaphoreType.DMA((4,))],
        scalars=[place],
    )


def place_body(rank, count, unused, plan, at, *refs):
    sources, outs = refs[:count], refs[count + unused :]
    for out, maps in zip(outs, plan):
        for n in range(out.shape[1]):
            for p, pieces in enumerate(maps):
                begin = 0
                for source, place in pieces:
                    value = sources[source][at[n], place * rank : (place + 1) * rank].astype(F32)
                    out[p, n, :, begin : begin + value.shape[-1]] = value
                    begin += value.shape[-1]


def on_device(
    tokens,
    cotangent,
    adapter_index,
    w_attn,
    w_gate_up,
    w_down,
    gains,
    a_wide,
    a_down,
    b_model,
    b_hidden,
):
    seqs, rows = tokens.shape[0], tokens.shape[1]
    shards, ctxs = lax.axis_size("shard"), lax.axis_size("ctx")
    shard, ctx = lax.axis_index("shard"), lax.axis_index("ctx")
    batch = seqs * shards
    per_sequence = ctxs // batch
    group_rows = batch * rows
    chunks = seqs
    chunk_rows = shards * rows
    wide = HEADS // shards * HD
    adapters, rank = a_down.shape[:2]

    groups = [[group_of(q, k, per_sequence, ctxs) for k in range(per_sequence)] for q in range(batch)]
    my_sequence, my_part = sequence_of(ctx, per_sequence, ctxs)
    my_slot = my_sequence % seqs
    my_spot = (ctx % batch) // shards

    pairs = []
    for p in range(seqs):
        pairs.append([])
        for c in range(ctxs):
            for s in range(shards):
                k, local = c // batch, c % batch
                spot, owner = local // shards, local % shards
                to = groups[seqs * s + (p + spot) % seqs][k]
                pairs[p].append((c * shards + s, to * shards + owner))

    windows = Windows()
    side_by_side = windows.side_by_side

    def is_place(index):
        return [index % seqs == at for at in range(1, seqs)]

    flags = {
        "cut": [((p + my_spot) % seqs).astype(jnp.uint32) for p in range(seqs)],
        "chunk": [is_place(my_slot - h) for h in range(seqs)],
        "return": [is_place(my_slot - p) for p in range(seqs)],
        "order": [is_place(j - my_spot) for j in range(seqs)],
        "columns": [((shard ^ flip) * wide).astype(jnp.uint32) for flip in FLIPS],
        "places": jnp.stack([shard, ctx % 4]).astype(jnp.int32),
        "turn": [((my_slot - p) % seqs)[None].astype(jnp.int32) for p in range(seqs)],
        "spot": my_spot[None].astype(jnp.int32),
    }

    def pick(parts, is_it):
        value = parts[0]
        for part, flag in zip(parts[1:], is_it):
            value = jnp.where(flag, part, value)
        return value

    def cut_rows(*values):
        return [
            jnp.concatenate(
                [
                    lax.dynamic_index_in_dim(value, flags["cut"][p], 0, keepdims=False)
                    for value in values
                ]
            )
            for p in range(seqs)
        ]

    def send_row(p):
        return lambda cut: lax.ppermute(cut, ("ctx", "shard"), pairs[p])

    def chunk_order(got):
        return [pick(got, flags["chunk"][h]) for h in range(seqs)]

    def return_cuts(parts):
        return [pick(parts, flags["return"][p]) for p in range(seqs)]

    def return_row(p):
        return lambda cut: lax.ppermute(cut, ("ctx", "shard"), [(b, a) for a, b in pairs[p]])

    def return_order(got):
        return jnp.stack([pick(got, flags["order"][j]) for j in range(seqs)])

    def core(value):
        return over_shard(value, 1)

    def chip(value):
        return over_shard(value, 2)

    def across(value):
        return over_shard(value, 3)

    def by_x(value):
        return over_ctx(value, 1)

    def by_z(value):
        return over_ctx(value, 2)

    def to_all(value):
        return [(functools.partial(over_shard, flip=flip), value) for flip in FLIPS[1:]]

    index_own = adapter_index[:, 0]
    (qkv_near, qkv_far, qkv_cross, flags), index_got = side_by_side(
        lambda x: (*cut(x[0], 0, 3, x[1]["places"], False), x[1]), [w_attn, flags], to_all(index_own)
    )
    places = flags["places"]
    index_all = jnp.concatenate(natural([index_own, *index_got], shard))
    sequence_with = jnp.sum(
        jnp.where(
            index_all[None, :] == jnp.arange(adapters, dtype=jnp.int32)[:, None],
            jnp.arange(batch, dtype=jnp.int32)[None, :],
            0,
        ),
        axis=1,
    )
    table = jnp.array(groups, jnp.int32)
    if per_sequence > 1:
        where = sequence_with
    else:
        group_with = jnp.sum(
            jnp.where(
                sequence_with[:, None] == jnp.arange(batch, dtype=jnp.int32)[None, :], table[:, 0][None, :], 0
            ),
            axis=1,
        )
        where = gathered_place(ctx, group_with)

    row_cuts = cut_rows(tokens)

    def rope_tables(place):
        spot, turn, row = np.indices((chunks, shards, rows)).reshape(3, -1).astype(np.int32)
        owner = place ^ np.array(FLIPS, np.int32)[turn]
        position = my_part * group_rows + (spot * shards + owner) * rows + row
        lane = np.arange(HD)
        freqs = np.exp((lane % (HD // 2)) * (-2.0 * math.log(rope_base) / HD)).astype(np.float32)
        angles = position.astype(F32)[:, None] * freqs[None, :]
        sign = np.where(lane < HD // 2, -1.0, 1.0).astype(np.float32)
        return position, jnp.cos(angles), jnp.sin(angles) * sign

    def prepare(x):
        chosen = choose(x[0], a_wide, a_down, b_model, b_hidden, gains)
        return chosen, cut(x[1], 0, 2, x[2], True), x[3], rope_tables(x[2][0])

    (chosen, gate_up_cuts, where, (positions, cosine, sine)), [qkv_a, *row_got, qkv_near] = side_by_side(
        prepare,
        [index_all[my_sequence][None], w_gate_up, places, where],
        [(chip, qkv_far), (send_row(0), row_cuts[0]), (send_row(1), row_cuts[1]), (core, qkv_near)],
    )
    own_wide, own_down, own_model, own_hidden, small = chosen
    near, gate_far, gate_cross, up_far, up_cross = gate_up_cuts

    token_rows = chunk_order(row_got)
    held = {}

    def load_out(x):
        held["out"], held["down"], done = load_plain(*x[:2])
        return done, jnp.concatenate(x[2:])

    (done, token_own), [qkv_b, qkv_xa, qkv_za] = side_by_side(
        load_out,
        [w_attn, w_down, *token_rows, small],
        [(across, qkv_cross), (by_x, qkv_a), (by_z, qkv_a)],
    )
    windows.carried.append(done)
    _, [token_far, qkv_xb, qkv_zb] = side_by_side(
        None, None, [(chip, token_own), (by_x, qkv_b), (by_z, qkv_b)]
    )
    _, [last_a, last_b, token_near, gate_a] = side_by_side(
        None,
        None,
        [
            (by_x, qkv_za),
            (by_z, qkv_xb),
            (core, jnp.stack([token_own, token_far])),
            (chip, gate_far),
        ],
    )
    w_qkv = [qkv_near, qkv_a, qkv_b, qkv_xa, qkv_xb, qkv_za, qkv_zb, last_a, last_b]
    token_parts = [token_own, token_far, token_near]
    small_parts = [part[..., seqs * rows :, :] for part in token_parts]
    small_parts = [small_parts[0], small_parts[1], small_parts[2][0], small_parts[2][1]]
    small_all = jnp.concatenate(
        natural(
            [
                jnp.concatenate([part[:, at * wide : (at + 1) * wide] for at in range(4)])
                for part in small_parts
            ],
            shard,
        ),
        axis=1,
    )
    qkv_downs = small_all[: 3 * rank]
    gate_downs = small_all[3 * rank : 5 * rank]
    out_up = small_all[5 * rank : 6 * rank]
    feed_up = small_all[6 * rank : 7 * rank]
    attn_gain = small_all[7 * rank : 7 * rank + 1].astype(F32)
    feed_gain = small_all[7 * rank + 1 : 7 * rank + 2].astype(F32)
    head_gains = gains[:2].astype(F32)

    (pre, qkv_low, squares, qkv_held), [gate_b, gate_xa, gate_za, near] = side_by_side(
        lambda x: qkv_forward(x, chunks, rows, w_attn, w_qkv, places, qkv_downs, own_model),
        token_parts,
        [(across, gate_cross), (by_x, gate_a), (by_z, gate_a), (core, near)],
    )

    def from_all(sums, others):
        _, got = side_by_side(None, None, to_all(sums) + others)
        return [sums, *got[:3]], got[3:]

    squares, _ = from_all(squares[:16], [])
    simple = per_sequence == 1 and chunk_rows == BLOCK
    attention_sends = [(chip, up_far), (by_x, gate_b), (by_z, gate_b)]
    if simple:
        (queries, key_rows, mixed, logs), got = side_by_side(
            lambda x: attention_forward(x[0], x[1], x[2], x[3], head_gains, chunks),
            [pre, squares, cosine, sine],
            attention_sends,
        )
    else:
        mixed, attention_grads = wide_attention(
            pre, squares, cosine, sine, head_gains, chunks, positions, groups
        )
        got = [send(value) for send, value in attention_sends]
    up_a, gate_xb, gate_zb = got

    every = range(chunks)
    assert chunks == 2
    def far_sum(keep, near):
        return by_rows(far_body, [keep, near], [BF])[0]

    def project_out(x, h):
        return partial_forward(x, h, chunks, held["out"], own_wide[3], out_up, False)

    def attention_rows(h, keep, near, got):
        return by_rows(attention_rows_body, [keep, near, got, token_rows[h], attn_gain], [F32, F32, BF])

    def feed_rows(h, keep, near, got):
        return by_rows(feed_rows_body, [keep, near, got, resid[h], cot[h], feed_gain], [BF, BF])

    def back_rows(h, keep, near, got):
        return by_rows(back_rows_body, [keep, near, got, attn_pre[h], cot[h], attn_gain], [F32, BF])

    def up_gate(parts):
        return gate_up_forward(parts, gate_up_held, gate_downs, own_hidden)

    def down(act):
        return partial_forward(act, 0, 1, held["down"], own_down, feed_up, False, [gate_up_held])

    def back_down(h, parts):
        return feed_back(
            parts, held["down"], own_down, hidden[h][0], hidden[h][1], hidden[h][3], feed_parts[h][2], feed_up, own_hidden, gate_up_held
        )

    def back_up_gate(h, gate_grad, upper_grad):
        return gate_up_back(
            gate_grad, upper_grad, gate_up_held, hidden_grads[h][2], gate_downs, resid_parts[h]
        )

    def back_out(h, parts):
        return out_back(parts, held["out"], own_wide[3], out_up, mixed, out_parts[h][2], h)

    none = [None] * PARTS

    def load_first(x):
        gate = [*x, None, None]
        held["gate_up"], done = load([gate, none], places, w_gate_up, near)
        return done

    def load_more(x):
        gate = none[:6] + x[:2]
        up = [*x[2:], None, None]
        held["gate_up"], done = load([gate, up], places, held=held["gate_up"])
        return done

    def load_last(x):
        held["gate_up"], done = load([none, none[:6] + x], places, held=held["gate_up"])
        return done

    attn_pre, resid, resid_low = [None] * 2, [None] * 2, [None] * 2
    resid_parts, hidden, feed_parts, output = [None] * 2, [None] * 2, [None] * 2, [None] * 2
    hidden_grads, resid_grads, grad_resid, out_grads = [None] * 2, [None] * 2, [None] * 2, [None] * 2
    out_parts, [up_b, up_xa, up_za] = side_by_side(
        lambda x: [project_out(x, h) for h in every], mixed, [(across, up_cross), (by_x, up_a), (by_z, up_a)]
    )
    _, [core0, core1] = side_by_side(None, None, [(core, out_parts[0][1]), (core, out_parts[1][1])])
    far0, far1 = far_sum(out_parts[0][0], core0), far_sum(out_parts[1][0], core1)
    done, [got0, got1, gate_last_a, gate_last_b] = side_by_side(
        load_first,
        [gate_a, gate_b, gate_xa, gate_xb, gate_za, gate_zb],
        [(chip, far0), (chip, far1), (by_x, gate_za), (by_z, gate_xb)],
    )
    windows.carried.append(done)
    attn_pre[0], resid[0], resid_low[0] = attention_rows(0, out_parts[0][0], core0, got0)
    attn_pre[1], resid[1], resid_low[1] = attention_rows(1, out_parts[1][0], core1, got1)
    _, [far0, near0, up_xb, up_zb] = side_by_side(
        None, None, [(chip, resid_low[0]), (core, resid_low[0]), (by_x, up_b), (by_z, up_b)]
    )
    done, [cross0, far1, near1, up_last_a, up_last_b] = side_by_side(
        load_more,
        [gate_last_a, gate_last_b, up_a, up_b, up_xa, up_xb, up_za, up_zb],
        [(core, far0), (chip, resid_low[1]), (core, resid_low[1]), (by_x, up_za), (by_z, up_xb)],
    )
    windows.carried.append(done)
    resid_parts[0] = [resid_low[0], far0, near0, cross0]
    done, [cross1] = side_by_side(load_last, [up_last_a, up_last_b], [(core, far1)])
    windows.carried.append(done)
    gate_up_held = held["gate_up"]
    resid_parts[1] = [resid_low[1], far1, near1, cross1]

    cot_cuts = cut_rows(cotangent)
    hidden[0], [cot0] = side_by_side(up_gate, resid_parts[0], [(send_row(0), cot_cuts[0])])
    feed_parts[0], _ = side_by_side(down, hidden[0][2], [])
    _, [core0] = side_by_side(None, None, [(core, feed_parts[0][1])])
    hidden[1], [got, cot1] = side_by_side(
        up_gate, resid_parts[1], [(chip, far_sum(feed_parts[0][0], core0)), (send_row(1), cot_cuts[1])]
    )
    cot = chunk_order([cot0, cot1])
    output[0], grad0 = feed_rows(0, feed_parts[0][0], core0, got)
    feed_parts[1], [far, near] = side_by_side(down, hidden[1][2], [(chip, grad0), (core, grad0)])
    _, [cross, core1] = side_by_side(None, None, [(core, far), (core, feed_parts[1][1])])
    hidden_grads[0], [got] = side_by_side(
        lambda x: back_down(0, x), [grad0, far, near, cross], [(chip, far_sum(feed_parts[1][0], core1))]
    )
    output[1], grad1 = feed_rows(1, feed_parts[1][0], core1, got)
    output = return_cuts(output)
    resid_grads[0], [far, near, output0] = side_by_side(
        lambda x: back_up_gate(0, *x),
        hidden_grads[0][:2],
        [(chip, grad1), (core, grad1), (return_row(0), output[0])],
    )
    _, [cross, core0] = side_by_side(None, None, [(core, far), (core, resid_grads[0][1])])
    hidden_grads[1], [got, output1] = side_by_side(
        lambda x: back_down(1, x),
        [grad1, far, near, cross],
        [(chip, far_sum(resid_grads[0][0], core0)), (return_row(1), output[1])],
    )
    output = return_order([output0, output1])
    grad_resid[0], grad0 = back_rows(0, resid_grads[0][0], core0, got)

    broad = jnp.concatenate(
        [sum(g[3] for g in hidden_grads), sum(g[5] for g in hidden_grads).reshape(2 * rank, -1)]
    ).astype(BF)
    broad = [x[None] for x in jnp.split(broad, 2, axis=1)]
    step0, step1, step2 = [ctx_step(at) for at in range(3)]

    def grown(value, got):
        return jnp.concatenate([value, got])

    resid_grads[1], [far, near, *got] = side_by_side(
        lambda x: back_up_gate(1, *x),
        hidden_grads[1][:2],
        [(chip, grad0), (core, grad0), (step0, broad[0]), (step0, broad[1])],
    )
    broad = [grown(*pair) for pair in zip(broad, got)]
    own_early, far_early, cuts = column_cuts(
        jnp.concatenate([sum(g[4] for g in hidden_grads), sum(g[2] for g in resid_grads)]), flags["columns"]
    )
    _, [cross, core1, got_early] = side_by_side(
        None, None, [(core, far), (core, resid_grads[1][1]), (core, cuts)]
    )
    own_early = own_early + got_early[0].astype(F32)
    far_early = (far_early + got_early[1].astype(F32)).astype(BF)
    out_grads[0], [got1, got_early, got] = side_by_side(
        lambda x: back_out(0, x),
        [grad0, far, near, cross],
        [(chip, far_sum(resid_grads[1][0], core1)), (chip, far_early), (step1, broad[0])],
    )
    broad[0] = grown(broad[0], got)
    early = (own_early + got_early.astype(F32)).astype(BF)[None]
    grad_resid[1], grad1 = back_rows(1, resid_grads[1][0], core1, got1)
    _, [far, near, got, got_b] = side_by_side(
        None, None, [(chip, grad1), (core, grad1), (step2, broad[0]), (step1, broad[1])]
    )
    broad = [grown(broad[0], got), grown(broad[1], got_b)]
    _, [cross] = side_by_side(None, None, [(core, far)])
    out_grads[1] = back_out(1, [grad1, far, near, cross])
    grad_mixed = jnp.concatenate([g[0] for g in out_grads])

    attention_sends = [(step0, early)]
    if simple:
        (query_turned, key_turned, grad_values, inner), [got] = side_by_side(
            lambda x: attention_back(
                queries, key_rows, pre, x, logs, cosine, sine, head_gains, chunks
            ),
            grad_mixed,
            attention_sends,
        )
    else:
        query_turned, key_turned, grad_values, inner = attention_grads(grad_mixed)
        [got] = [send(value) for send, value in attention_sends]
    early = grown(early, got)
    inners, _ = from_all(inner, [])
    grads, lows, down_late, up_late = qkv_grads(
        [query_turned, key_turned], grad_values, pre, squares, inners, token_parts, qkv_low, own_model, chunks
    )
    partial = jnp.concatenate([down_late, sum(g[2] for g in out_grads)])
    cuts = [lax.dynamic_slice(partial, (jnp.uint32(0), start), (partial.shape[0], wide)) for start in flags["columns"]]

    def rest_of(value):
        for at in range(3, len(ctx_flips())):
            value = grown(value, ctx_step(at)(value))
        if per_sequence > 1:
            value = jnp.sum(value.astype(F32)[gathered_place(ctx, table)], axis=1)
        return value

    def placed(sources, counts, plan, carried=()):
        width = sum(sources[piece[0]].shape[-1] for piece in plan[0][0])
        outs = [shape_of((count, adapters, rank, width), F32) for count in counts]
        return call(
            functools.partial(place_body, rank, len(sources), len(carried), plan),
            (1,),
            [*sources, *carried],
            [whole(x) for x in (*sources, *carried)],
            [(o, whole(o)) for o in outs],
            scalars=[where],
        )

    def place_broad(x):
        return placed([rest_of(value) for value in x], (1, 2), ((((0, 0), (1, 0)),), (((0, 1), (1, 1)), ((0, 2), (1, 2)))))

    sends = [(send, piece.astype(BF)) for send, piece in zip((chip, core, across), cuts[1:])]
    (keep, send), [*got, got_early] = side_by_side(
        lambda x: qkv_back(x, lows, qkv_held, qkv_downs, chunks), grads, sends + [(step1, early)]
    )
    early = grown(early, got_early)
    late = jnp.concatenate(
        [
            cuts[0] + sum(piece.astype(F32) for piece in got),
            up_late.reshape(3 * rank, -1),
            sum(g[1] for g in out_grads),
        ]
    ).astype(BF)[None]
    _, [near_sum, got, got_early] = side_by_side(None, None, [(core, send), (step0, late), (step2, early)])
    early = grown(early, got_early)
    late = jnp.split(grown(late, got), 2, axis=2)
    far = shape_of(grad_resid[0].shape, BF)
    fars = call(
        far_two_body, (1,), [keep, near_sum], [whole(keep), whole(near_sum)], [(far, whole(far))] * chunks
    )
    _, [got0, got_a, got] = side_by_side(
        None, None, [(chip, fars[0]), (step1, late[0]), (step2, broad[1])]
    )
    broad[1] = grown(broad[1], got)
    late[0] = grown(late[0], got_a)
    (grad_down, grad_hidden), [got1, got_a, got_b] = side_by_side(
        place_broad, broad, [(chip, fars[1]), (step2, late[0]), (step1, late[1])]
    )
    late = [grown(late[0], got_a), grown(late[1], got_b)]
    def place_late(x):
        return placed(
            x,
            (6, 5),
            (
                (*[((1, at), (2, at)) for at in (0, 1, 2, 7)], ((0, 1),), ((0, 2),)),
                (*[((1, at), (2, at)) for at in (4, 5, 6, 3)], ((0, 0),)),
            ),
            windows.carried,
        )

    sends, [got_late] = side_by_side(
        lambda x: input_rows(keep, near_sum, x, grad_resid, flags["turn"][0]), [got0, got1], [(step2, late[1])]
    )
    sources = [rest_of(early), rest_of(late[0]), rest_of(grown(late[1], got_late))]
    (grad_wide, grad_model), got = side_by_side(
        place_late, sources, [(return_row(p), rows_back) for p, rows_back in enumerate(sends)]
    )
    input_grad = order_rows(got, flags["spot"])
    return (output, input_grad, grad_wide, grad_down[0], grad_model, grad_hidden)


def solution(mesh):
    return jax.shard_map(
        on_device,
        mesh=mesh,
        in_specs=(
            P("shard", "ctx", None),
            P("shard", "ctx", None),
            P("shard", None),
            P(None, "shard", None),
            P(None, "shard", None),
            P("shard", None),
            P(None, "shard"),
            P(None, None, None, "shard"),
            P(None, None, "shard"),
            P(None, None, None, "shard"),
            P(None, None, None, "shard"),
        ),
        out_specs=(
            P("shard", "ctx", None),
            P("shard", "ctx", None),
            P(None, None, None, "shard"),
            P(None, None, "shard"),
            P(None, None, None, "shard"),
            P(None, None, None, "shard"),
        ),
        check_vma=False,
    )
```
